32 devices in a mesh: dp: 8 (over z, x), tensor: 4 (over y, core).
Axes of the slice: x: 2, y: 2, z: 4, core: 2. Of those that a mesh axis runs over, the one named last changes fastest.
Arguments:
- coords: float32 [6, 6144], P(None, 'dp'), may hold values from 0 to 2.5, as said below
- model_ids: int32 [6144], P('dp'), may hold values from 0 to 3
- cells: int32 [6144], P('dp'), may hold values from 0 to 65535
- valid: int32 [6144], P('dp'), may hold values 0 or 1
- slowness_grid: float32 [4, 512, 128], replicated, may hold values from 0.2 to 6
- master_blocks: float32 [2, 2, 512, 512], P(None, None, 'dp', 'tensor'), may hold values from -0.25 to 0.25
- small_params: float32 [12, 512], P(None, 'tensor'), may hold values from -1.5 to 1.5
- moment_blocks: float32 [2, 2, 512, 512], P(None, None, 'dp', 'tensor'), may hold values from -1 to 1
- moment_small: float32 [12, 512], P(None, 'tensor'), may hold values from -6 to 6
- average_blocks: float32 [2, 2, 512, 512], P(None, None, 'dp', 'tensor'), may hold values from -0.25 to 0.25
- average_small: float32 [12, 512], P(None, 'tensor'), may hold values from -4 to 4
Outputs:
- loss: float32 [], replicated
- grad_blocks: float32 [2, 2, 512, 512], P(None, None, 'dp', 'tensor')
- grad_small: float32 [12, 512], P(None, 'tensor')
- bias_grads: float32 [4, 512], P(None, 'tensor')
- new_moment_blocks: float32 [2, 2, 512, 512], P(None, None, 'dp', 'tensor')
- new_moment_small: float32 [12, 512], P(None, 'tensor')
- new_master_blocks: float32 [2, 2, 512, 512], P(None, None, 'dp', 'tensor')
- new_small: float32 [12, 512], P(None, 'tensor')
- new_average_blocks: float32 [2, 2, 512, 512], P(None, None, 'dp', 'tensor')
- new_average_small: float32 [12, 512], P(None, 'tensor')
- low_blocks: bfloat16 [2, 2, 512, 512], P(None, None, 'dp', 'tensor')
The draws below stay inside these ranges and needn't reach their ends.
Inputs may be any that keep to these rules, and one draw needn't show every extreme that they name: `coords`: rows 0 to 2 are a source in the unit cube; the receiver's first coordinate exceeds the source's by 0.5 or more.
All inputs are finite; a program needn't handle non-finite values. No bound on the sum of `valid` on one device may be relied on, other than what follows from the above.
Results may differ from the reference program's by a relative error of at most 0.012.
Values may be sent and summed in bfloat16 or wider, within the bound.
A program may use at most 128 MiB of HBM per device.

```python
import math
import jax
import jax.numpy as jnp
from jax import lax

D = 512
LAYERS = 2
MICRO = 3
MB_DEV = 256
MODELS = 4
GRID_ROWS = 512
GRID_COLS = 128
SMALL_ROWS = 12
PAIRS = 6144
N_DP = 8


def draw_coords(key, part):
    key = jax.random.fold_in(key, 11)
    points = jax.random.uniform(key, (6, PAIRS), jnp.float32)
    rows = lax.broadcasted_iota(jnp.int32, (6, PAIRS), 0)
    return points + jnp.where(rows == 3, 1.5, 0.0)


def draw_small_params(key, part):
    key = jax.random.fold_in(key, 23)
    normal = jax.random.truncated_normal(key, -3.0, 3.0, (SMALL_ROWS, D), jnp.float32)
    rows = lax.broadcasted_iota(jnp.int32, (SMALL_ROWS, D), 0)
    scale = jnp.where(rows < 6, 0.5, 0.3)
    scale = jnp.where(rows == SMALL_ROWS - 1, 1.5 * D ** (-0.5), scale)
    return normal * scale


def set_ends(array, rng, low, top_value):
    shape = array.shape
    index_at = [jax.random.randint(jax.random.fold_in(rng, axis), (), 0, shape[axis]) for axis in range(len(shape))]
    array = array.at[tuple(index_at)].set(low)
    longest = shape.index(max(shape))
    index_at[longest] = (index_at[longest] + 1) % shape[longest]
    return array.at[tuple(index_at)].set(top_value)


def steps_of(stream_key, extent, split, least, top_value):
    def one(position, parts):
        draws = jax.random.uniform(jax.random.fold_in(jax.random.fold_in(stream_key, 6), position), (parts,), jnp.float32, least / len(split), top_value / len(split))
        return jnp.repeat(jnp.exp(draws), extent[position] // parts).reshape((-1,) + (1,) * (len(extent) - position - 1))

    level = one(*split[0])
    for cut in split[1:]:
        level = level * one(*cut)
    return level


def gaussian(stream_key, dims, deviation, limit, shards=(), held_as=jnp.bfloat16):
    array = deviation * jax.random.normal(stream_key, dims, jnp.float32)
    if shards:
        array = array * steps_of(stream_key, dims, shards, -0.22, 0.18)
    return jnp.clip(array, -limit, limit).astype(held_as)


def setup_inputs(seed: int = 0) -> dict:
    arg_keys = jax.random.split(jax.random.key(seed), 12)
    return {
        "coords": draw_coords(jax.random.fold_in(arg_keys[11], 71), 0),
        "model_ids": set_ends(jax.random.randint(arg_keys[1], (PAIRS,), 0, MODELS), jax.random.fold_in(arg_keys[1], 1), 0, MODELS - 1).astype(jnp.int32),
        "cells": set_ends(jax.random.randint(arg_keys[2], (PAIRS,), 0, GRID_ROWS * GRID_COLS), jax.random.fold_in(arg_keys[2], 1), 0, (GRID_ROWS * GRID_COLS) - 1).astype(jnp.int32),
        "valid": set_ends((jax.random.randint(arg_keys[3], (PAIRS,), 0, 4) < 3).astype(jnp.int32), jax.random.fold_in(arg_keys[3], 1), 0, 1),
        "slowness_grid": jnp.clip(jnp.exp(jax.random.uniform(arg_keys[4], (MODELS, GRID_ROWS, GRID_COLS), jnp.float32, math.log(0.2), math.log(6.0))), 0.2, 6.0),
        "master_blocks": gaussian(arg_keys[5], (LAYERS, 2, D, D), D ** -0.5, 0.25, ((2, 8), (3, 4)), jnp.float32),
        "small_params": draw_small_params(jax.random.fold_in(arg_keys[11], 71), 0),
        "moment_blocks": gaussian(arg_keys[7], (LAYERS, 2, D, D), (6.0 * (MB_DEV * MICRO * N_DP) ** -0.5), 1.0, ((2, 8), (3, 4)), jnp.float32),
        "moment_small": gaussian(arg_keys[8], (SMALL_ROWS, D), (30.0 * (MB_DEV * MICRO * N_DP) ** -0.5), 6.0, ((1, 4),), jnp.float32),
        "average_blocks": gaussian(arg_keys[9], (LAYERS, 2, D, D), D ** -0.5, 0.25, ((2, 8), (3, 4)), jnp.float32),
        "average_small": gaussian(arg_keys[10], (SMALL_ROWS, D), 0.3, 4.0, ((1, 4),), jnp.float32),
    }


@jax.custom_vjp
def low(v):
    return lax.optimization_barrier(v.astype(jnp.bfloat16)).astype(jnp.float32)

@jax.custom_vjp
def low_back(v):
    return v

def low_keep(v):
    return (low(v), None)

def low_pass(kept, grad):
    return (grad,)

def back_keep(v):
    return (v, None)

def back_low(kept, grad):
    return (low(grad),)
low.defvjp(low_keep, low_pass)
low_back.defvjp(back_keep, back_low)
highest = lax.Precision.HIGHEST
momentum_coef = 0.5
average_decay = 0.5
spread_rate = 0.5
norm_epsilon = 1e-12

def elu(values):
    return jnp.where(values > 0, values, jnp.expm1(jnp.minimum(values, 0.0)))

def slope_of(values):
    return jnp.where(values > 0, 1.0, jnp.exp(jnp.minimum(values, 0.0)))

def block_total(blocks, small, coord_rows, model_rows, cell_rows, mask_rows, grid):
    weights = low(blocks)
    first_rows = small[0:6]
    inner_pre = jnp.dot(coord_rows.T, first_rows, precision=highest) + small[6]
    slopes = slope_of(inner_pre)
    streams = jnp.concatenate([elu(inner_pre)[None], slopes[None] * first_rows[3:6][:, None, :]], 0)
    for layer_index in range(LAYERS):
        acts_low = low(streams)
        pre_all = low_back(jnp.einsum('sbd,dh->sbh', acts_low, weights[layer_index, 0], precision=highest))
        value_pre = pre_all[0] + small[7 + layer_index]
        hidden = low(jnp.concatenate([elu(value_pre)[None], slope_of(value_pre)[None] * pre_all[1:]], 0))
        branch = low_back(jnp.einsum('sbh,oh->sbo', hidden, weights[layer_index, 1], precision=highest))
        streams = streams + branch
        streams = streams.at[0].add(small[7 + LAYERS + layer_index])
    projected = jnp.einsum('sbd,d->sb', streams, small[7 + 2 * LAYERS], precision=highest)
    separation = coord_rows[3:6] - coord_rows[0:3]
    distance = jnp.sqrt(lax.optimization_barrier(jnp.sum(separation * separation, 0)))
    factor_tau = projected[0]
    grad_time = separation / distance * jnp.abs(factor_tau) + distance * jnp.sign(factor_tau) * projected[1:]
    square = lax.optimization_barrier(jnp.sum(grad_time * grad_time, 0))
    true_slow = grid.reshape(MODELS, GRID_ROWS * GRID_COLS)[model_rows, cell_rows]
    return jnp.sum(mask_rows * jnp.abs(square - true_slow * true_slow))

def reference(coords, model_ids, cells, valid, slowness_grid, master_blocks, small_params, moment_blocks, moment_small, average_blocks, average_small):
    mask_all = valid.astype(jnp.float32)
    count_valid = jnp.sum(mask_all)
    groups = coords.shape[1] // MB_DEV

    def one_group(carry, group_index):
        start = group_index * MB_DEV
        coord_rows = lax.dynamic_slice_in_dim(coords, start, MB_DEV, 1)
        model_rows = lax.dynamic_slice_in_dim(model_ids, start, MB_DEV, 0)
        cell_rows = lax.dynamic_slice_in_dim(cells, start, MB_DEV, 0)
        mask_rows = lax.dynamic_slice_in_dim(mask_all, start, MB_DEV, 0)

        def local_total(blocks, small):
            return block_total(blocks, small, coord_rows, model_rows, cell_rows, mask_rows, slowness_grid)
        total_err, pull_back = jax.vjp(local_total, master_blocks, small_params)
        grad_b, grad_s = pull_back(jnp.ones_like(total_err))
        return ((carry[0] + total_err, carry[1] + grad_b, carry[2] + grad_s), None)
    start_carry = (jnp.zeros((), jnp.float32), jnp.zeros_like(master_blocks), jnp.zeros_like(small_params))
    (total_err, sum_blocks, sum_small), unused = lax.scan(one_group, start_carry, jnp.arange(groups, dtype=jnp.int32))
    loss = total_err / count_valid
    grad_blocks = sum_blocks / count_valid
    grad_small = sum_small / count_valid
    bias_grads = grad_small[7:7 + 2 * LAYERS]
    new_moment_blocks = momentum_coef * moment_blocks + grad_blocks
    new_moment_small = momentum_coef * moment_small + grad_small
    dir_blocks = grad_blocks + momentum_coef * new_moment_blocks
    dir_small = grad_small + momentum_coef * new_moment_small
    rate_blocks = spread_rate * jnp.sqrt(lax.optimization_barrier(jnp.sum(master_blocks * master_blocks, (2, 3)))) / jnp.sqrt(lax.optimization_barrier(jnp.sum(dir_blocks * dir_blocks, (2, 3))) + norm_epsilon)
    rate_small = spread_rate * jnp.sqrt(jnp.sum(small_params * small_params)) / jnp.sqrt(jnp.sum(dir_small * dir_small) + norm_epsilon)
    new_master_blocks = master_blocks - rate_blocks[:, :, None, None] * dir_blocks
    new_small = small_params - rate_small * dir_small
    new_average_blocks = average_decay * average_blocks + (1.0 - average_decay) * new_master_blocks
    new_average_small = average_decay * average_small + (1.0 - average_decay) * new_small
    return (loss, grad_blocks, grad_small, bias_grads, new_moment_blocks, new_moment_small, new_master_blocks, new_small, new_average_blocks, new_average_small, new_master_blocks.astype(jnp.bfloat16))
```

```python
import functools

import jax
import jax.numpy as jnp
from jax import lax
from jax.experimental import pallas as pl
from jax.experimental.pallas import tpu as pltpu
from jax.sharding import PartitionSpec as P

LAYERS = 2
MATS = 2 * LAYERS
SMALL = 12
MESH = pl.DeviceIdType.MESH
F32 = jnp.float32
BF16 = jnp.bfloat16

momentum_coef = 0.5
average_decay = 0.5
spread_rate = 0.5
norm_epsilon = 1e-12

FAR_LAST = 3


def nn(left, right):
    return lax.dot_general(left, right, (((1,), (0,)), ((), ())), preferred_element_type=F32)


def nt(left, right):
    return lax.dot_general(left, right, (((1,), (1,)), ((), ())), preferred_element_type=F32)


def tn(left, right):
    return lax.dot_general(left, right, (((0,), (0,)), ((), ())), preferred_element_type=F32)


def sign_of(v):
    return jnp.where(v > 0, 1.0, jnp.where(v < 0, -1.0, 0.0))


def kernel(
    dims,
    coords_hbm,
    model_hbm,
    cells_hbm,
    valid_hbm,
    grid_hbm,
    master_hbm,
    small_hbm,
    moment_hbm,
    msmall_hbm,
    gsum,
    sred,
    tot,
    coords,
    model,
    cells,
    valid,
    grid,
    master,
    moment,
    msmall,
    spbuf,
    columns,
    wbuf,
    streams,
    acts,
    pre,
    hidden,
    grad,
    gbranch,
    gpre,
    inner,
    gsend,
    gcore,
    gone,
    gslot_g,
    gtwo_g,
    gslot_z,
    gtwo_z,
    gback_g,
    sgsend,
    sgcore,
    sgone,
    sgslot_g,
    sgtwo,
    sgslot_z,
    arslot_g,
    artwo,
    arslot_z,
    in_sem,
    w_send,
    w_recv,
    g_send,
    g_recv,
    s_send,
    s_recv,
):
    A, B, C, R, cw, Pn, D = dims
    n_t = 2 * C
    G = C * B
    dp = lax.axis_index("dp")
    t = lax.axis_index("tensor")
    a, b = dp // B, dp % B
    y, c = t // 2, t % 2
    g = y * B + b

    def device(a_, g_, c_):
        return (a_ * B + g_ % B, (g_ // B) * 2 + c_)

    far = [(a + k) % A for k in range(1, A)]
    near = [(g + k) % G for k in range(1, G)]
    z_devices = [device(o, g, c) for o in far]
    g_devices = [device(a, o, c) for o in near]
    core_device = device(a, g, 1 - c)
    group = [(o, 1 - c) for o in near]
    q_devices = g_devices + [device(a, o, cc) for o, cc in group] + [core_device]
    q_slots = [o * 2 + c for o in near] + [o * 2 + cc for o, cc in group] + [g * 2 + 1 - c]
    NQ = 2 * G
    FAR, NEAR, CORE = 0, A - 1, A + G - 2

    S1 = 1
    S2 = S1 + G - 1
    S3 = S2 + A - 1
    S4 = S3 + NQ - 1
    S5 = S4 + n_t - 1

    sends = []

    def remote(src, dst, ssem, rsem, device_id):
        copy = pltpu.make_async_remote_copy(
            src_ref=src,
            dst_ref=dst,
            send_sem=ssem,
            recv_sem=rsem,
            device_id=device_id,
            device_id_type=MESH,
        )
        copy.start()
        sends.append(copy)
        return copy

    def arrived(copies):
        for copy in copies:
            copy.wait_recv()

    local = []
    for i, (src, dst) in enumerate(
        [
            (master_hbm, master),
            (small_hbm, spbuf.at[t]),
            (coords_hbm, coords),
            (model_hbm, model),
            (cells_hbm, cells),
            (valid_hbm, valid),
            (grid_hbm, grid),
            (moment_hbm, moment),
            (msmall_hbm, msmall),
        ]
    ):
        copy = pltpu.make_async_copy(src, dst, in_sem.at[i])
        copy.start()
        local.append(copy)

    barrier = pltpu.get_barrier_semaphore()
    peers = z_devices + q_devices
    for d in peers:
        pl.semaphore_signal(barrier, inc=1, device_id=d, device_id_type=MESH)

    local[0].wait()
    for m in range(MATS):
        wbuf[m, c, y, a, b] = master[m // 2, m % 2].astype(BF16)
    local[1].wait()
    pl.semaphore_wait(barrier, len(peers))

    def w_far(m, src_of):
        return [
            remote(src_of(m), src_of(m), w_send.at[m, FAR + k], w_recv.at[m, FAR + k], d)
            for k, d in enumerate(z_devices)
        ]

    def w_near(m, src_of):
        return [
            remote(src_of(m), src_of(m), w_send.at[m, NEAR + k], w_recv.at[m, NEAR + k], d)
            for k, d in enumerate(g_devices)
        ]

    def own(m):
        return wbuf.at[m, c, y, a, b]

    def line(m):
        return wbuf.at[m, c, y, :, b]

    def plane(m):
        return wbuf.at[m, c, :, a]

    def w_core(m):
        return [remote(wbuf.at[m, c], wbuf.at[m, c], w_send.at[m, CORE], w_recv.at[m, CORE], core_device)]

    def owner_t(o, cc):
        return (o // B) * 2 + cc

    first = {}
    normal = [m for m in range(MATS) if m != FAR_LAST]
    sp_copies = []
    for k in range(1, n_t):
        o = (t + k) % n_t
        sp_copies.append(
            remote(spbuf.at[t], spbuf.at[t], s_send.at[S4 + k - 1], s_recv.at[S4 + k - 1], (dp, o))
        )
    for i, m in enumerate(normal):
        first[m] = w_far(m, own)
        if i == 0:
            first[FAR_LAST] = w_near(FAR_LAST, own)

    for copy in local[2:7]:
        copy.wait()
    cols = grid.shape[2]
    shift = (cols - 1).bit_length()
    cell = cells[...].reshape(1, -1)
    row_id = model[...].reshape(1, -1) * grid.shape[1] + (cell >> shift)
    col_id = cell & (cols - 1)
    PB = row_id.shape[1]
    packed = jnp.concatenate(
        [
            coords[...],
            row_id.astype(F32),
            col_id.astype(F32),
            valid[...].reshape(1, -1).astype(F32),
            jnp.zeros((128 - 9, PB), F32),
        ],
        0,
    )
    columns[...] = packed.T
    mine = columns[pl.ds(pl.multiple_of(t * Pn, 8), Pn), :]
    xs = [mine[:, j : j + 1] for j in range(6)]
    mask = mine[:, 8:9]
    row_of = mine[:, 6:7].astype(jnp.int32)
    col_of = mine[:, 7:8].astype(jnp.int32)
    table = grid[...].reshape(-1, cols)
    onehot = (
        lax.broadcasted_iota(jnp.int32, (Pn, table.shape[0]), 1) == row_of
    ).astype(BF16)
    high = table.astype(BF16)
    rest = table - high.astype(F32)
    middle = rest.astype(BF16)
    lowest = (rest - middle.astype(F32)).astype(BF16)
    picked = nn(onehot, high) + nn(onehot, middle) + nn(onehot, lowest)
    lane = lax.broadcasted_iota(jnp.int32, (Pn, cols), 1)
    truth = jnp.sum(jnp.where(lane == col_of, picked, 0.0), 1, keepdims=True)
    seps = [xs[3 + k] - xs[k] for k in range(3)]
    distance = jnp.sqrt(seps[0] * seps[0] + seps[1] * seps[1] + seps[2] * seps[2])
    units = [s / distance for s in seps]

    arrived(sp_copies)

    def small_row(i):
        return jnp.concatenate([spbuf[tt, i : i + 1, :] for tt in range(n_t)], 1)

    first_rows = [small_row(j) for j in range(6)]
    z0 = small_row(6) + xs[0] * first_rows[0]
    for j in range(1, 6):
        z0 = z0 + xs[j] * first_rows[j]
    inner[...] = z0
    e0 = jnp.exp(jnp.minimum(z0, 0.0))
    slope0 = jnp.where(z0 > 0, 1.0, e0)
    streams[0] = jnp.where(z0 > 0, z0, e0 - 1.0)
    acts[0, 0] = streams[0].astype(BF16)
    for k in range(3):
        streams[1 + k] = slope0 * first_rows[3 + k]
        acts[0, 1 + k] = streams[1 + k].astype(BF16)

    second = {}
    arrived(first[FAR_LAST])
    second[FAR_LAST] = w_far(FAR_LAST, plane)
    for m in normal:
        arrived(first[m])
        second[m] = w_near(m, line)

    third = {}

    def weight(m):
        return jnp.concatenate([wbuf[m, tt % 2, tt // 2].reshape(D, cw) for tt in range(n_t)], 1)

    M = 4 * Pn

    def block_in(l):
        pre[l] = nn(acts[l].reshape(M, D), weight(2 * l)).reshape(4, Pn, D)
        z = pre[l, 0] + small_row(7 + l)
        e = jnp.exp(jnp.minimum(z, 0.0))
        slope = jnp.where(z > 0, 1.0, e)
        hidden[l, 0] = jnp.where(z > 0, z, e - 1.0).astype(BF16)
        for k in range(1, 4):
            hidden[l, k] = (slope * pre[l, k]).astype(BF16)

    def block_out(l):
        branch = nt(hidden[l].reshape(M, D), weight(2 * l + 1)).reshape(4, Pn, D)
        for s in range(4):
            new = streams[s] + branch[s]
            if s == 0:
                new = new + small_row(7 + LAYERS + l)
            streams[s] = new
            if l + 1 < LAYERS:
                acts[l + 1, s] = new.astype(BF16)

    def fetch(m):
        arrived(second[m])
        third[m] = w_core(m)

    for m in range(MATS):
        fetch(m)
        arrived(third[m])
        if m % 2 == 0:
            block_in(m // 2)
        else:
            block_out(m // 2)

    out_row = small_row(7 + 2 * LAYERS)
    proj = [jnp.sum(streams[s] * out_row, 1, keepdims=True) for s in range(4)]
    tau = proj[0]
    sign_tau = sign_of(tau)
    abs_tau = jnp.abs(tau)
    grad_time = [units[k] * abs_tau + distance * sign_tau * proj[1 + k] for k in range(3)]
    square = grad_time[0] * grad_time[0] + grad_time[1] * grad_time[1] + grad_time[2] * grad_time[2]
    error = square - truth * truth
    total_err = jnp.sum(mask * jnp.abs(error), axis=0, keepdims=True)
    count = jnp.sum(mask, axis=0, keepdims=True)
    seed = mask * sign_of(error)
    g_time = [2.0 * grad_time[k] * seed for k in range(3)]
    g_tau = sign_tau * (units[0] * g_time[0] + units[1] * g_time[1] + units[2] * g_time[2])
    g_proj = [g_tau] + [distance * sign_tau * g_time[k] for k in range(3)]
    g_out_row = jnp.sum(
        streams[0] * g_proj[0] + streams[1] * g_proj[1] + streams[2] * g_proj[2] + streams[3] * g_proj[3],
        axis=0,
        keepdims=True,
    )
    for s in range(4):
        value = g_proj[s] * out_row
        grad[s] = value
        gbranch[s] = value.astype(BF16)

    flying = {}

    def start_core(m, value):
        low = value.astype(BF16)
        for tt in range(n_t):
            gsend[m, tt % 2, tt // 2] = low[:, tt * cw : (tt + 1) * cw].reshape(A, B, R, cw)
        flying[m] = [
            remote(gsend.at[m, 1 - c], gcore.at[m], g_send.at[m, CORE], g_recv.at[m, CORE], core_device)
        ]

    def core_sum(m):
        arrived(flying[m])
        return (gsend[m, c].astype(F32) + gcore[m].astype(F32)).astype(BF16)

    def slot_sum(ref, count_of):
        value = ref[0].astype(F32)
        for i in range(1, count_of):
            value = value + ref[i].astype(F32)
        return value

    def start_near(m):
        gone[m] = core_sum(m)
        gslot_g[m, g] = gone[m, y, :, b]
        flying[m] = [
            remote(
                gone.at[m, o // B, :, o % B],
                gslot_g.at[m, g],
                g_send.at[m, NEAR + k],
                g_recv.at[m, NEAR + k],
                g_devices[k],
            )
            for k, o in enumerate(near)
        ]

    def start_far(m):
        arrived(flying[m])
        gtwo_g[m] = slot_sum(gslot_g.at[m], G).astype(BF16)
        gslot_z[m, a] = gtwo_g[m, a]
        flying[m] = [
            remote(gtwo_g.at[m, o], gslot_z.at[m, a], g_send.at[m, FAR + k], g_recv.at[m, FAR + k], z_devices[k])
            for k, o in enumerate(far)
        ]

    def start_far_first(m):
        gone[m] = core_sum(m)
        gtwo_z[a] = gone[m, :, a]
        flying[m] = [
            remote(
                gone.at[m, :, o], gtwo_z.at[a], g_send.at[m, FAR + k], g_recv.at[m, FAR + k], z_devices[k]
            )
            for k, o in enumerate(far)
        ]

    def start_near_last(m):
        arrived(flying[m])
        total = slot_sum(gtwo_z, A).astype(BF16)
        for i in range(G):
            gback_g[0, i] = total[i // B, i % B]
        gback_g[1, g] = gback_g[0, g]
        flying[m] = [
            remote(gback_g.at[0, o], gback_g.at[1, g], g_send.at[m, NEAR + k], g_recv.at[m, NEAR + k], g_devices[k])
            for k, o in enumerate(near)
        ]

    bias_in = [None] * LAYERS
    bias_out = [None] * LAYERS

    def back_out(l):
        bias_out[l] = jnp.sum(grad[0], axis=0, keepdims=True)
        gb = gbranch[...].reshape(M, D)
        start_core(2 * l + 1, tn(gb, hidden[l].reshape(M, D)))

    def back_in(l):
        gb = gbranch[...].reshape(M, D)
        gh = nn(gb, weight(2 * l + 1)).reshape(4, Pn, D)
        z = pre[l, 0] + small_row(7 + l)
        e = jnp.exp(jnp.minimum(z, 0.0))
        slope = jnp.where(z > 0, 1.0, e)
        curve = jnp.where(z > 0, 0.0, e)
        gz = gh[0] * slope + curve * (gh[1] * pre[l, 1] + gh[2] * pre[l, 2] + gh[3] * pre[l, 3])
        bias_in[l] = jnp.sum(gz, axis=0, keepdims=True)
        gpre[0] = gz.astype(BF16)
        for k in range(1, 4):
            gpre[k] = (gh[k] * slope).astype(BF16)
        start_core(2 * l, tn(acts[l].reshape(M, D), gpre[...].reshape(M, D)))

    def back_through(l):
        back = nt(gpre[...].reshape(M, D), weight(2 * l)).reshape(4, Pn, D)
        for s in range(4):
            value = grad[s] + back[s]
            grad[s] = value
            if l > 0:
                gbranch[s] = value.astype(BF16)

    def forward_first(m):
        if m == FAR_LAST:
            start_far_first(m)
        else:
            start_near(m)

    back_out(1)
    back_in(1)
    forward_first(3)
    back_through(1)
    back_out(0)
    forward_first(2)
    back_in(0)
    forward_first(1)
    back_through(0)
    forward_first(0)

    z0 = inner[...]
    e0 = jnp.exp(jnp.minimum(z0, 0.0))
    slope0 = jnp.where(z0 > 0, 1.0, e0)
    curve0 = jnp.where(z0 > 0, 0.0, e0)
    first_rows = [small_row(j) for j in range(6)]
    g_inner = grad[0] * slope0 + curve0 * (
        grad[1] * first_rows[3] + grad[2] * first_rows[4] + grad[3] * first_rows[5]
    )
    rows = [jnp.sum(xs[j] * g_inner, axis=0, keepdims=True) for j in range(6)]
    for k in range(3):
        rows[3 + k] = rows[3 + k] + jnp.sum(grad[1 + k] * slope0, axis=0, keepdims=True)
    rows.append(jnp.sum(g_inner, axis=0, keepdims=True))
    rows = rows + bias_in + bias_out + [g_out_row]

    lanes = lax.broadcasted_iota(jnp.int32, (1, cw), 1)
    weight_sq = jnp.zeros((1, cw), F32)
    for m in range(MATS):
        part = jnp.sum(master[m // 2, m % 2] * master[m // 2, m % 2], keepdims=True)
        weight_sq = jnp.where(lanes == m, part, weight_sq)
    own_small = spbuf[t]
    weight_sq = jnp.where(lanes == MATS, jnp.sum(own_small * own_small, keepdims=True) / (A * B), weight_sq)
    tail = [
        jnp.broadcast_to(total_err, (1, cw)),
        jnp.broadcast_to(count, (1, cw)),
        weight_sq,
        jnp.zeros((1, cw), F32),
    ]
    for tt in range(n_t):
        sgsend[tt % 2, tt // 2] = jnp.concatenate([r[:, tt * cw : (tt + 1) * cw] for r in rows] + tail, 0)
    sg = [remote(sgsend.at[1 - c], sgcore, s_send.at[0], s_recv.at[0], core_device)]
    arrived(sg)
    sgone[...] = sgsend[c] + sgcore[...]
    sgslot_g[g] = sgone[y]
    sg = [
        remote(sgone.at[o // B], sgslot_g.at[g], s_send.at[S1 + k], s_recv.at[S1 + k], g_devices[k])
        for k, o in enumerate(near)
    ]

    start_near_last(FAR_LAST)
    for m in reversed(normal):
        start_far(m)
    arrived(sg)
    sgtwo[...] = slot_sum(sgslot_g, G)
    sgslot_z[a] = sgtwo[...]
    sg = [
        remote(sgtwo, sgslot_z.at[a], s_send.at[S2 + k], s_recv.at[S2 + k], z_devices[k]) for k in range(A - 1)
    ]

    for copy in local[7:]:
        copy.wait()
    arrived(flying[FAR_LAST])
    for i in range(MATS):
        m = MATS - 1 - i
        if m == FAR_LAST:
            gsum[m] = slot_sum(gback_g.at[1], G)
        else:
            arrived(flying[m])
            gsum[m] = slot_sum(gslot_z.at[m], A)
    arrived(sg)
    sred[...] = slot_sum(sgslot_z, A)
    counted = sred[SMALL + 1 : SMALL + 2, 0:1]
    tile_rows = lax.broadcasted_iota(jnp.int32, (8, 128), 0)
    parts = jnp.zeros((8, 128), F32)
    for m in range(MATS):
        gr = gsum[m] / counted
        direction = gr + momentum_coef * (momentum_coef * moment[m // 2, m % 2] + gr)
        parts = jnp.where(tile_rows == m, jnp.sum(direction * direction, keepdims=True), parts)
    gr = sred[0:SMALL, :] / counted
    direction = gr + momentum_coef * (momentum_coef * msmall[...] + gr)
    parts = jnp.where(
        tile_rows == MATS, jnp.sum(direction * direction, keepdims=True) / (A * B), parts
    )
    me = g * 2 + c
    arslot_g[me] = parts
    ar = [
        remote(arslot_g.at[me], arslot_g.at[me], s_send.at[S3 + k], s_recv.at[S3 + k], d)
        for k, d in enumerate(q_devices)
    ]
    arrived(ar)
    artwo[...] = slot_sum(arslot_g, NQ)
    arslot_z[a] = artwo[...]
    ar = [
        remote(artwo, arslot_z.at[a], s_send.at[S5 + k], s_recv.at[S5 + k], d) for k, d in enumerate(z_devices)
    ]
    arrived(ar)
    tot[...] = slot_sum(arslot_z, A)

    for copy in sends:
        copy.wait_send()


def body(
    axes,
    coords,
    model_ids,
    cells,
    valid,
    slowness_grid,
    master_blocks,
    small_params,
    moment_blocks,
    moment_small,
    average_blocks,
    average_small,
):
    n_dp, n_t = axes
    A = 4 if n_dp % 4 == 0 else n_dp
    B = n_dp // A
    C = n_t // 2
    G = C * B
    R, cw = master_blocks.shape[2:]
    D = R * n_dp
    PB = coords.shape[1]
    Pn = PB // n_t
    dims = (A, B, C, R, cw, Pn, D)
    anywhere = pl.BlockSpec(memory_space=pl.ANY)
    vmem = pl.BlockSpec(memory_space=pltpu.VMEM)
    S = SMALL + 4
    args = (
        coords,
        model_ids,
        cells,
        valid,
        slowness_grid,
        master_blocks,
        small_params,
        moment_blocks,
        moment_small,
    )
    V = pltpu.VMEM
    gsum, sred, tot = pl.pallas_call(
        functools.partial(kernel, dims),
        out_shape=(
            jax.ShapeDtypeStruct((MATS, R, cw), F32),
            jax.ShapeDtypeStruct((S, cw), F32),
            jax.ShapeDtypeStruct((8, 128), F32),
        ),
        in_specs=[anywhere] * len(args),
        out_specs=(vmem,) * 3,
        scratch_shapes=[
            V(coords.shape, F32),
            V((PB,), jnp.int32),
            V((PB,), jnp.int32),
            V((PB,), jnp.int32),
            V(slowness_grid.shape, F32),
            V(master_blocks.shape, F32),
            V(master_blocks.shape, F32),
            V(small_params.shape, F32),
            V((n_t, SMALL, cw), F32),
            V((PB, 128), F32),
            V((MATS, 2, C, A, B, R, cw), BF16),
            V((4, Pn, D), F32),
            V((LAYERS, 4, Pn, D), BF16),
            V((LAYERS, 4, Pn, D), F32),
            V((LAYERS, 4, Pn, D), BF16),
            V((4, Pn, D), F32),
            V((4, Pn, D), BF16),
            V((4, Pn, D), BF16),
            V((Pn, D), F32),
            V((MATS, 2, C, A, B, R, cw), BF16),
            V((MATS, C, A, B, R, cw), BF16),
            V((MATS, C, A, B, R, cw), BF16),
            V((MATS, G, A, R, cw), BF16),
            V((MATS, A, R, cw), BF16),
            V((MATS, A, R, cw), BF16),
            V((A, C, B, R, cw), BF16),
            V((2, G, R, cw), BF16),
            V((2, C, S, cw), F32),
            V((C, S, cw), F32),
            V((C, S, cw), F32),
            V((G, S, cw), F32),
            V((S, cw), F32),
            V((A, S, cw), F32),
            V((2 * G, 8, 128), F32),
            V((8, 128), F32),
            V((A, 8, 128), F32),
            pltpu.SemaphoreType.DMA((len(args),)),
            pltpu.SemaphoreType.DMA((MATS, A + G - 1)),
            pltpu.SemaphoreType.DMA((MATS, A + G - 1)),
            pltpu.SemaphoreType.DMA((MATS, A + G - 1)),
            pltpu.SemaphoreType.DMA((MATS, A + G - 1)),
            pltpu.SemaphoreType.DMA((G + 2 * A + 2 * G + n_t,)),
            pltpu.SemaphoreType.DMA((G + 2 * A + 2 * G + n_t,)),
        ],
        compiler_params=pltpu.CompilerParams(
            collective_id=0, has_side_effects=True, vmem_limit_bytes=60 << 20
        ),
    )(*args)

    total_err = sred[SMALL, 0]
    count_valid = sred[SMALL + 1, 0]
    weight_sq = sred[SMALL + 2, 0 : MATS + 1]
    dir_sq = tot[0 : MATS + 1, 0]
    loss = total_err / count_valid
    grad_blocks = gsum.reshape(master_blocks.shape) / count_valid
    grad_small = sred[0:SMALL] / count_valid
    bias_grads = grad_small[7 : 7 + 2 * LAYERS]
    new_moment_blocks = momentum_coef * moment_blocks + grad_blocks
    new_moment_small = momentum_coef * moment_small + grad_small
    dir_blocks = grad_blocks + momentum_coef * new_moment_blocks
    dir_small = grad_small + momentum_coef * new_moment_small
    step_rate = spread_rate * jnp.sqrt(weight_sq) / jnp.sqrt(dir_sq + norm_epsilon)
    rate_blocks = step_rate[:-1].reshape(LAYERS, 2)
    new_master_blocks = master_blocks - rate_blocks[:, :, None, None] * dir_blocks
    new_small = small_params - step_rate[-1] * dir_small
    new_average_blocks = average_decay * average_blocks + (1.0 - average_decay) * new_master_blocks
    new_average_small = average_decay * average_small + (1.0 - average_decay) * new_small
    return (
        loss,
        grad_blocks,
        grad_small,
        bias_grads,
        new_moment_blocks,
        new_moment_small,
        new_master_blocks,
        new_small,
        new_average_blocks,
        new_average_small,
        new_master_blocks.astype(BF16),
    )


def solution(mesh):
    blocks = P(None, None, "dp", "tensor")
    small = P(None, "tensor")
    in_specs = (
        P(None, "dp"),
        P("dp"),
        P("dp"),
        P("dp"),
        P(),
        blocks,
        small,
        blocks,
        small,
        blocks,
        small,
    )
    out_specs = (P(), blocks, small, small, blocks, small, blocks, small, blocks, small, blocks)
    axes = (mesh.shape["dp"], mesh.shape["tensor"])
    return jax.shard_map(
        functools.partial(body, axes), mesh=mesh, in_specs=in_specs, out_specs=out_specs, check_vma=False
    )
```

```python
import functools

import jax
import jax.numpy as jnp
from jax import lax
from jax.experimental import pallas as pl
from jax.experimental.pallas import tpu as pltpu
from jax.sharding import PartitionSpec as P

LAYERS = 2
MATS = 2 * LAYERS
SMALL = 12
MESH = pl.DeviceIdType.MESH
F32 = jnp.float32
BF16 = jnp.bfloat16

momentum_coef = 0.5
average_decay = 0.5
spread_rate = 0.5
norm_epsilon = 1e-12

TURNED = 2


def partner(i, k, size):
    bit = 1
    while bit < size:
        if (k // bit) % 2:
            i = i + bit - 2 * bit * ((i // bit) % 2)
        bit *= 2
    return i


def nn(left, right):
    return lax.dot_general(left, right, (((1,), (0,)), ((), ())), preferred_element_type=F32)


def nt(left, right):
    return lax.dot_general(left, right, (((1,), (1,)), ((), ())), preferred_element_type=F32)


def tn(left, right):
    return lax.dot_general(left, right, (((0,), (0,)), ((), ())), preferred_element_type=F32)


def sign_of(v):
    return jnp.where(v > 0, 1.0, jnp.where(v < 0, -1.0, 0.0))


def kernel(
    dims,
    coords_hbm,
    model_hbm,
    cells_hbm,
    valid_hbm,
    grid_hbm,
    master_hbm,
    small_hbm,
    moment_hbm,
    msmall_hbm,
    average_hbm,
    asmall_hbm,
    loss_b,
    grad_b,
    grad_s,
    bias_b,
    moment_b,
    moment_s,
    master_b,
    master_s,
    average_b,
    average_s,
    low_b,
    coords,
    model,
    cells,
    valid,
    grid,
    master,
    moment,
    msmall,
    average,
    asmall,
    spbuf,
    columns,
    sred,
    wbuf,
    streams,
    acts,
    pre,
    hidden,
    grad,
    gbranch,
    gpre,
    inner,
    gsend,
    gcore,
    gone,
    gslot_n,
    gtwo,
    gslot_z,
    gown,
    tslot_z,
    tback,
    tslot_n,
    sgsend,
    sgcore,
    sgone,
    sgslot_g,
    sgtwo,
    sgslot_z,
    arslot_g,
    artwo,
    arslot_z,
    in_sem,
    wz_send,
    wz_recv,
    wn_send,
    wn_recv,
    wt_send,
    wc_send,
    wc_recv,
    gz_send,
    gz_recv,
    gn_send,
    gn_recv,
    gc_send,
    gc_recv,
    s_send,
    s_recv,
):
    A, B, C, R, cw, Pn, D = dims
    n_t = 2 * C
    G = C * B
    dp = lax.axis_index("dp")
    t = lax.axis_index("tensor")
    a, b = dp // B, dp % B
    y, c = t // 2, t % 2
    g = y * B + b

    def device(a_, g_, c_):
        return (a_ * B + g_ % B, (g_ // B) * 2 + c_)

    far = [partner(a, k, A) for k in range(1, A)]
    near = [partner(g, k, G) for k in range(1, G)]
    z_devices = [device(o, g, c) for o in far]
    g_devices = [device(a, o, c) for o in near]
    core_device = device(a, g, 1 - c)
    group = [(o, 1 - c) for o in near]
    q_devices = g_devices + [device(a, o, cc) for o, cc in group] + [core_device]
    q_slots = [o * 2 + c for o in near] + [o * 2 + cc for o, cc in group] + [g * 2 + 1 - c]
    NQ = 2 * G

    S1 = 1
    S2 = S1 + G - 1
    S3 = S2 + A - 1
    S4 = S3 + NQ - 1
    S5 = S4 + n_t - 1

    sends = []

    def remote(src, dst, ssem, rsem, device_id):
        copy = pltpu.make_async_remote_copy(
            src_ref=src,
            dst_ref=dst,
            send_sem=ssem,
            recv_sem=rsem,
            device_id=device_id,
            device_id_type=MESH,
        )
        copy.start()
        sends.append(copy)
        return copy

    def arrived(copies):
        for copy in copies:
            copy.wait_recv()

    local = []
    for i, (src, dst) in enumerate(
        [
            (master_hbm, master),
            (small_hbm, spbuf.at[t]),
            (coords_hbm, coords),
            (model_hbm, model),
            (cells_hbm, cells),
            (valid_hbm, valid),
            (grid_hbm, grid),
            (moment_hbm, moment),
            (msmall_hbm, msmall),
            (average_hbm, average),
            (asmall_hbm, asmall),
        ]
    ):
        copy = pltpu.make_async_copy(src, dst, in_sem.at[i])
        copy.start()
        local.append(copy)

    barrier = pltpu.get_barrier_semaphore()
    peers = z_devices + q_devices
    for d in peers:
        pl.semaphore_signal(barrier, inc=1, device_id=d, device_id_type=MESH)

    local[0].wait()
    for m in range(MATS):
        wbuf[m, c, y, a, b] = master[m // 2, m % 2].astype(BF16)
    local[1].wait()
    pl.semaphore_wait(barrier, len(peers))

    def piece(m, o, z):
        return wbuf.at[m, c, o // B, z, o % B]

    def line(m, o):
        return wbuf.at[m, c, o // B, :, o % B]

    def plane(m, z):
        return wbuf.at[m, c, :, z]

    def await_bytes(ref, rsem, d):
        pltpu.make_async_remote_copy(
            src_ref=ref, dst_ref=ref, send_sem=s_send.at[0], recv_sem=rsem, device_id=d, device_id_type=MESH
        ).wait_recv()

    def w_far(m, ref):
        return [
            remote(ref, ref, wz_send.at[m, k], wz_recv.at[m, k], d) for k, d in enumerate(z_devices)
        ]

    def w_near(m, ref, j):
        return [
            remote(ref, ref, wn_send.at[m, j, k], wn_recv.at[m, k], d) for k, d in enumerate(g_devices)
        ]

    def w_far_turned(ref, j):
        for k, d in enumerate(z_devices):
            remote(ref, ref, wt_send.at[j, k], wz_recv.at[TURNED, k], d)

    def w_core(m, ref, j):
        remote(ref, ref, wc_send.at[m, j], wc_recv.at[m], core_device)

    straight = [m for m in range(MATS) if m != TURNED]
    sp_copies = []
    for k in range(1, n_t):
        o = (t + k) % n_t
        sp_copies.append(
            remote(spbuf.at[t], spbuf.at[t], s_send.at[S4 + k - 1], s_recv.at[S4 + k - 1], (dp, o))
        )
    first = {}
    for i, m in enumerate(straight):
        first[m] = w_far(m, piece(m, g, a))
        if i == 0:
            first[TURNED] = w_near(TURNED, piece(TURNED, g, a), 0)
    for i, m in enumerate(straight):
        w_near(m, piece(m, g, a), 0)
        if i == 0:
            w_far_turned(piece(TURNED, g, a), 0)

    for copy in local[2:7]:
        copy.wait()
    cols = grid.shape[2]
    shift = (cols - 1).bit_length()
    cell = cells[...].reshape(1, -1)
    row_id = model[...].reshape(1, -1) * grid.shape[1] + (cell >> shift)
    col_id = cell & (cols - 1)
    PB = row_id.shape[1]
    packed = jnp.concatenate(
        [
            coords[...],
            row_id.astype(F32),
            col_id.astype(F32),
            valid[...].reshape(1, -1).astype(F32),
            jnp.zeros((128 - 9, PB), F32),
        ],
        0,
    )
    columns[...] = packed.T
    mine = columns[pl.ds(pl.multiple_of(t * Pn, 8), Pn), :]
    xs = [mine[:, j : j + 1] for j in range(6)]
    mask = mine[:, 8:9]
    row_of = mine[:, 6:7].astype(jnp.int32)
    col_of = mine[:, 7:8].astype(jnp.int32)
    table = grid[...].reshape(-1, cols)
    onehot = (
        lax.broadcasted_iota(jnp.int32, (Pn, table.shape[0]), 1) == row_of
    ).astype(BF16)
    high = table.astype(BF16)
    rest = table - high.astype(F32)
    middle = rest.astype(BF16)
    lowest = (rest - middle.astype(F32)).astype(BF16)
    picked = nn(onehot, high) + nn(onehot, middle) + nn(onehot, lowest)
    lane = lax.broadcasted_iota(jnp.int32, (Pn, cols), 1)
    truth = jnp.sum(jnp.where(lane == col_of, picked, 0.0), 1, keepdims=True)
    seps = [xs[3 + k] - xs[k] for k in range(3)]
    distance = jnp.sqrt(seps[0] * seps[0] + seps[1] * seps[1] + seps[2] * seps[2])
    units = [s / distance for s in seps]

    arrived(sp_copies)

    def small_row(i):
        return jnp.concatenate([spbuf[tt, i : i + 1, :] for tt in range(n_t)], 1)

    first_rows = [small_row(j) for j in range(6)]
    z0 = small_row(6) + xs[0] * first_rows[0]
    for j in range(1, 6):
        z0 = z0 + xs[j] * first_rows[j]
    inner[...] = z0
    e0 = jnp.exp(jnp.minimum(z0, 0.0))
    slope0 = jnp.where(z0 > 0, 1.0, e0)
    streams[0] = jnp.where(z0 > 0, z0, e0 - 1.0)
    acts[0, 0] = streams[0].astype(BF16)
    for k in range(3):
        streams[1 + k] = slope0 * first_rows[3 + k]
        acts[0, 1 + k] = streams[1 + k].astype(BF16)

    def pass_on(m):
        for k in range(A - 1):
            first[m][k].wait_recv()
            w_near(m, piece(m, g, far[k]), k + 1)
        w_core(m, line(m, g), 0)

    def pass_on_turned():
        for k in range(G - 1):
            first[TURNED][k].wait_recv()
            w_far_turned(piece(TURNED, near[k], a), k + 1)
        w_core(TURNED, plane(TURNED, a), 0)

    pass_on(straight[0])
    pass_on_turned()
    for m in straight[1:]:
        pass_on(m)

    def weight(m):
        return jnp.concatenate([wbuf[m, tt % 2, tt // 2].reshape(D, cw) for tt in range(n_t)], 1)

    M = 4 * Pn

    def block_in(l):
        pre[l] = nn(acts[l].reshape(M, D), weight(2 * l)).reshape(4, Pn, D)
        z = pre[l, 0] + small_row(7 + l)
        e = jnp.exp(jnp.minimum(z, 0.0))
        slope = jnp.where(z > 0, 1.0, e)
        hidden[l, 0] = jnp.where(z > 0, z, e - 1.0).astype(BF16)
        for k in range(1, 4):
            hidden[l, k] = (slope * pre[l, k]).astype(BF16)

    def block_out(l):
        branch = nt(hidden[l].reshape(M, D), weight(2 * l + 1)).reshape(4, Pn, D)
        for s in range(4):
            new = streams[s] + branch[s]
            if s == 0:
                new = new + small_row(7 + LAYERS + l)
            streams[s] = new
            if l + 1 < LAYERS:
                acts[l + 1, s] = new.astype(BF16)

    def fetch(m):
        if m == TURNED:
            for k in range(A - 1):
                await_bytes(plane(m, far[k]), wz_recv.at[m, k], z_devices[k])
                w_core(m, plane(m, far[k]), k + 1)
        else:
            for k in range(G - 1):
                await_bytes(line(m, near[k]), wn_recv.at[m, k], g_devices[k])
                w_core(m, line(m, near[k]), k + 1)

    def fetched(m):
        await_bytes(wbuf.at[m, c], wc_recv.at[m], core_device)

    for m in range(MATS):
        fetch(m)
        fetched(m)
        if m % 2 == 0:
            block_in(m // 2)
        else:
            block_out(m // 2)

    out_row = small_row(7 + 2 * LAYERS)
    proj = [jnp.sum(streams[s] * out_row, 1, keepdims=True) for s in range(4)]
    tau = proj[0]
    sign_tau = sign_of(tau)
    abs_tau = jnp.abs(tau)
    grad_time = [units[k] * abs_tau + distance * sign_tau * proj[1 + k] for k in range(3)]
    square = grad_time[0] * grad_time[0] + grad_time[1] * grad_time[1] + grad_time[2] * grad_time[2]
    error = square - truth * truth
    total_err = jnp.sum(mask * jnp.abs(error), axis=0, keepdims=True)
    count = jnp.sum(mask, axis=0, keepdims=True)
    seed = mask * sign_of(error)
    g_time = [2.0 * grad_time[k] * seed for k in range(3)]
    g_tau = sign_tau * (units[0] * g_time[0] + units[1] * g_time[1] + units[2] * g_time[2])
    g_proj = [g_tau] + [distance * sign_tau * g_time[k] for k in range(3)]
    g_out_row = jnp.sum(
        streams[0] * g_proj[0] + streams[1] * g_proj[1] + streams[2] * g_proj[2] + streams[3] * g_proj[3],
        axis=0,
        keepdims=True,
    )
    for s in range(4):
        value = g_proj[s] * out_row
        grad[s] = value
        gbranch[s] = value.astype(BF16)

    pieces = [(far[k], k) for k in reversed(range(A - 1))] + [(a, None)]

    def start_core(m, value):
        low = value.astype(BF16)
        for tt in range(n_t):
            block = low[:, tt * cw : (tt + 1) * cw].reshape(A, B, R, cw)
            for i in range(B):
                gsend[m, tt % 2, :, (tt // 2) * B + i] = block[:, i]
        return [
            remote(
                gsend.at[m, 1 - c, z], gcore.at[m, z], gc_send.at[m, j], gc_recv.at[m, j], core_device
            )
            for j, (z, k) in enumerate(pieces)
        ]

    def core_sum(m, j):
        z = pieces[j][0]
        flying[m][j].wait_recv()
        gone[m, z] = (gsend[m, c, z].astype(F32) + gcore[m, z].astype(F32)).astype(BF16)

    def slot_sum(ref, count_of, value=None):
        for i in range(count_of):
            term = ref[i].astype(F32)
            value = term if value is None else value + term
        return value

    def start_near(m):
        for j, (z, _) in enumerate(pieces):
            core_sum(m, j)
            for k, o in enumerate(near):
                remote(
                    gone.at[m, z, o], gslot_n.at[m, j, k], gn_send.at[m, j, k], gn_recv.at[m, j], g_devices[k]
                )

    def start_far(m):
        flying[m] = []
        for j, (z, k) in enumerate(pieces):
            if G > 1:
                await_bytes(gslot_n.at[m, j], gn_recv.at[m, j], core_device)
            total = slot_sum(gslot_n.at[m, j], G - 1, gone[m, z, g].astype(F32))
            if k is None:
                gown[m] = total
            else:
                gtwo[m, k] = total.astype(BF16)
                flying[m].append(
                    remote(gtwo.at[m, k], gslot_z.at[m, k], gz_send.at[m, k], gz_recv.at[m, k], z_devices[k])
                )

    def finish(m):
        if m == TURNED:
            return slot_sum(tslot_n, G - 1, gown[m])
        return slot_sum(gslot_z.at[m], A - 1, gown[m])

    def start_far_turned():
        m = TURNED
        copies = []
        for j, (z, k) in enumerate(pieces):
            core_sum(m, j)
            if k is not None:
                copies.append(
                    remote(gone.at[m, z], tslot_z.at[k], gz_send.at[m, k], gz_recv.at[m, k], z_devices[k])
                )
        flying[m] = copies

    def start_near_turned():
        m = TURNED
        arrived(flying[m])
        tback[...] = slot_sum(tslot_z, A - 1, gone[m, a].astype(F32))
        gown[m] = tback[g]
        tlow = gone.at[m, a]
        tlow[...] = tback[...].astype(BF16)
        flying[m] = [
            remote(tlow.at[o], tslot_n.at[k], gn_send.at[m, 0, k], gn_recv.at[m, k], g_devices[k])
            for k, o in enumerate(near)
        ]

    flying = {}
    bias_in = [None] * LAYERS
    bias_out = [None] * LAYERS

    def back_out(l):
        bias_out[l] = jnp.sum(grad[0], axis=0, keepdims=True)
        gb = gbranch[...].reshape(M, D)
        flying[2 * l + 1] = start_core(2 * l + 1, tn(gb, hidden[l].reshape(M, D)))

    def back_in(l):
        gb = gbranch[...].reshape(M, D)
        gh = nn(gb, weight(2 * l + 1)).reshape(4, Pn, D)
        z = pre[l, 0] + small_row(7 + l)
        e = jnp.exp(jnp.minimum(z, 0.0))
        slope = jnp.where(z > 0, 1.0, e)
        curve = jnp.where(z > 0, 0.0, e)
        gz = gh[0] * slope + curve * (gh[1] * pre[l, 1] + gh[2] * pre[l, 2] + gh[3] * pre[l, 3])
        bias_in[l] = jnp.sum(gz, axis=0, keepdims=True)
        gpre[0] = gz.astype(BF16)
        for k in range(1, 4):
            gpre[k] = (gh[k] * slope).astype(BF16)
        flying[2 * l] = start_core(2 * l, tn(acts[l].reshape(M, D), gpre[...].reshape(M, D)))

    def back_through(l):
        back = nt(gpre[...].reshape(M, D), weight(2 * l)).reshape(4, Pn, D)
        for s in range(4):
            value = grad[s] + back[s]
            grad[s] = value
            if l > 0:
                gbranch[s] = value.astype(BF16)

    back_out(1)
    back_in(1)
    start_near(3)
    back_through(1)
    back_out(0)
    start_far_turned()
    back_in(0)
    start_near(1)
    back_through(0)
    start_near(0)

    z0 = inner[...]
    e0 = jnp.exp(jnp.minimum(z0, 0.0))
    slope0 = jnp.where(z0 > 0, 1.0, e0)
    curve0 = jnp.where(z0 > 0, 0.0, e0)
    first_rows = [small_row(j) for j in range(6)]
    g_inner = grad[0] * slope0 + curve0 * (
        grad[1] * first_rows[3] + grad[2] * first_rows[4] + grad[3] * first_rows[5]
    )
    rows = [jnp.sum(xs[j] * g_inner, axis=0, keepdims=True) for j in range(6)]
    for k in range(3):
        rows[3 + k] = rows[3 + k] + jnp.sum(grad[1 + k] * slope0, axis=0, keepdims=True)
    rows.append(jnp.sum(g_inner, axis=0, keepdims=True))
    rows = rows + bias_in + bias_out + [g_out_row]

    lanes = lax.broadcasted_iota(jnp.int32, (1, cw), 1)
    weight_sq = jnp.zeros((1, cw), F32)
    for m in range(MATS):
        part = jnp.sum(master[m // 2, m % 2] * master[m // 2, m % 2], keepdims=True)
        weight_sq = jnp.where(lanes == m, part, weight_sq)
    own_small = spbuf[t]
    weight_sq = jnp.where(lanes == MATS, jnp.sum(own_small * own_small, keepdims=True) / (A * B), weight_sq)
    tail = [
        jnp.broadcast_to(total_err, (1, cw)),
        jnp.broadcast_to(count, (1, cw)),
        weight_sq,
        jnp.zeros((1, cw), F32),
    ]
    for tt in range(n_t):
        sgsend[tt % 2, tt // 2] = jnp.concatenate([r[:, tt * cw : (tt + 1) * cw] for r in rows] + tail, 0)
    sg = [remote(sgsend.at[1 - c], sgcore, s_send.at[0], s_recv.at[0], core_device)]
    arrived(sg)
    sgone[...] = sgsend[c] + sgcore[...]
    sgslot_g[g] = sgone[y]
    sg = [
        remote(sgone.at[o // B], sgslot_g.at[g], s_send.at[S1 + k], s_recv.at[S1 + k], g_devices[k])
        for k, o in enumerate(near)
    ]

    start_far(3)
    start_near_turned()
    start_far(1)
    start_far(0)
    arrived(sg)
    sgtwo[...] = slot_sum(sgslot_g, G)
    sgslot_z[a] = sgtwo[...]
    sg = [
        remote(sgtwo, sgslot_z.at[a], s_send.at[S2 + k], s_recv.at[S2 + k], z_devices[k]) for k in range(A - 1)
    ]

    for copy in local[7:]:
        copy.wait()
    for m in (3, 1, TURNED, 0):
        arrived(flying[m])
        grad_b[m // 2, m % 2] = finish(m)
    arrived(sg)
    sred[...] = slot_sum(sgslot_z, A)
    counted = sred[SMALL + 1 : SMALL + 2, 0:1]
    tile_rows = lax.broadcasted_iota(jnp.int32, (8, 128), 0)
    parts = jnp.zeros((8, 128), F32)

    def step(gradient, momentum):
        new = momentum_coef * momentum + gradient
        return new, gradient + momentum_coef * new

    for m in range(MATS):
        at = (m // 2, m % 2)
        gr = grad_b[at] / counted
        new, direction = step(gr, moment[at])
        grad_b[at] = gr
        moment_b[at] = new
        parts = jnp.where(tile_rows == m, jnp.sum(direction * direction, keepdims=True), parts)
    gr = sred[0:SMALL, :] / counted
    new, dir_small = step(gr, msmall[...])
    grad_s[...] = gr
    moment_s[...] = new
    parts = jnp.where(
        tile_rows == MATS, jnp.sum(dir_small * dir_small, keepdims=True) / (A * B), parts
    )
    me = g * 2 + c
    arslot_g[me] = parts
    ar = [
        remote(arslot_g.at[me], arslot_g.at[me], s_send.at[S3 + k], s_recv.at[S3 + k], d)
        for k, d in enumerate(q_devices)
    ]
    loss_b[...] = sred[SMALL : SMALL + 1, 0:1] / counted
    bias_b[...] = grad_s[7 : 7 + 2 * LAYERS, :]
    arrived(ar)
    artwo[...] = slot_sum(arslot_g, NQ)
    arslot_z[a] = artwo[...]
    ar = [
        remote(artwo, arslot_z.at[a], s_send.at[S5 + k], s_recv.at[S5 + k], d)
        for k, d in enumerate(z_devices)
    ]
    arrived(ar)
    dir_sq = slot_sum(arslot_z, A)

    def rate_of(m):
        size = sred[SMALL + 2 : SMALL + 3, m : m + 1]
        return spread_rate * jnp.sqrt(size) / jnp.sqrt(dir_sq[m : m + 1, 0:1] + norm_epsilon)

    for m in range(MATS):
        at = (m // 2, m % 2)
        direction = grad_b[at] + momentum_coef * moment_b[at]
        new = master[at] - rate_of(m) * direction
        master_b[at] = new
        average_b[at] = average_decay * average[at] + (1.0 - average_decay) * new
        low_b[at] = new.astype(BF16)
    new = own_small - rate_of(MATS) * dir_small
    master_s[...] = new
    average_s[...] = average_decay * asmall[...] + (1.0 - average_decay) * new

    for copy in sends:
        copy.wait_send()


def write_out(*refs):
    sems = refs[-1]
    count = (len(refs) - 1) // 2
    copies = [
        pltpu.make_async_copy(refs[i], refs[count + i], sems.at[i]) for i in range(count)
    ]
    for copy in copies:
        copy.start()
    for copy in copies:
        copy.wait()


def body(
    axes,
    coords,
    model_ids,
    cells,
    valid,
    slowness_grid,
    master_blocks,
    small_params,
    moment_blocks,
    moment_small,
    average_blocks,
    average_small,
):
    n_dp, n_t = axes
    A = 4 if n_dp % 4 == 0 else n_dp
    B = n_dp // A
    C = n_t // 2
    G = C * B
    R, cw = master_blocks.shape[2:]
    D = R * n_dp
    PB = coords.shape[1]
    Pn = PB // n_t
    dims = (A, B, C, R, cw, Pn, D)
    anywhere = pl.BlockSpec(memory_space=pltpu.HBM)
    vmem = pl.BlockSpec(memory_space=pltpu.VMEM)
    S = SMALL + 4
    args = (
        coords,
        model_ids,
        cells,
        valid,
        slowness_grid,
        master_blocks,
        small_params,
        moment_blocks,
        moment_small,
        average_blocks,
        average_small,
    )
    V = pltpu.VMEM
    DMA = pltpu.SemaphoreType.DMA
    block = (master_blocks.shape, F32)
    short = (small_params.shape, F32)
    shapes = [
        ((1, 1), F32),
        block,
        short,
        ((2 * LAYERS, cw), F32),
        block,
        short,
        block,
        short,
        block,
        short,
        (master_blocks.shape, BF16),
    ]
    results = pl.pallas_call(
        functools.partial(kernel, dims),
        out_shape=tuple(V(*shape) for shape in shapes),
        in_specs=[anywhere] * len(args),
        out_specs=(vmem,) * len(shapes),
        scratch_shapes=[
            V(coords.shape, F32),
            V((PB,), jnp.int32),
            V((PB,), jnp.int32),
            V((PB,), jnp.int32),
            V(slowness_grid.shape, F32),
            V(master_blocks.shape, F32),
            V(master_blocks.shape, F32),
            V(small_params.shape, F32),
            V(master_blocks.shape, F32),
            V(small_params.shape, F32),
            V((n_t, SMALL, cw), F32),
            V((PB, 128), F32),
            V((S, cw), F32),
            V((MATS, 2, C, A, B, R, cw), BF16),
            V((4, Pn, D), F32),
            V((LAYERS, 4, Pn, D), BF16),
            V((LAYERS, 4, Pn, D), F32),
            V((LAYERS, 4, Pn, D), BF16),
            V((4, Pn, D), F32),
            V((4, Pn, D), BF16),
            V((4, Pn, D), BF16),
            V((Pn, D), F32),
            V((MATS, 2, A, G, R, cw), BF16),
            V((MATS, A, G, R, cw), BF16),
            V((MATS, A, G, R, cw), BF16),
            V((MATS, A, G - 1, R, cw), BF16),
            V((MATS, A - 1, R, cw), BF16),
            V((MATS, A - 1, R, cw), BF16),
            V((MATS, R, cw), F32),
            V((A - 1, G, R, cw), BF16),
            V((G, R, cw), F32),
            V((G - 1, R, cw), BF16),
            V((2, C, S, cw), F32),
            V((C, S, cw), F32),
            V((C, S, cw), F32),
            V((G, S, cw), F32),
            V((S, cw), F32),
            V((A, S, cw), F32),
            V((2 * G, 8, 128), F32),
            V((8, 128), F32),
            V((A, 8, 128), F32),
            pltpu.SemaphoreType.DMA((len(args),)),
            DMA((MATS, A - 1)),
            DMA((MATS, A - 1)),
            DMA((MATS, A, G - 1)),
            DMA((MATS, G - 1)),
            DMA((G, A - 1)),
            DMA((MATS, max(A, G))),
            DMA((MATS,)),
            DMA((MATS, A - 1)),
            DMA((MATS, A - 1)),
            DMA((MATS, A, G - 1)),
            DMA((MATS, max(A, G - 1))),
            DMA((MATS, A)),
            DMA((MATS, A)),
            pltpu.SemaphoreType.DMA((G + 2 * A + 2 * G + n_t,)),
            pltpu.SemaphoreType.DMA((G + 2 * A + 2 * G + n_t,)),
        ],
        compiler_params=pltpu.CompilerParams(
            collective_id=0, has_side_effects=True, vmem_limit_bytes=60 << 20
        ),
    )(*args)

    results = pl.pallas_call(
        write_out,
        out_shape=tuple(jax.ShapeDtypeStruct(*shape) for shape in shapes),
        in_specs=[vmem] * len(shapes),
        out_specs=(anywhere,) * len(shapes),
        scratch_shapes=[pltpu.SemaphoreType.DMA((len(shapes),))],
        compiler_params=pltpu.CompilerParams(vmem_limit_bytes=4 << 20),
    )(*results)
    return (results[0].reshape(()),) + tuple(results[1:])


def solution(mesh):
    blocks = P(None, None, "dp", "tensor")
    small = P(None, "tensor")
    in_specs = (
        P(None, "dp"),
        P("dp"),
        P("dp"),
        P("dp"),
        P(),
        blocks,
        small,
        blocks,
        small,
        blocks,
        small,
    )
    out_specs = (P(), blocks, small, small, blocks, small, blocks, small, blocks, small, blocks)
    axes = (mesh.shape["dp"], mesh.shape["tensor"])
    return jax.shard_map(
        functools.partial(body, axes), mesh=mesh, in_specs=in_specs, out_specs=out_specs, check_vma=False
    )
```

```python
import functools

import jax
import jax.numpy as jnp
from jax import lax
from jax.experimental import pallas as pl
from jax.experimental.pallas import tpu as pltpu
from jax.sharding import PartitionSpec as P

LAYERS = 2
MATS = 2 * LAYERS
SMALL = 12
MESH = pl.DeviceIdType.MESH
F32 = jnp.float32
BF16 = jnp.bfloat16

momentum_coef = 0.5
average_decay = 0.5
spread_rate = 0.5
norm_epsilon = 1e-12

TURNED = 2


def partner(i, k, size):
    bit = 1
    while bit < size:
        if (k // bit) % 2:
            i = i + bit - 2 * bit * ((i // bit) % 2)
        bit *= 2
    return i


def nn(left, right):
    return lax.dot_general(left, right, (((1,), (0,)), ((), ())), preferred_element_type=F32)


def nt(left, right):
    return lax.dot_general(left, right, (((1,), (1,)), ((), ())), preferred_element_type=F32)


def tn(left, right):
    return lax.dot_general(left, right, (((0,), (0,)), ((), ())), preferred_element_type=F32)


def sign_of(v):
    return jnp.where(v > 0, 1.0, jnp.where(v < 0, -1.0, 0.0))


def kernel(
    dims,
    coords_hbm,
    model_hbm,
    cells_hbm,
    valid_hbm,
    grid_hbm,
    master_hbm,
    small_hbm,
    moment_hbm,
    msmall_hbm,
    average_hbm,
    asmall_hbm,
    loss_b,
    grad_b,
    grad_s,
    bias_b,
    moment_b,
    moment_s,
    master_b,
    master_s,
    average_b,
    average_s,
    low_b,
    coords,
    model,
    cells,
    valid,
    grid,
    master,
    moment,
    msmall,
    average,
    asmall,
    spbuf,
    columns,
    sred,
    wbuf,
    streams,
    acts,
    pre,
    hidden,
    grad,
    gbranch,
    gpre,
    inner,
    gsend,
    gcore,
    gone,
    gslot_n,
    gtwo,
    gslot_z,
    gown,
    tslot_z,
    tback,
    tslot_n,
    sgsend,
    sgcore,
    sgone,
    sgslot_g,
    sgtwo,
    sgslot_z,
    arslot,
    in_sem,
    w_send,
    wz_recv,
    wn_recv,
    wc_recv,
    g_send,
    gz_recv,
    gn_recv,
    gc_recv,
    s_send,
    s_recv,
):
    A, B, C, R, cw, Pn, D = dims
    n_t = 2 * C
    G = C * B
    dp = lax.axis_index("dp")
    t = lax.axis_index("tensor")
    a, b = dp // B, dp % B
    y, c = t // 2, t % 2
    g = y * B + b

    def device(a_, g_, c_):
        return (a_ * B + g_ % B, (g_ // B) * 2 + c_)

    far = [partner(a, k, A) for k in range(1, A)]
    near = [partner(g, k, G) for k in range(1, G)]
    z_devices = [device(o, g, c) for o in far]
    g_devices = [device(a, o, c) for o in near]
    core_device = device(a, g, 1 - c)
    q_devices = [device(a, partner(g, kg, G), partner(c, kc, 2)) for kg in range(G) for kc in range(2)][1:]
    steps = [(ka, kg, kc) for ka in range(A) for kg in range(G) for kc in range(2)][1:]
    steps.sort(key=lambda step: -(step[0] + bin(step[1]).count("1") + step[2] / 2))
    everyone = [device(partner(a, ka, A), partner(g, kg, G), partner(c, kc, 2)) for ka, kg, kc in steps]
    others = [d for d, step in zip(everyone, steps) if step[0] and (step[1] or step[2])]

    WZ, WN, WT, WP, WC = range(5)
    S_CORE, S_NEAR, S_FAR, S_ALL, S_PAR = range(5)

    def remote(src, dst, ssem, rsem, device_id):
        copy = pltpu.make_async_remote_copy(
            src_ref=src,
            dst_ref=dst,
            send_sem=ssem,
            recv_sem=rsem,
            device_id=device_id,
            device_id_type=MESH,
        )
        copy.start()
        return copy

    def arrived(copies):
        for copy in copies:
            copy.wait_recv()

    local = []
    for i, (src, dst) in enumerate(
        [
            (master_hbm, master),
            (small_hbm, spbuf.at[t]),
            (coords_hbm, coords),
            (model_hbm, model),
            (cells_hbm, cells),
            (valid_hbm, valid),
            (grid_hbm, grid),
            (moment_hbm, moment),
            (msmall_hbm, msmall),
            (average_hbm, average),
            (asmall_hbm, asmall),
        ]
    ):
        copy = pltpu.make_async_copy(src, dst, in_sem.at[i])
        copy.start()
        local.append(copy)

    barrier = pltpu.get_barrier_semaphore()
    peers = z_devices + q_devices
    for d in peers:
        pl.semaphore_signal(barrier, inc=1, device_id=d, device_id_type=MESH)

    local[0].wait()
    for m in range(MATS):
        wbuf[m, c, y, a, b] = master[m // 2, m % 2].astype(BF16)
    local[1].wait()
    pl.semaphore_wait(barrier, len(peers))

    def piece(m, o, z):
        return wbuf.at[m, c, o // B, z, o % B]

    def line(m, o):
        return wbuf.at[m, c, o // B, :, o % B]

    def plane(m, z):
        return wbuf.at[m, c, :, z]

    def await_bytes(ref, rsem):
        pltpu.make_async_remote_copy(
            src_ref=ref,
            dst_ref=ref,
            send_sem=s_send.at[0],
            recv_sem=rsem,
            device_id=core_device,
            device_id_type=MESH,
        ).wait_recv()

    def await_sent(ref, ssem):
        pltpu.make_async_remote_copy(
            src_ref=ref,
            dst_ref=ref,
            send_sem=ssem,
            recv_sem=s_recv.at[0],
            device_id=core_device,
            device_id_type=MESH,
        ).wait_send()

    def w_far(m, ref):
        return [
            remote(ref, ref, w_send.at[WZ], wz_recv.at[m, k], d) for k, d in enumerate(z_devices)
        ]

    def w_near(m, ref, j):
        return [
            remote(ref, ref, w_send.at[WT if m == TURNED else WN], wn_recv.at[m, k], d)
            for k, d in enumerate(g_devices)
        ]

    def w_far_turned(ref, j):
        for k, d in enumerate(z_devices):
            remote(ref, ref, w_send.at[WP], wz_recv.at[TURNED, k], d)

    def w_core(m, ref, j):
        remote(ref, ref, w_send.at[WC], wc_recv.at[m], core_device)

    straight = [m for m in range(MATS) if m != TURNED]
    for k in range(1, n_t):
        o = (t + k) % n_t
        remote(spbuf.at[t], spbuf.at[t], s_send.at[S_PAR], s_recv.at[S_PAR], (dp, o))
    first = {}
    for i, m in enumerate(straight):
        first[m] = w_far(m, piece(m, g, a))
        if i == 0:
            first[TURNED] = w_near(TURNED, piece(TURNED, g, a), 0)
    for i, m in enumerate(straight):
        w_near(m, piece(m, g, a), 0)
        if i == 0:
            w_far_turned(piece(TURNED, g, a), 0)

    for copy in local[2:7]:
        copy.wait()
    cols = grid.shape[2]
    shift = (cols - 1).bit_length()
    cell = cells[...].reshape(1, -1)
    row_id = model[...].reshape(1, -1) * grid.shape[1] + (cell >> shift)
    col_id = cell & (cols - 1)
    PB = row_id.shape[1]
    packed = jnp.concatenate(
        [
            coords[...],
            row_id.astype(F32),
            col_id.astype(F32),
            valid[...].reshape(1, -1).astype(F32),
            jnp.zeros((128 - 9, PB), F32),
        ],
        0,
    )
    columns[...] = packed.T
    mine = columns[pl.ds(pl.multiple_of(t * Pn, 8), Pn), :]
    xs = [mine[:, j : j + 1] for j in range(6)]
    mask = mine[:, 8:9]
    row_of = mine[:, 6:7].astype(jnp.int32)
    col_of = mine[:, 7:8].astype(jnp.int32)
    table = grid[...].reshape(-1, cols)
    onehot = (
        lax.broadcasted_iota(jnp.int32, (Pn, table.shape[0]), 1) == row_of
    ).astype(BF16)
    high = table.astype(BF16)
    rest = table - high.astype(F32)
    middle = rest.astype(BF16)
    lowest = (rest - middle.astype(F32)).astype(BF16)
    picked = nn(onehot, high) + nn(onehot, middle) + nn(onehot, lowest)
    lane = lax.broadcasted_iota(jnp.int32, (Pn, cols), 1)
    truth = jnp.sum(jnp.where(lane == col_of, picked, 0.0), 1, keepdims=True)
    seps = [xs[3 + k] - xs[k] for k in range(3)]
    distance = jnp.sqrt(seps[0] * seps[0] + seps[1] * seps[1] + seps[2] * seps[2])
    units = [s / distance for s in seps]

    await_bytes(spbuf.at[pl.ds(0, n_t - 1)], s_recv.at[S_PAR])

    def small_row(i):
        return jnp.concatenate([spbuf[tt, i : i + 1, :] for tt in range(n_t)], 1)

    first_rows = [small_row(j) for j in range(6)]
    z0 = small_row(6) + xs[0] * first_rows[0]
    for j in range(1, 6):
        z0 = z0 + xs[j] * first_rows[j]
    inner[...] = z0
    e0 = jnp.exp(jnp.minimum(z0, 0.0))
    slope0 = jnp.where(z0 > 0, 1.0, e0)
    streams[0] = jnp.where(z0 > 0, z0, e0 - 1.0)
    acts[0, 0] = streams[0].astype(BF16)
    for k in range(3):
        streams[1 + k] = slope0 * first_rows[3 + k]
        acts[0, 1 + k] = streams[1 + k].astype(BF16)

    def pass_on(m):
        for k in range(A - 1):
            first[m][k].wait_recv()
            w_near(m, piece(m, g, far[k]), k + 1)
        w_core(m, line(m, g), 0)

    def pass_on_turned():
        for k in range(G - 1):
            first[TURNED][k].wait_recv()
            w_far_turned(piece(TURNED, near[k], a), k + 1)
        w_core(TURNED, plane(TURNED, a), 0)

    pass_on(straight[0])
    pass_on_turned()
    for m in straight[1:]:
        pass_on(m)

    def weight(m):
        return jnp.concatenate([wbuf[m, tt % 2, tt // 2].reshape(D, cw) for tt in range(n_t)], 1)

    M = 4 * Pn

    def block_in(l):
        pre[l] = nn(acts[l].reshape(M, D), weight(2 * l)).reshape(4, Pn, D)
        z = pre[l, 0] + small_row(7 + l)
        e = jnp.exp(jnp.minimum(z, 0.0))
        slope = jnp.where(z > 0, 1.0, e)
        hidden[l, 0] = jnp.where(z > 0, z, e - 1.0).astype(BF16)
        for k in range(1, 4):
            hidden[l, k] = (slope * pre[l, k]).astype(BF16)

    def block_out(l):
        branch = nt(hidden[l].reshape(M, D), weight(2 * l + 1)).reshape(4, Pn, D)
        for s in range(4):
            new = streams[s] + branch[s]
            if s == 0:
                new = new + small_row(7 + LAYERS + l)
            streams[s] = new
            if l + 1 < LAYERS:
                acts[l + 1, s] = new.astype(BF16)

    def fetch(m):
        if m == TURNED:
            for k in range(A - 1):
                await_bytes(plane(m, far[k]), wz_recv.at[m, k])
                w_core(m, plane(m, far[k]), k + 1)
        else:
            for k in range(G - 1):
                await_bytes(line(m, near[k]), wn_recv.at[m, k])
                w_core(m, line(m, near[k]), k + 1)

    def fetched(m):
        await_bytes(wbuf.at[m, c], wc_recv.at[m])

    for m in range(MATS):
        fetch(m)
        fetched(m)
        if m == 0:
            for d in others:
                pl.semaphore_signal(barrier, inc=1, device_id=d, device_id_type=MESH)
        if m % 2 == 0:
            block_in(m // 2)
        else:
            block_out(m // 2)

    out_row = small_row(7 + 2 * LAYERS)
    proj = [jnp.sum(streams[s] * out_row, 1, keepdims=True) for s in range(4)]
    tau = proj[0]
    sign_tau = sign_of(tau)
    abs_tau = jnp.abs(tau)
    grad_time = [units[k] * abs_tau + distance * sign_tau * proj[1 + k] for k in range(3)]
    square = grad_time[0] * grad_time[0] + grad_time[1] * grad_time[1] + grad_time[2] * grad_time[2]
    error = square - truth * truth
    total_err = jnp.sum(mask * jnp.abs(error), axis=0, keepdims=True)
    count = jnp.sum(mask, axis=0, keepdims=True)
    seed = mask * sign_of(error)
    g_time = [2.0 * grad_time[k] * seed for k in range(3)]
    g_tau = sign_tau * (units[0] * g_time[0] + units[1] * g_time[1] + units[2] * g_time[2])
    g_proj = [g_tau] + [distance * sign_tau * g_time[k] for k in range(3)]
    g_out_row = jnp.sum(
        streams[0] * g_proj[0] + streams[1] * g_proj[1] + streams[2] * g_proj[2] + streams[3] * g_proj[3],
        axis=0,
        keepdims=True,
    )
    for s in range(4):
        value = g_proj[s] * out_row
        grad[s] = value
        gbranch[s] = value.astype(BF16)

    pieces = [(far[k], k) for k in reversed(range(A - 1))] + [(a, None)]

    def start_core(m, value):
        low = value.astype(BF16)
        for tt in range(n_t):
            block = low[:, tt * cw : (tt + 1) * cw].reshape(A, B, R, cw)
            for i in range(B):
                gsend[m, tt % 2, :, (tt // 2) * B + i] = block[:, i]
        return [
            remote(
                gsend.at[m, 1 - c, z], gcore.at[m, z], g_send.at[WC], gc_recv.at[m, j], core_device
            )
            for j, (z, k) in enumerate(pieces)
        ]

    def core_sum(m, j):
        z = pieces[j][0]
        flying[m][j].wait_recv()
        gone[m, z] = (gsend[m, c, z].astype(F32) + gcore[m, z].astype(F32)).astype(BF16)

    def slot_sum(ref, count_of, value=None):
        for i in range(count_of):
            term = ref[i].astype(F32)
            value = term if value is None else value + term
        return value

    def start_near(m):
        for j, (z, _) in enumerate(pieces):
            core_sum(m, j)
            for k, o in enumerate(near):
                remote(
                    gone.at[m, z, o], gslot_n.at[m, j, k], g_send.at[WN], gn_recv.at[m, j], g_devices[k]
                )

    def start_far(m):
        for j, (z, k) in enumerate(pieces):
            if G > 1:
                await_bytes(gslot_n.at[m, j], gn_recv.at[m, j])
            total = slot_sum(gslot_n.at[m, j], G - 1, gone[m, z, g].astype(F32))
            if k is None:
                gown[m] = total
            else:
                gtwo[m, k] = total.astype(BF16)
                remote(gtwo.at[m, k], gslot_z.at[m, k], g_send.at[WZ], gz_recv.at[m], z_devices[k])

    def finish(m):
        if m == TURNED:
            await_bytes(tslot_n, gn_recv.at[m, 0])
            return slot_sum(tslot_n, G - 1, gown[m])
        await_bytes(gslot_z.at[m], gz_recv.at[m])
        return slot_sum(gslot_z.at[m], A - 1, gown[m])

    def start_far_turned():
        m = TURNED
        for j, (z, k) in enumerate(pieces):
            core_sum(m, j)
            if k is not None:
                remote(gone.at[m, z], tslot_z.at[k], g_send.at[WP], gz_recv.at[m], z_devices[k])

    def start_near_turned():
        m = TURNED
        await_bytes(tslot_z, gz_recv.at[m])
        tback[...] = slot_sum(tslot_z, A - 1, gone[m, a].astype(F32))
        gown[m] = tback[g]
        tlow = gone.at[m, a]
        tlow[...] = tback[...].astype(BF16)
        for k, o in enumerate(near):
            remote(tlow.at[o], tslot_n.at[k], g_send.at[WT], gn_recv.at[m, 0], g_devices[k])

    flying = {}
    bias_in = [None] * LAYERS
    bias_out = [None] * LAYERS

    def back_out(l):
        bias_out[l] = jnp.sum(grad[0], axis=0, keepdims=True)
        gb = gbranch[...].reshape(M, D)
        flying[2 * l + 1] = start_core(2 * l + 1, tn(gb, hidden[l].reshape(M, D)))

    def back_in(l):
        gb = gbranch[...].reshape(M, D)
        gh = nn(gb, weight(2 * l + 1)).reshape(4, Pn, D)
        z = pre[l, 0] + small_row(7 + l)
        e = jnp.exp(jnp.minimum(z, 0.0))
        slope = jnp.where(z > 0, 1.0, e)
        curve = jnp.where(z > 0, 0.0, e)
        gz = gh[0] * slope + curve * (gh[1] * pre[l, 1] + gh[2] * pre[l, 2] + gh[3] * pre[l, 3])
        bias_in[l] = jnp.sum(gz, axis=0, keepdims=True)
        gpre[0] = gz.astype(BF16)
        for k in range(1, 4):
            gpre[k] = (gh[k] * slope).astype(BF16)

    def back_weight(l):
        flying[2 * l] = start_core(2 * l, tn(acts[l].reshape(M, D), gpre[...].reshape(M, D)))

    def back_through(l):
        back = nt(gpre[...].reshape(M, D), weight(2 * l)).reshape(4, Pn, D)
        for s in range(4):
            value = grad[s] + back[s]
            grad[s] = value
            if l > 0:
                gbranch[s] = value.astype(BF16)

    back_out(1)
    back_in(1)
    start_near(3)
    back_weight(1)
    back_through(1)
    start_far_turned()
    back_out(0)
    back_in(0)
    start_near(1)
    back_weight(0)
    back_through(0)
    start_near(0)

    z0 = inner[...]
    e0 = jnp.exp(jnp.minimum(z0, 0.0))
    slope0 = jnp.where(z0 > 0, 1.0, e0)
    curve0 = jnp.where(z0 > 0, 0.0, e0)
    first_rows = [small_row(j) for j in range(6)]
    g_inner = grad[0] * slope0 + curve0 * (
        grad[1] * first_rows[3] + grad[2] * first_rows[4] + grad[3] * first_rows[5]
    )
    rows = [jnp.sum(xs[j] * g_inner, axis=0, keepdims=True) for j in range(6)]
    for k in range(3):
        rows[3 + k] = rows[3 + k] + jnp.sum(grad[1 + k] * slope0, axis=0, keepdims=True)
    rows.append(jnp.sum(g_inner, axis=0, keepdims=True))
    rows = rows + bias_in + bias_out + [g_out_row]

    lanes = lax.broadcasted_iota(jnp.int32, (1, cw), 1)
    weight_sq = jnp.zeros((1, cw), F32)
    for m in range(MATS):
        part = jnp.sum(master[m // 2, m % 2] * master[m // 2, m % 2], keepdims=True)
        weight_sq = jnp.where(lanes == m, part, weight_sq)
    own_small = spbuf[t]
    weight_sq = jnp.where(lanes == MATS, jnp.sum(own_small * own_small, keepdims=True) / (A * B), weight_sq)
    tail = [
        jnp.broadcast_to(total_err, (1, cw)),
        jnp.broadcast_to(count, (1, cw)),
        weight_sq,
        jnp.zeros((1, cw), F32),
    ]
    for tt in range(n_t):
        sgsend[tt % 2, tt // 2] = jnp.concatenate([r[:, tt * cw : (tt + 1) * cw] for r in rows] + tail, 0)
    remote(sgsend.at[1 - c], sgcore, s_send.at[S_CORE], s_recv.at[S_CORE], core_device)
    start_far(3)
    await_bytes(sgcore, s_recv.at[S_CORE])
    sgone[...] = sgsend[c] + sgcore[...]
    sgslot_g[g] = sgone[y]
    for k, o in enumerate(near):
        remote(sgone.at[o // B], sgslot_g.at[g], s_send.at[S_NEAR], s_recv.at[S_NEAR], g_devices[k])

    start_far(1)
    start_near_turned()
    start_far(0)
    await_bytes(sgslot_g.at[pl.ds(0, G - 1)], s_recv.at[S_NEAR])
    sgtwo[...] = slot_sum(sgslot_g, G)
    sgslot_z[a] = sgtwo[...]
    for d in z_devices:
        remote(sgtwo, sgslot_z.at[a], s_send.at[S_FAR], s_recv.at[S_FAR], d)

    for copy in local[7:]:
        copy.wait()
    for m in (3, 1, TURNED, 0):
        grad_b[m // 2, m % 2] = finish(m)
    await_bytes(sgslot_z.at[pl.ds(0, A - 1)], s_recv.at[S_FAR])
    sred[...] = slot_sum(sgslot_z, A)
    counted = sred[SMALL + 1 : SMALL + 2, 0:1]
    tile_rows = lax.broadcasted_iota(jnp.int32, (8, 128), 0)
    parts = jnp.zeros((8, 128), F32)

    def step(gradient, momentum):
        new = momentum_coef * momentum + gradient
        return new, gradient + momentum_coef * new

    for m in range(MATS):
        at = (m // 2, m % 2)
        gr = grad_b[at] / counted
        new, direction = step(gr, moment[at])
        grad_b[at] = gr
        moment_b[at] = new
        parts = jnp.where(tile_rows == m, jnp.sum(direction * direction, keepdims=True), parts)
    gr = sred[0:SMALL, :] / counted
    new, dir_small = step(gr, msmall[...])
    grad_s[...] = gr
    moment_s[...] = new
    parts = jnp.where(
        tile_rows == MATS, jnp.sum(dir_small * dir_small, keepdims=True) / (A * B), parts
    )
    me = (a * G + g) * 2 + c
    arslot[me] = parts
    pl.semaphore_wait(barrier, len(others))
    for d in everyone:
        remote(arslot.at[me], arslot.at[me], s_send.at[S_ALL], s_recv.at[S_ALL], d)
    loss_b[...] = sred[SMALL : SMALL + 1, 0:1] / counted
    bias_b[...] = grad_s[7 : 7 + 2 * LAYERS, :]
    await_bytes(arslot.at[pl.ds(0, len(everyone))], s_recv.at[S_ALL])
    dir_sq = jnp.sum(arslot[...], axis=0)

    def rate_of(m):
        size = sred[SMALL + 2 : SMALL + 3, m : m + 1]
        return spread_rate * jnp.sqrt(size) / jnp.sqrt(dir_sq[m : m + 1, 0:1] + norm_epsilon)

    for m in range(MATS):
        at = (m // 2, m % 2)
        direction = grad_b[at] + momentum_coef * moment_b[at]
        new = master[at] - rate_of(m) * direction
        master_b[at] = new
        average_b[at] = average_decay * average[at] + (1.0 - average_decay) * new
        low_b[at] = new.astype(BF16)
    new = own_small - rate_of(MATS) * dir_small
    master_s[...] = new
    average_s[...] = average_decay * asmall[...] + (1.0 - average_decay) * new

    straights, nears, fars = pl.ds(0, MATS - 1), pl.ds(0, G - 1), pl.ds(0, A - 1)
    for sems in (w_send, g_send):
        await_sent(gone.at[straights, fars, 0], sems.at[WZ])
        await_sent(gone.at[straights, :, nears], sems.at[WN])
        await_sent(gone.at[0, 0, nears], sems.at[WT])
        await_sent(gone.at[0, fars], sems.at[WP])
        await_sent(gone, sems.at[WC])
    await_sent(sgcore, s_send.at[S_CORE])
    await_sent(sgslot_g.at[nears], s_send.at[S_NEAR])
    await_sent(sgslot_z.at[fars], s_send.at[S_FAR])
    await_sent(arslot.at[pl.ds(0, len(everyone))], s_send.at[S_ALL])
    await_sent(spbuf.at[pl.ds(0, n_t - 1)], s_send.at[S_PAR])


def write_out(*refs):
    sems = refs[-1]
    count = (len(refs) - 1) // 2
    copies = [
        pltpu.make_async_copy(refs[i], refs[count + i], sems.at[i]) for i in range(count)
    ]
    for copy in copies:
        copy.start()
    for copy in copies:
        copy.wait()


def body(
    axes,
    coords,
    model_ids,
    cells,
    valid,
    slowness_grid,
    master_blocks,
    small_params,
    moment_blocks,
    moment_small,
    average_blocks,
    average_small,
):
    n_dp, n_t = axes
    A = 4 if n_dp % 4 == 0 else n_dp
    B = n_dp // A
    C = n_t // 2
    G = C * B
    R, cw = master_blocks.shape[2:]
    D = R * n_dp
    PB = coords.shape[1]
    Pn = PB // n_t
    dims = (A, B, C, R, cw, Pn, D)
    anywhere = pl.BlockSpec(memory_space=pltpu.HBM)
    vmem = pl.BlockSpec(memory_space=pltpu.VMEM)
    S = SMALL + 4
    args = (
        coords,
        model_ids,
        cells,
        valid,
        slowness_grid,
        master_blocks,
        small_params,
        moment_blocks,
        moment_small,
        average_blocks,
        average_small,
    )
    V = pltpu.VMEM
    DMA = pltpu.SemaphoreType.DMA
    block = (master_blocks.shape, F32)
    short = (small_params.shape, F32)
    shapes = [
        ((1, 1), F32),
        block,
        short,
        ((2 * LAYERS, cw), F32),
        block,
        short,
        block,
        short,
        block,
        short,
        (master_blocks.shape, BF16),
    ]
    results = pl.pallas_call(
        functools.partial(kernel, dims),
        out_shape=tuple(V(*shape) for shape in shapes),
        in_specs=[anywhere] * len(args),
        out_specs=(vmem,) * len(shapes),
        scratch_shapes=[
            V(coords.shape, F32),
            V((PB,), jnp.int32),
            V((PB,), jnp.int32),
            V((PB,), jnp.int32),
            V(slowness_grid.shape, F32),
            V(master_blocks.shape, F32),
            V(master_blocks.shape, F32),
            V(small_params.shape, F32),
            V(master_blocks.shape, F32),
            V(small_params.shape, F32),
            V((n_t, SMALL, cw), F32),
            V((PB, 128), F32),
            V((S, cw), F32),
            V((MATS, 2, C, A, B, R, cw), BF16),
            V((4, Pn, D), F32),
            V((LAYERS, 4, Pn, D), BF16),
            V((LAYERS, 4, Pn, D), F32),
            V((LAYERS, 4, Pn, D), BF16),
            V((4, Pn, D), F32),
            V((4, Pn, D), BF16),
            V((4, Pn, D), BF16),
            V((Pn, D), F32),
            V((MATS, 2, A, G, R, cw), BF16),
            V((MATS, A, G, R, cw), BF16),
            V((MATS, A, G, R, cw), BF16),
            V((MATS, A, G - 1, R, cw), BF16),
            V((MATS, A - 1, R, cw), BF16),
            V((MATS, A - 1, R, cw), BF16),
            V((MATS, R, cw), F32),
            V((A - 1, G, R, cw), BF16),
            V((G, R, cw), F32),
            V((G - 1, R, cw), BF16),
            V((2, C, S, cw), F32),
            V((C, S, cw), F32),
            V((C, S, cw), F32),
            V((G, S, cw), F32),
            V((S, cw), F32),
            V((A, S, cw), F32),
            V((2 * A * G, 8, 128), F32),
            pltpu.SemaphoreType.DMA((len(args),)),
            DMA((5,)),
            DMA((MATS, A - 1)),
            DMA((MATS, G - 1)),
            DMA((MATS,)),
            DMA((5,)),
            DMA((MATS,)),
            DMA((MATS, A)),
            DMA((MATS, A)),
            DMA((5,)),
            DMA((5,)),
        ],
        compiler_params=pltpu.CompilerParams(
            collective_id=0, has_side_effects=True, vmem_limit_bytes=60 << 20
        ),
    )(*args)

    results = pl.pallas_call(
        write_out,
        out_shape=tuple(jax.ShapeDtypeStruct(*shape) for shape in shapes),
        in_specs=[vmem] * len(shapes),
        out_specs=(anywhere,) * len(shapes),
        scratch_shapes=[pltpu.SemaphoreType.DMA((len(shapes),))],
        compiler_params=pltpu.CompilerParams(vmem_limit_bytes=4 << 20),
    )(*results)
    return (results[0].reshape(()),) + tuple(results[1:])


def solution(mesh):
    blocks = P(None, None, "dp", "tensor")
    small = P(None, "tensor")
    in_specs = (
        P(None, "dp"),
        P("dp"),
        P("dp"),
        P("dp"),
        P(),
        blocks,
        small,
        blocks,
        small,
        blocks,
        small,
    )
    out_specs = (P(), blocks, small, small, blocks, small, blocks, small, blocks, small, blocks)
    axes = (mesh.shape["dp"], mesh.shape["tensor"])
    return jax.shard_map(
        functools.partial(body, axes), mesh=mesh, in_specs=in_specs, out_specs=out_specs, check_vma=False
    )
```

```python
import functools

import jax
import jax.numpy as jnp
from jax import lax
from jax.experimental import pallas as pl
from jax.experimental.pallas import tpu as pltpu
from jax.sharding import PartitionSpec as P

LAYERS = 2
MATS = 2 * LAYERS
SMALL = 12
MESH = pl.DeviceIdType.MESH
F32 = jnp.float32
BF16 = jnp.bfloat16

momentum_coef = 0.5
average_decay = 0.5
spread_rate = 0.5
norm_epsilon = 1e-12

MOVED = MATS - 1
W_TURNED = 2
G_TURNED = None


def partner(i, k, size):
    bit = 1
    while bit < size:
        if (k // bit) % 2:
            i = i + bit - 2 * bit * ((i // bit) % 2)
        bit *= 2
    return i


def nn(left, right):
    return lax.dot_general(left, right, (((1,), (0,)), ((), ())), preferred_element_type=F32)


def nt(left, right):
    return lax.dot_general(left, right, (((1,), (1,)), ((), ())), preferred_element_type=F32)


def tn(left, right):
    return lax.dot_general(left, right, (((0,), (0,)), ((), ())), preferred_element_type=F32)


def sign_of(v):
    return jnp.where(v > 0, 1.0, jnp.where(v < 0, -1.0, 0.0))


def kernel(
    dims,
    coords_hbm,
    model_hbm,
    cells_hbm,
    valid_hbm,
    grid_hbm,
    master_hbm,
    small_hbm,
    moment_hbm,
    msmall_hbm,
    average_hbm,
    asmall_hbm,
    loss_b,
    grad_b,
    grad_s,
    bias_b,
    moment_b,
    moment_s,
    master_b,
    master_s,
    average_b,
    average_s,
    low_b,
    coords,
    model,
    cells,
    valid,
    grid,
    master,
    moment,
    msmall,
    average,
    asmall,
    spbuf,
    columns,
    sred,
    wbuf,
    streams,
    acts,
    pre,
    hidden,
    grad,
    gbranch,
    gpre,
    inner,
    gsend,
    gcore,
    gone,
    gslot_n,
    gtwo,
    gslot_z,
    gown,
    tslot_z,
    tback,
    tslot_n,
    sgsend,
    psend,
    pslot,
    pdone,
    sgslot_g,
    sgtwo,
    sgslot_z,
    arslot,
    qslot_z,
    qslot_g,
    vsend,
    vslot_g,
    vslot_z,
    in_sem,
    w_send,
    wz_recv,
    wn_recv,
    wc_recv,
    g_send,
    gz_recv,
    gn_recv,
    gc_recv,
    s_send,
    s_recv,
):
    A, B, C, R, cw, Pn, D = dims
    n_t = 2 * C
    G = C * B
    dp = lax.axis_index("dp")
    t = lax.axis_index("tensor")
    a, b = dp // B, dp % B
    y, c = t // 2, t % 2
    g = y * B + b

    def device(a_, g_, c_):
        return (a_ * B + g_ % B, (g_ // B) * 2 + c_)

    far = [partner(a, k, A) for k in range(1, A)]
    near = [partner(g, k, G) for k in range(1, G)]
    z_devices = [device(o, g, c) for o in far]
    g_devices = [device(a, o, c) for o in near]
    core_device = device(a, g, 1 - c)
    q_coords = [(partner(g, kg, G), partner(c, kc, 2)) for kg in range(G) for kc in range(2)][1:]
    q_devices = [device(a, o, cc) for o, cc in q_coords]
    steps = [(ka, kg, kc) for ka in range(A) for kg in range(G) for kc in range(2)][1:]
    steps.sort(key=lambda step: -(step[0] + bin(step[1]).count("1") + step[2] / 2))
    everyone = [device(partner(a, ka, A), partner(g, kg, G), partner(c, kc, 2)) for ka, kg, kc in steps]
    others = [d for d, step in zip(everyone, steps) if step[0] and (step[1] or step[2])]

    WZ, WN, WT, WP, WC = range(5)
    S_PROD, S_NEAR, S_FAR, S_ALL, S_PAR, S_QFAR, S_QNEAR, S_VNEAR, S_VFAR = range(9)

    def remote(src, dst, ssem, rsem, device_id):
        copy = pltpu.make_async_remote_copy(
            src_ref=src,
            dst_ref=dst,
            send_sem=ssem,
            recv_sem=rsem,
            device_id=device_id,
            device_id_type=MESH,
        )
        copy.start()
        return copy

    def arrived(copies):
        for copy in copies:
            copy.wait_recv()

    nears, fars = pl.ds(0, G - 1), pl.ds(0, A - 1)

    local = []
    for i, (src, dst) in enumerate(
        [
            (master_hbm, master),
            (small_hbm, spbuf.at[t]),
            (coords_hbm, coords),
            (model_hbm, model),
            (cells_hbm, cells),
            (valid_hbm, valid),
            (grid_hbm, grid),
            (moment_hbm, moment),
            (msmall_hbm, msmall),
            (average_hbm, average),
            (asmall_hbm, asmall),
        ]
    ):
        copy = pltpu.make_async_copy(src, dst, in_sem.at[i])
        copy.start()
        local.append(copy)

    barrier = pltpu.get_barrier_semaphore()
    peers = z_devices + q_devices
    for d in peers:
        pl.semaphore_signal(barrier, inc=1, device_id=d, device_id_type=MESH)

    local[0].wait()
    for m in range(MOVED):
        wbuf[m, c, y, a, b] = master[m // 2, m % 2].astype(BF16)
    local[1].wait()
    pl.semaphore_wait(barrier, len(peers))

    def piece(m, o, z):
        return wbuf.at[m, c, o // B, z, o % B]

    def line(m, o):
        return wbuf.at[m, c, o // B, :, o % B]

    def plane(m, z):
        return wbuf.at[m, c, :, z]

    def await_bytes(ref, rsem):
        pltpu.make_async_remote_copy(
            src_ref=ref,
            dst_ref=ref,
            send_sem=s_send.at[0],
            recv_sem=rsem,
            device_id=core_device,
            device_id_type=MESH,
        ).wait_recv()

    def slot_sum(ref, count_of, value=None):
        for i in range(count_of):
            term = ref[i].astype(F32)
            value = term if value is None else value + term
        return value

    def await_sent(ref, ssem):
        pltpu.make_async_remote_copy(
            src_ref=ref,
            dst_ref=ref,
            send_sem=ssem,
            recv_sem=s_recv.at[0],
            device_id=core_device,
            device_id_type=MESH,
        ).wait_send()

    def w_far(m, ref):
        return [
            remote(ref, ref, w_send.at[WZ], wz_recv.at[m, k], d) for k, d in enumerate(z_devices)
        ]

    def w_near(m, ref, j):
        return [
            remote(ref, ref, w_send.at[WT if m == W_TURNED else WN], wn_recv.at[m, k], d)
            for k, d in enumerate(g_devices)
        ]

    def w_far_turned(ref, j):
        for k, d in enumerate(z_devices):
            remote(ref, ref, w_send.at[WP], wz_recv.at[W_TURNED, k], d)

    def w_core(m, ref, j):
        remote(ref, ref, w_send.at[WC], wc_recv.at[m], core_device)

    straight = [m for m in range(MOVED) if m != W_TURNED]
    for k in range(1, n_t):
        o = (t + k) % n_t
        remote(spbuf.at[t], spbuf.at[t], s_send.at[S_PAR], s_recv.at[S_PAR], (dp, o))
    first = {}
    for i, m in enumerate(straight):
        first[m] = w_far(m, piece(m, g, a))
        if i == 0 and W_TURNED is not None:
            first[W_TURNED] = w_near(W_TURNED, piece(W_TURNED, g, a), 0)
    for i, m in enumerate(straight):
        w_near(m, piece(m, g, a), 0)
        if i == 0 and W_TURNED is not None:
            w_far_turned(piece(W_TURNED, g, a), 0)

    for copy in local[2:7]:
        copy.wait()
    cols = grid.shape[2]
    shift = (cols - 1).bit_length()
    cell = cells[...].reshape(1, -1)
    row_id = model[...].reshape(1, -1) * grid.shape[1] + (cell >> shift)
    col_id = cell & (cols - 1)
    PB = row_id.shape[1]
    packed = jnp.concatenate(
        [
            coords[...],
            row_id.astype(F32),
            col_id.astype(F32),
            valid[...].reshape(1, -1).astype(F32),
            jnp.zeros((128 - 9, PB), F32),
        ],
        0,
    )
    columns[...] = packed.T
    mine = columns[pl.ds(pl.multiple_of(t * Pn, 8), Pn), :]
    xs = [mine[:, j : j + 1] for j in range(6)]
    mask = mine[:, 8:9]
    row_of = mine[:, 6:7].astype(jnp.int32)
    col_of = mine[:, 7:8].astype(jnp.int32)
    table = grid[...].reshape(-1, cols)
    onehot = (
        lax.broadcasted_iota(jnp.int32, (Pn, table.shape[0]), 1) == row_of
    ).astype(BF16)
    high = table.astype(BF16)
    rest = table - high.astype(F32)
    middle = rest.astype(BF16)
    lowest = (rest - middle.astype(F32)).astype(BF16)
    picked = nn(onehot, high) + nn(onehot, middle) + nn(onehot, lowest)
    lane = lax.broadcasted_iota(jnp.int32, (Pn, cols), 1)
    truth = jnp.sum(jnp.where(lane == col_of, picked, 0.0), 1, keepdims=True)
    seps = [xs[3 + k] - xs[k] for k in range(3)]
    distance = jnp.sqrt(seps[0] * seps[0] + seps[1] * seps[1] + seps[2] * seps[2])
    units = [s / distance for s in seps]

    await_bytes(spbuf.at[pl.ds(0, n_t - 1)], s_recv.at[S_PAR])

    def small_row(i):
        return jnp.concatenate([spbuf[tt, i : i + 1, :] for tt in range(n_t)], 1)

    out_row = small_row(7 + 2 * LAYERS)
    last_low = master[LAYERS - 1, 1].astype(BF16).astype(F32)
    feature = lax.broadcasted_iota(jnp.int32, (R, D), 1) - lax.broadcasted_iota(jnp.int32, (R, D), 0)
    out_column = jnp.sum(jnp.where(feature == dp * R, out_row, 0.0), axis=1, keepdims=True)
    q_part = jnp.sum(last_low * out_column, axis=0, keepdims=True)
    qslot_z[a] = jnp.broadcast_to(q_part, (8, cw))
    for d in z_devices:
        remote(qslot_z.at[a], qslot_z.at[a], s_send.at[S_QFAR], s_recv.at[S_QFAR], d)

    first_rows = [small_row(j) for j in range(6)]
    z0 = small_row(6) + xs[0] * first_rows[0]
    for j in range(1, 6):
        z0 = z0 + xs[j] * first_rows[j]
    inner[...] = z0
    e0 = jnp.exp(jnp.minimum(z0, 0.0))
    slope0 = jnp.where(z0 > 0, 1.0, e0)
    streams[0] = jnp.where(z0 > 0, z0, e0 - 1.0)
    acts[0, 0] = streams[0].astype(BF16)
    for k in range(3):
        streams[1 + k] = slope0 * first_rows[3 + k]
        acts[0, 1 + k] = streams[1 + k].astype(BF16)

    def pass_on(m):
        for k in range(A - 1):
            first[m][k].wait_recv()
            w_near(m, piece(m, g, far[k]), k + 1)
        w_core(m, line(m, g), 0)

    def pass_on_turned():
        for k in range(G - 1):
            first[W_TURNED][k].wait_recv()
            w_far_turned(piece(W_TURNED, near[k], a), k + 1)
        w_core(W_TURNED, plane(W_TURNED, a), 0)

    pass_on(straight[0])
    me_near = g * 2 + c
    await_bytes(qslot_z.at[pl.ds(0, A - 1)], s_recv.at[S_QFAR])
    qslot_g[me_near] = slot_sum(qslot_z, A)
    for d in q_devices:
        remote(qslot_g.at[me_near], qslot_g.at[me_near], s_send.at[S_QNEAR], s_recv.at[S_QNEAR], d)
    if W_TURNED is not None:
        pass_on_turned()
    for m in straight[1:]:
        pass_on(m)

    def weight(m):
        return jnp.concatenate([wbuf[m, tt % 2, tt // 2].reshape(D, cw) for tt in range(n_t)], 1)

    M = 4 * Pn

    def block_in(l):
        pre[l] = nn(acts[l].reshape(M, D), weight(2 * l)).reshape(4, Pn, D)
        z = pre[l, 0] + small_row(7 + l)
        e = jnp.exp(jnp.minimum(z, 0.0))
        slope = jnp.where(z > 0, 1.0, e)
        hidden[l, 0] = jnp.where(z > 0, z, e - 1.0).astype(BF16)
        for k in range(1, 4):
            hidden[l, k] = (slope * pre[l, k]).astype(BF16)

    def block_out(l):
        branch = nt(hidden[l].reshape(M, D), weight(2 * l + 1)).reshape(4, Pn, D)
        for s in range(4):
            new = streams[s] + branch[s]
            if s == 0:
                new = new + small_row(7 + LAYERS + l)
            streams[s] = new
            if l + 1 < LAYERS:
                acts[l + 1, s] = new.astype(BF16)

    def fetch(m):
        if m == W_TURNED:
            for k in range(A - 1):
                await_bytes(plane(m, far[k]), wz_recv.at[m, k])
                w_core(m, plane(m, far[k]), k + 1)
        else:
            for k in range(G - 1):
                await_bytes(line(m, near[k]), wn_recv.at[m, k])
                w_core(m, line(m, near[k]), k + 1)

    def fetched(m):
        await_bytes(wbuf.at[m, c], wc_recv.at[m])

    for m in range(MOVED):
        fetch(m)
        fetched(m)
        if m == 0:
            for d in others:
                pl.semaphore_signal(barrier, inc=1, device_id=d, device_id_type=MESH)
        if m % 2 == 0:
            block_in(m // 2)
        else:
            block_out(m // 2)
        if m == MOVED - 2:
            proj_a = [jnp.sum(streams[s] * out_row, axis=1, keepdims=True) for s in range(4)]
            bias_row = small_row(6 + 2 * LAYERS)
            proj_a[0] = proj_a[0] + jnp.sum(bias_row * out_row, axis=1, keepdims=True)
            await_bytes(qslot_g.at[pl.ds(0, 2 * G - 1)], s_recv.at[S_QNEAR])
            q_row = []
            for tt in range(n_t):
                total = qslot_g[(tt // 2) * B * 2 + tt % 2, 0:1]
                for i in range(1, B):
                    total = total + qslot_g[((tt // 2) * B + i) * 2 + tt % 2, 0:1]
                q_row.append(total)
            q_row = jnp.concatenate(q_row, 1)

    last = LAYERS - 1
    proj = [
        proj_a[s] + jnp.sum(hidden[last, s].astype(F32) * q_row, axis=1, keepdims=True) for s in range(4)
    ]
    tau = proj[0]
    sign_tau = sign_of(tau)
    abs_tau = jnp.abs(tau)
    grad_time = [units[k] * abs_tau + distance * sign_tau * proj[1 + k] for k in range(3)]
    square = grad_time[0] * grad_time[0] + grad_time[1] * grad_time[1] + grad_time[2] * grad_time[2]
    error = square - truth * truth
    total_err = jnp.sum(mask * jnp.abs(error), axis=0, keepdims=True)
    count = jnp.sum(mask, axis=0, keepdims=True)
    seed = mask * sign_of(error)
    g_time = [2.0 * grad_time[k] * seed for k in range(3)]
    g_tau = sign_tau * (units[0] * g_time[0] + units[1] * g_time[1] + units[2] * g_time[2])
    g_proj = [g_tau] + [distance * sign_tau * g_time[k] for k in range(3)]
    v_row = jnp.sum(
        sum(hidden[last, s].astype(F32) * g_proj[s] for s in range(4)), axis=0, keepdims=True
    )
    for tt in range(n_t):
        vsend[tt % 2, tt // 2] = jnp.broadcast_to(v_row[:, tt * cw : (tt + 1) * cw], (8, cw))
    vslot_g[me_near] = vsend[c, y]
    for (o, cc), d in zip(q_coords, q_devices):
        remote(vsend.at[cc, o // B], vslot_g.at[me_near], s_send.at[S_VNEAR], s_recv.at[S_VNEAR], d)

    def v_far():
        await_bytes(vslot_g.at[pl.ds(0, 2 * G - 1)], s_recv.at[S_VNEAR])
        vslot_z[a] = slot_sum(vslot_g, 2 * G)
        for d in z_devices:
            remote(vslot_z.at[a], vslot_z.at[a], s_send.at[S_VFAR], s_recv.at[S_VFAR], d)

    pieces = [(far[k], k) for k in reversed(range(A - 1))] + [(a, None)]

    def start_core(m, value):
        low = value.astype(BF16)
        for tt in range(n_t):
            block = low[:, tt * cw : (tt + 1) * cw].reshape(A, B, R, cw)
            for i in range(B):
                gsend[m, tt % 2, :, (tt // 2) * B + i] = block[:, i]
        return [
            remote(
                gsend.at[m, 1 - c, z], gcore.at[m, z], g_send.at[WC], gc_recv.at[m, j], core_device
            )
            for j, (z, k) in enumerate(pieces)
        ]

    def core_sum(m, j):
        z = pieces[j][0]
        flying[m][j].wait_recv()
        gone[m, z] = (gsend[m, c, z].astype(F32) + gcore[m, z].astype(F32)).astype(BF16)

    def start_near(m):
        for j, (z, _) in enumerate(pieces):
            core_sum(m, j)
            for k, o in enumerate(near):
                remote(
                    gone.at[m, z, o], gslot_n.at[m, j, k], g_send.at[WN], gn_recv.at[m, j], g_devices[k]
                )

    def start_far(m):
        for j, (z, k) in enumerate(pieces):
            if G > 1:
                await_bytes(gslot_n.at[m, j], gn_recv.at[m, j])
            total = slot_sum(gslot_n.at[m, j], G - 1, gone[m, z, g].astype(F32))
            if k is None:
                gown[m] = total
            else:
                gtwo[m, k] = total.astype(BF16)
                remote(gtwo.at[m, k], gslot_z.at[m, k], g_send.at[WZ], gz_recv.at[m], z_devices[k])

    def finish(m):
        if m == G_TURNED:
            await_bytes(tslot_n, gn_recv.at[m, 0])
            return slot_sum(tslot_n, G - 1, gown[m])
        await_bytes(gslot_z.at[m], gz_recv.at[m])
        return slot_sum(gslot_z.at[m], A - 1, gown[m])

    def start_far_turned():
        m = G_TURNED
        for j, (z, k) in enumerate(pieces):
            core_sum(m, j)
            if k is not None:
                remote(gone.at[m, z], tslot_z.at[k], g_send.at[WP], gz_recv.at[m], z_devices[k])

    def start_near_turned():
        m = G_TURNED
        await_bytes(tslot_z, gz_recv.at[m])
        tback[...] = slot_sum(tslot_z, A - 1, gone[m, a].astype(F32))
        gown[m] = tback[g]
        tlow = gone.at[m, a]
        tlow[...] = tback[...].astype(BF16)
        for k, o in enumerate(near):
            remote(tlow.at[o], tslot_n.at[k], g_send.at[WT], gn_recv.at[m, 0], g_devices[k])

    flying = {}

    def start_first(m):
        if m == G_TURNED:
            start_far_turned()
        else:
            start_near(m)

    bias_in = [None] * LAYERS
    bias_out = [None] * LAYERS

    def back_last():
        z = pre[last, 0] + small_row(7 + last)
        e = jnp.exp(jnp.minimum(z, 0.0))
        slope = jnp.where(z > 0, 1.0, e)
        curve = jnp.where(z > 0, 0.0, e)
        mixed = g_proj[1] * pre[last, 1] + g_proj[2] * pre[last, 2] + g_proj[3] * pre[last, 3]
        gz = q_row * (g_proj[0] * slope + curve * mixed)
        bias_in[last] = jnp.sum(gz, axis=0, keepdims=True)
        gpre[0] = gz.astype(BF16)
        slope = slope * q_row
        for k in range(1, 4):
            gpre[k] = (g_proj[k] * slope).astype(BF16)

    def back_out(l):
        bias_out[l] = jnp.sum(grad[0], axis=0, keepdims=True)
        gb = gbranch[...].reshape(M, D)
        flying[2 * l + 1] = start_core(2 * l + 1, tn(gb, hidden[l].reshape(M, D)))

    def back_in(l):
        gb = gbranch[...].reshape(M, D)
        gh = nn(gb, weight(2 * l + 1)).reshape(4, Pn, D)
        z = pre[l, 0] + small_row(7 + l)
        e = jnp.exp(jnp.minimum(z, 0.0))
        slope = jnp.where(z > 0, 1.0, e)
        curve = jnp.where(z > 0, 0.0, e)
        gz = gh[0] * slope + curve * (gh[1] * pre[l, 1] + gh[2] * pre[l, 2] + gh[3] * pre[l, 3])
        bias_in[l] = jnp.sum(gz, axis=0, keepdims=True)
        gpre[0] = gz.astype(BF16)
        for k in range(1, 4):
            gpre[k] = (gh[k] * slope).astype(BF16)

    def back_weight(l):
        flying[2 * l] = start_core(2 * l, tn(acts[l].reshape(M, D), gpre[...].reshape(M, D)))

    def back_through(l):
        back = nt(gpre[...].reshape(M, D), weight(2 * l)).reshape(4, Pn, D)
        for s in range(4):
            value = (out_row * g_proj[s] if l == last else grad[s]) + back[s]
            grad[s] = value
            if l > 0:
                gbranch[s] = value.astype(BF16)

    back_last()
    back_weight(1)
    tau_sum = jnp.sum(g_proj[0], axis=0, keepdims=True)
    bias_out[last] = out_row * tau_sum
    g_out_row = bias_row * tau_sum + jnp.sum(
        streams[0] * g_proj[0] + streams[1] * g_proj[1] + streams[2] * g_proj[2] + streams[3] * g_proj[3],
        axis=0,
        keepdims=True,
    )
    back_through(1)
    back_out(0)
    start_first(2)
    back_in(0)
    back_weight(0)
    start_first(1)
    v_far()
    back_through(0)
    start_first(0)

    z0 = inner[...]
    e0 = jnp.exp(jnp.minimum(z0, 0.0))
    slope0 = jnp.where(z0 > 0, 1.0, e0)
    curve0 = jnp.where(z0 > 0, 0.0, e0)
    first_rows = [small_row(j) for j in range(6)]
    g_inner = grad[0] * slope0 + curve0 * (
        grad[1] * first_rows[3] + grad[2] * first_rows[4] + grad[3] * first_rows[5]
    )
    rows = [jnp.sum(xs[j] * g_inner, axis=0, keepdims=True) for j in range(6)]
    for k in range(3):
        rows[3 + k] = rows[3 + k] + jnp.sum(grad[1 + k] * slope0, axis=0, keepdims=True)
    rows.append(jnp.sum(g_inner, axis=0, keepdims=True))
    rows = rows + bias_in + bias_out + [g_out_row]

    lanes = lax.broadcasted_iota(jnp.int32, (1, cw), 1)
    weight_sq = jnp.zeros((1, cw), F32)
    for m in range(MATS):
        part = jnp.sum(master[m // 2, m % 2] * master[m // 2, m % 2], keepdims=True)
        weight_sq = jnp.where(lanes == m, part, weight_sq)
    own_small = spbuf[t]
    weight_sq = jnp.where(lanes == MATS, jnp.sum(own_small * own_small, keepdims=True) / (A * B), weight_sq)
    tail = [
        jnp.broadcast_to(total_err, (1, cw)),
        jnp.broadcast_to(count, (1, cw)),
        weight_sq,
        jnp.zeros((1, cw), F32),
    ]
    for tt in range(n_t):
        sgsend[tt % 2, tt // 2] = jnp.concatenate([r[:, tt * cw : (tt + 1) * cw] for r in rows] + tail, 0)
    sgslot_g[me_near] = sgsend[c, y]
    for (o, cc), d in zip(q_coords, q_devices):
        remote(sgsend.at[cc, o // B], sgslot_g.at[me_near], s_send.at[S_NEAR], s_recv.at[S_NEAR], d)

    await_bytes(vslot_z.at[fars], s_recv.at[S_VFAR])
    v_part = slot_sum(vslot_z, A)[0:1]
    product = jnp.sum(last_low * v_part, axis=1, keepdims=True)
    place = lax.broadcasted_iota(jnp.int32, (R, cw), 1) - lax.broadcasted_iota(jnp.int32, (R, cw), 0)
    product_row = jnp.sum(jnp.where(place == (dp * R) % cw, product, 0.0), axis=0, keepdims=True)
    psend[...] = jnp.broadcast_to(product_row, (8, cw))
    column = (dp * R) // cw
    mine_too = column == t
    slot = (dp % (cw // R)) * n_t + t
    pl.semaphore_wait(barrier, len(others))
    for k in range(1, A * B):
        remote(
            psend, pslot.at[slot], s_send.at[S_PROD], s_recv.at[S_PROD], (partner(dp, k, A * B), column)
        )

    @pl.when(mine_too)
    def _():
        pslot[slot] = psend[...]

    @pl.when(jnp.logical_not(mine_too))
    def _():
        remote(psend, pslot.at[slot], s_send.at[S_PROD], s_recv.at[S_PROD], (dp, column))

    def await_products(wait, ref, count_of, sems):
        @pl.when(mine_too)
        def _():
            wait(ref.at[pl.ds(0, count_of - 1)], sems.at[S_PROD])

        @pl.when(jnp.logical_not(mine_too))
        def _():
            wait(ref.at[pl.ds(0, count_of)], sems.at[S_PROD])

    if G_TURNED is None:
        start_far(2)
    start_far(1)
    if G_TURNED is not None:
        start_near_turned()
    start_far(0)
    await_bytes(sgslot_g.at[pl.ds(0, 2 * G - 1)], s_recv.at[S_NEAR])
    sgtwo[...] = slot_sum(sgslot_g, 2 * G)
    sgslot_z[a] = sgtwo[...]
    for d in z_devices:
        remote(sgtwo, sgslot_z.at[a], s_send.at[S_FAR], s_recv.at[S_FAR], d)

    for copy in local[7:]:
        copy.wait()
    grad_b[last, 1] = out_column * v_part
    for m in (1, 2, 0):
        grad_b[m // 2, m % 2] = finish(m)
    await_bytes(sgslot_z.at[pl.ds(0, A - 1)], s_recv.at[S_FAR])
    sred[...] = slot_sum(sgslot_z, A)
    slots = (cw // R) * n_t
    await_products(await_bytes, pslot, slots, s_recv)
    head_row = sred[SMALL - 1 : SMALL]
    for i in range(slots):
        head_row = head_row + pslot[i, 0:1]
    sred[SMALL - 1 : SMALL] = head_row
    counted = sred[SMALL + 1 : SMALL + 2, 0:1]
    tile_rows = lax.broadcasted_iota(jnp.int32, (8, 128), 0)
    parts = jnp.zeros((8, 128), F32)

    def step(gradient, momentum):
        new = momentum_coef * momentum + gradient
        return new, gradient + momentum_coef * new

    for m in range(MATS):
        at = (m // 2, m % 2)
        gr = grad_b[at] / counted
        new, direction = step(gr, moment[at])
        grad_b[at] = gr
        moment_b[at] = new
        parts = jnp.where(tile_rows == m, jnp.sum(direction * direction, keepdims=True), parts)
    gr = sred[0:SMALL, :] / counted
    new, dir_small = step(gr, msmall[...])
    grad_s[...] = gr
    moment_s[...] = new
    parts = jnp.where(
        tile_rows == MATS, jnp.sum(dir_small * dir_small, keepdims=True) / (A * B), parts
    )
    me = (a * G + g) * 2 + c
    arslot[me] = parts
    for d in everyone:
        remote(arslot.at[me], arslot.at[me], s_send.at[S_ALL], s_recv.at[S_ALL], d)
    loss_b[...] = sred[SMALL : SMALL + 1, 0:1] / counted
    bias_b[...] = grad_s[7 : 7 + 2 * LAYERS, :]
    await_bytes(arslot.at[pl.ds(0, len(everyone))], s_recv.at[S_ALL])
    dir_sq = jnp.sum(arslot[...], axis=0)

    def rate_of(m):
        size = sred[SMALL + 2 : SMALL + 3, m : m + 1]
        return spread_rate * jnp.sqrt(size) / jnp.sqrt(dir_sq[m : m + 1, 0:1] + norm_epsilon)

    for m in range(MATS):
        at = (m // 2, m % 2)
        direction = grad_b[at] + momentum_coef * moment_b[at]
        new = master[at] - rate_of(m) * direction
        master_b[at] = new
        average_b[at] = average_decay * average[at] + (1.0 - average_decay) * new
        low_b[at] = new.astype(BF16)
    new = own_small - rate_of(MATS) * dir_small
    master_s[...] = new
    average_s[...] = average_decay * asmall[...] + (1.0 - average_decay) * new

    for sems, turned in ((w_send, W_TURNED), (g_send, G_TURNED)):
        straights = pl.ds(0, MOVED if turned is None else MOVED - 1)
        await_sent(gone.at[straights, fars, 0], sems.at[WZ])
        await_sent(gone.at[straights, :, nears], sems.at[WN])
        if turned is not None:
            await_sent(gone.at[0, 0, nears], sems.at[WT])
            await_sent(gone.at[0, fars], sems.at[WP])
        await_sent(gone, sems.at[WC])
    await_sent(qslot_z.at[fars], s_send.at[S_QFAR])
    await_sent(vslot_z.at[fars], s_send.at[S_VFAR])
    await_sent(qslot_g.at[pl.ds(0, 2 * G - 1)], s_send.at[S_QNEAR])
    await_sent(vslot_g.at[pl.ds(0, 2 * G - 1)], s_send.at[S_VNEAR])
    await_sent(sgslot_g.at[pl.ds(0, 2 * G - 1)], s_send.at[S_NEAR])
    await_products(await_sent, pdone, A * B, s_send)
    await_sent(sgslot_z.at[fars], s_send.at[S_FAR])
    await_sent(arslot.at[pl.ds(0, len(everyone))], s_send.at[S_ALL])
    await_sent(spbuf.at[pl.ds(0, n_t - 1)], s_send.at[S_PAR])


def write_out(*refs):
    sems = refs[-1]
    count = (len(refs) - 1) // 2
    copies = [
        pltpu.make_async_copy(refs[i], refs[count + i], sems.at[i]) for i in range(count)
    ]
    for copy in copies:
        copy.start()
    for copy in copies:
        copy.wait()


def body(
    axes,
    coords,
    model_ids,
    cells,
    valid,
    slowness_grid,
    master_blocks,
    small_params,
    moment_blocks,
    moment_small,
    average_blocks,
    average_small,
):
    n_dp, n_t = axes
    A = 4 if n_dp % 4 == 0 else n_dp
    B = n_dp // A
    C = n_t // 2
    G = C * B
    R, cw = master_blocks.shape[2:]
    D = R * n_dp
    PB = coords.shape[1]
    Pn = PB // n_t
    dims = (A, B, C, R, cw, Pn, D)
    anywhere = pl.BlockSpec(memory_space=pltpu.HBM)
    vmem = pl.BlockSpec(memory_space=pltpu.VMEM)
    S = SMALL + 4
    args = (
        coords,
        model_ids,
        cells,
        valid,
        slowness_grid,
        master_blocks,
        small_params,
        moment_blocks,
        moment_small,
        average_blocks,
        average_small,
    )
    V = pltpu.VMEM
    DMA = pltpu.SemaphoreType.DMA
    block = (master_blocks.shape, F32)
    short = (small_params.shape, F32)
    shapes = [
        ((1, 1), F32),
        block,
        short,
        ((2 * LAYERS, cw), F32),
        block,
        short,
        block,
        short,
        block,
        short,
        (master_blocks.shape, BF16),
    ]
    results = pl.pallas_call(
        functools.partial(kernel, dims),
        out_shape=tuple(V(*shape) for shape in shapes),
        in_specs=[anywhere] * len(args),
        out_specs=(vmem,) * len(shapes),
        scratch_shapes=[
            V(coords.shape, F32),
            V((PB,), jnp.int32),
            V((PB,), jnp.int32),
            V((PB,), jnp.int32),
            V(slowness_grid.shape, F32),
            V(master_blocks.shape, F32),
            V(master_blocks.shape, F32),
            V(small_params.shape, F32),
            V(master_blocks.shape, F32),
            V(small_params.shape, F32),
            V((n_t, SMALL, cw), F32),
            V((PB, 128), F32),
            V((S, cw), F32),
            V((MOVED, 2, C, A, B, R, cw), BF16),
            V((4, Pn, D), F32),
            V((LAYERS, 4, Pn, D), BF16),
            V((LAYERS, 4, Pn, D), F32),
            V((LAYERS, 4, Pn, D), BF16),
            V((4, Pn, D), F32),
            V((4, Pn, D), BF16),
            V((4, Pn, D), BF16),
            V((Pn, D), F32),
            V((MOVED, 2, A, G, R, cw), BF16),
            V((MOVED, A, G, R, cw), BF16),
            V((MOVED, A, G, R, cw), BF16),
            V((MOVED, A, G - 1, R, cw), BF16),
            V((MOVED, A - 1, R, cw), BF16),
            V((MOVED, A - 1, R, cw), BF16),
            V((MOVED, R, cw), F32),
            V((A - 1, G, R, cw), BF16),
            V((G, R, cw), F32),
            V((G - 1, R, cw), BF16),
            V((2, C, S, cw), F32),
            V((8, cw), F32),
            V(((cw // R) * n_t, 8, cw), F32),
            V((n_dp, 8, cw), F32),
            V((2 * G, S, cw), F32),
            V((S, cw), F32),
            V((A, S, cw), F32),
            V((2 * A * G, 8, 128), F32),
            V((A, 8, cw), F32),
            V((2 * G, 8, cw), F32),
            V((2, C, 8, cw), F32),
            V((2 * G, 8, cw), F32),
            V((A, 8, cw), F32),
            pltpu.SemaphoreType.DMA((len(args),)),
            DMA((5,)),
            DMA((MOVED, A - 1)),
            DMA((MOVED, G - 1)),
            DMA((MOVED,)),
            DMA((5,)),
            DMA((MOVED,)),
            DMA((MOVED, A)),
            DMA((MOVED, A)),
            DMA((9,)),
            DMA((9,)),
        ],
        compiler_params=pltpu.CompilerParams(
            collective_id=0, has_side_effects=True, vmem_limit_bytes=60 << 20
        ),
    )(*args)

    results = pl.pallas_call(
        write_out,
        out_shape=tuple(jax.ShapeDtypeStruct(*shape) for shape in shapes),
        in_specs=[vmem] * len(shapes),
        out_specs=(anywhere,) * len(shapes),
        scratch_shapes=[pltpu.SemaphoreType.DMA((len(shapes),))],
        compiler_params=pltpu.CompilerParams(vmem_limit_bytes=4 << 20),
    )(*results)
    return (results[0].reshape(()),) + tuple(results[1:])


def solution(mesh):
    blocks = P(None, None, "dp", "tensor")
    small = P(None, "tensor")
    in_specs = (
        P(None, "dp"),
        P("dp"),
        P("dp"),
        P("dp"),
        P(),
        blocks,
        small,
        blocks,
        small,
        blocks,
        small,
    )
    out_specs = (P(), blocks, small, small, blocks, small, blocks, small, blocks, small, blocks)
    axes = (mesh.shape["dp"], mesh.shape["tensor"])
    return jax.shard_map(
        functools.partial(body, axes), mesh=mesh, in_specs=in_specs, out_specs=out_specs, check_vma=False
    )
```

```python
import functools

import jax
import jax.numpy as jnp
from jax import lax
from jax.experimental import pallas as pl
from jax.experimental.pallas import tpu as pltpu
from jax.sharding import PartitionSpec as P

LAYERS = 2
MATS = 2 * LAYERS
SMALL = 12
MESH = pl.DeviceIdType.MESH
F32 = jnp.float32
BF16 = jnp.bfloat16

momentum_coef = 0.5
average_decay = 0.5
spread_rate = 0.5
norm_epsilon = 1e-12

MOVED = MATS - 1
W_TURNED = (0, 1)
G_TURNED = (1, 0)


def partner(i, k, size):
    bit = 1
    while bit < size:
        if (k // bit) % 2:
            i = i + bit - 2 * bit * ((i // bit) % 2)
        bit *= 2
    return i


def nn(left, right):
    return lax.dot_general(left, right, (((1,), (0,)), ((), ())), preferred_element_type=F32)


def nt(left, right):
    return lax.dot_general(left, right, (((1,), (1,)), ((), ())), preferred_element_type=F32)


def tn(left, right):
    return lax.dot_general(left, right, (((0,), (0,)), ((), ())), preferred_element_type=F32)


def sign_of(v):
    return jnp.where(v > 0, 1.0, jnp.where(v < 0, -1.0, 0.0))


def kernel(
    dims,
    coords_hbm,
    model_hbm,
    cells_hbm,
    valid_hbm,
    grid_hbm,
    master_hbm,
    small_hbm,
    moment_hbm,
    msmall_hbm,
    average_hbm,
    asmall_hbm,
    loss_b,
    grad_b,
    grad_s,
    bias_b,
    moment_b,
    moment_s,
    master_b,
    master_s,
    average_b,
    average_s,
    low_b,
    coords,
    model,
    cells,
    valid,
    grid,
    master,
    moment,
    msmall,
    average,
    asmall,
    spbuf,
    columns,
    sred,
    wbuf,
    streams,
    acts,
    pre,
    hidden,
    grad,
    gbranch,
    gpre,
    inner,
    gsend,
    gcore,
    gone,
    gslot_n,
    gtwo,
    gslot_z,
    gown,
    tslot_z,
    tlow,
    tslot_n,
    sgsend,
    psend,
    pslot,
    pdone,
    sgslot_g,
    sgtwo,
    sgslot_z,
    arslot,
    qslot_z,
    qslot_g,
    vsend,
    vslot_g,
    vslot_z,
    in_sem,
    w_send,
    wz_recv,
    wn_recv,
    wt_recv,
    wc_recv,
    g_send,
    gz_recv,
    gn_recv,
    gt_recv,
    gc_recv,
    s_send,
    s_recv,
):
    A, B, C, R, cw, Pn, D = dims
    n_t = 2 * C
    G = C * B
    dp = lax.axis_index("dp")
    t = lax.axis_index("tensor")
    a, b = dp // B, dp % B
    y, c = t // 2, t % 2
    g = y * B + b

    def device(a_, g_, c_):
        return (a_ * B + g_ % B, (g_ // B) * 2 + c_)

    far = [partner(a, k, A) for k in range(1, A)]
    near = [partner(g, k, G) for k in range(1, G)]
    z_devices = [device(o, g, c) for o in far]
    g_devices = [device(a, o, c) for o in near]
    core_device = device(a, g, 1 - c)
    q_coords = [(partner(g, kg, G), partner(c, kc, 2)) for kg in range(G) for kc in range(2)][1:]
    q_devices = [device(a, o, cc) for o, cc in q_coords]
    steps = [(ka, kg, kc) for ka in range(A) for kg in range(G) for kc in range(2)][1:]
    steps.sort(key=lambda step: -(step[0] + bin(step[1]).count("1") + step[2] / 2))
    everyone = [device(partner(a, ka, A), partner(g, kg, G), partner(c, kc, 2)) for ka, kg, kc in steps]
    others = [d for d, step in zip(everyone, steps) if step[0] and (step[1] or step[2])]

    WZ, WO, WN, WX, WT, WP, WC = range(7)
    FARTHEST = G - 2
    w_turned = W_TURNED if G > 2 else ()
    g_turned = G_TURNED if G > 2 else ()

    def plain_near(m, turned):
        return range(G - 2 if m in turned else G - 1)

    S_PROD, S_NEAR, S_FAR, S_ALL, S_PAR, S_QFAR, S_QNEAR, S_VNEAR, S_VFAR = range(9)

    def remote(src, dst, ssem, rsem, device_id):
        copy = pltpu.make_async_remote_copy(
            src_ref=src,
            dst_ref=dst,
            send_sem=ssem,
            recv_sem=rsem,
            device_id=device_id,
            device_id_type=MESH,
        )
        copy.start()
        return copy

    def arrived(copies):
        for copy in copies:
            copy.wait_recv()

    nears, fars = pl.ds(0, G - 1), pl.ds(0, A - 1)

    local = []
    for i, (src, dst) in enumerate(
        [
            (master_hbm, master),
            (small_hbm, spbuf.at[t]),
            (coords_hbm, coords),
            (model_hbm, model),
            (cells_hbm, cells),
            (valid_hbm, valid),
            (grid_hbm, grid),
            (moment_hbm, moment),
            (msmall_hbm, msmall),
            (average_hbm, average),
            (asmall_hbm, asmall),
        ]
    ):
        copy = pltpu.make_async_copy(src, dst, in_sem.at[i])
        copy.start()
        local.append(copy)

    barrier = pltpu.get_barrier_semaphore()
    peers = z_devices + q_devices
    for d in peers:
        pl.semaphore_signal(barrier, inc=1, device_id=d, device_id_type=MESH)

    local[0].wait()
    for m in range(MOVED):
        wbuf[m, c, y, a, b] = master[m // 2, m % 2].astype(BF16)
    local[1].wait()
    pl.semaphore_wait(barrier, len(peers))

    def piece(m, o, z):
        return wbuf.at[m, c, o // B, z, o % B]

    def line(m, o):
        return wbuf.at[m, c, o // B, :, o % B]

    def plane(m, z):
        return wbuf.at[m, c, :, z]

    def await_bytes(ref, rsem):
        pltpu.make_async_remote_copy(
            src_ref=ref,
            dst_ref=ref,
            send_sem=s_send.at[0],
            recv_sem=rsem,
            device_id=core_device,
            device_id_type=MESH,
        ).wait_recv()

    def slot_sum(ref, count_of, value=None):
        for i in range(count_of):
            term = ref[i].astype(F32)
            value = term if value is None else value + term
        return value

    def await_sent(ref, ssem):
        pltpu.make_async_remote_copy(
            src_ref=ref,
            dst_ref=ref,
            send_sem=ssem,
            recv_sem=s_recv.at[0],
            device_id=core_device,
            device_id_type=MESH,
        ).wait_send()

    def w_far(m, ref):
        return [
            remote(ref, ref, w_send.at[WZ], wz_recv.at[m, k], d) for k, d in enumerate(z_devices)
        ]

    def w_near(m, ref, ks, ssem):
        for k in ks:
            remote(ref, ref, w_send.at[ssem], wn_recv.at[m, k], g_devices[k])

    def w_core(m, ref):
        remote(ref, ref, w_send.at[WC], wc_recv.at[m], core_device)

    for k in range(1, n_t):
        o = (t + k) % n_t
        remote(spbuf.at[t], spbuf.at[t], s_send.at[S_PAR], s_recv.at[S_PAR], (dp, o))
    first = {}
    for m in range(MOVED):
        first[m] = w_far(m, piece(m, g, a))
        w_near(m, piece(m, g, a), reversed(range(G - 1)), WO)

    for copy in local[2:7]:
        copy.wait()
    cols = grid.shape[2]
    shift = (cols - 1).bit_length()
    cell = cells[...].reshape(1, -1)
    row_id = model[...].reshape(1, -1) * grid.shape[1] + (cell >> shift)
    col_id = cell & (cols - 1)
    PB = row_id.shape[1]
    packed = jnp.concatenate(
        [
            coords[...],
            row_id.astype(F32),
            col_id.astype(F32),
            valid[...].reshape(1, -1).astype(F32),
            jnp.zeros((128 - 9, PB), F32),
        ],
        0,
    )
    columns[...] = packed.T
    mine = columns[pl.ds(pl.multiple_of(t * Pn, 8), Pn), :]
    xs = [mine[:, j : j + 1] for j in range(6)]
    mask = mine[:, 8:9]
    row_of = mine[:, 6:7].astype(jnp.int32)
    col_of = mine[:, 7:8].astype(jnp.int32)
    table = grid[...].reshape(-1, cols)
    onehot = (
        lax.broadcasted_iota(jnp.int32, (Pn, table.shape[0]), 1) == row_of
    ).astype(BF16)
    high = table.astype(BF16)
    rest = table - high.astype(F32)
    middle = rest.astype(BF16)
    lowest = (rest - middle.astype(F32)).astype(BF16)
    picked = nn(onehot, high) + nn(onehot, middle) + nn(onehot, lowest)
    lane = lax.broadcasted_iota(jnp.int32, (Pn, cols), 1)
    truth = jnp.sum(jnp.where(lane == col_of, picked, 0.0), 1, keepdims=True)
    seps = [xs[3 + k] - xs[k] for k in range(3)]
    distance = jnp.sqrt(seps[0] * seps[0] + seps[1] * seps[1] + seps[2] * seps[2])
    units = [s / distance for s in seps]

    await_bytes(spbuf.at[pl.ds(0, n_t - 1)], s_recv.at[S_PAR])

    def small_row(i):
        return jnp.concatenate([spbuf[tt, i : i + 1, :] for tt in range(n_t)], 1)

    out_row = small_row(7 + 2 * LAYERS)
    last_low = master[LAYERS - 1, 1].astype(BF16).astype(F32)
    feature = lax.broadcasted_iota(jnp.int32, (R, D), 1) - lax.broadcasted_iota(jnp.int32, (R, D), 0)
    out_column = jnp.sum(jnp.where(feature == dp * R, out_row, 0.0), axis=1, keepdims=True)
    q_part = jnp.sum(last_low * out_column, axis=0, keepdims=True)
    qslot_z[a] = jnp.broadcast_to(q_part, (8, cw))
    for d in z_devices:
        remote(qslot_z.at[a], qslot_z.at[a], s_send.at[S_QFAR], s_recv.at[S_QFAR], d)

    first_rows = [small_row(j) for j in range(6)]
    z0 = small_row(6) + xs[0] * first_rows[0]
    for j in range(1, 6):
        z0 = z0 + xs[j] * first_rows[j]
    inner[...] = z0
    e0 = jnp.exp(jnp.minimum(z0, 0.0))
    slope0 = jnp.where(z0 > 0, 1.0, e0)
    streams[0] = jnp.where(z0 > 0, z0, e0 - 1.0)
    acts[0, 0] = streams[0].astype(BF16)
    for k in range(3):
        streams[1 + k] = slope0 * first_rows[3 + k]
        acts[0, 1 + k] = streams[1 + k].astype(BF16)

    def pass_on(m):
        for k in range(A - 1):
            first[m][k].wait_recv()
            w_near(m, piece(m, g, far[k]), plain_near(m, w_turned), WX if m in w_turned else WN)
        w_core(m, line(m, g))
        if m in w_turned:
            o = near[FARTHEST]
            ref = piece(m, o, a)
            await_bytes(ref, wn_recv.at[m, FARTHEST])
            for d in z_devices:
                remote(ref, ref, w_send.at[WT], wt_recv.at[m], d)

    pass_on(0)
    me_near = g * 2 + c
    await_bytes(qslot_z.at[fars], s_recv.at[S_QFAR])
    qslot_g[me_near] = slot_sum(qslot_z, A)
    for d in q_devices:
        remote(qslot_g.at[me_near], qslot_g.at[me_near], s_send.at[S_QNEAR], s_recv.at[S_QNEAR], d)
    for m in range(1, MOVED):
        pass_on(m)

    def weight(m):
        return jnp.concatenate([wbuf[m, tt % 2, tt // 2].reshape(D, cw) for tt in range(n_t)], 1)

    M = 4 * Pn

    def block_in(l):
        pre[l] = nn(acts[l].reshape(M, D), weight(2 * l)).reshape(4, Pn, D)
        z = pre[l, 0] + small_row(7 + l)
        e = jnp.exp(jnp.minimum(z, 0.0))
        slope = jnp.where(z > 0, 1.0, e)
        hidden[l, 0] = jnp.where(z > 0, z, e - 1.0).astype(BF16)
        for k in range(1, 4):
            hidden[l, k] = (slope * pre[l, k]).astype(BF16)

    def block_out(l):
        branch = nt(hidden[l].reshape(M, D), weight(2 * l + 1)).reshape(4, Pn, D)
        for s in range(4):
            new = streams[s] + branch[s]
            if s == 0:
                new = new + small_row(7 + LAYERS + l)
            streams[s] = new
            if l + 1 < LAYERS:
                acts[l + 1, s] = new.astype(BF16)

    def fetch(m):
        for k in range(G - 1):
            if m in w_turned and k == FARTHEST:
                await_bytes(wbuf.at[m, c, 0, fars, 0], wt_recv.at[m])
            else:
                await_bytes(line(m, near[k]), wn_recv.at[m, k])
            w_core(m, line(m, near[k]))

    def fetched(m):
        await_bytes(wbuf.at[m, c], wc_recv.at[m])

    for m in range(MOVED):
        fetch(m)
        fetched(m)
        if m == 0:
            for d in others:
                pl.semaphore_signal(barrier, inc=1, device_id=d, device_id_type=MESH)
        if m % 2 == 0:
            block_in(m // 2)
        else:
            block_out(m // 2)
        if m == MOVED - 2:
            proj_a = [jnp.sum(streams[s] * out_row, axis=1, keepdims=True) for s in range(4)]
            bias_row = small_row(6 + 2 * LAYERS)
            proj_a[0] = proj_a[0] + jnp.sum(bias_row * out_row, axis=1, keepdims=True)
            await_bytes(qslot_g.at[pl.ds(0, 2 * G - 1)], s_recv.at[S_QNEAR])
            q_row = []
            for tt in range(n_t):
                total = qslot_g[(tt // 2) * B * 2 + tt % 2, 0:1]
                for i in range(1, B):
                    total = total + qslot_g[((tt // 2) * B + i) * 2 + tt % 2, 0:1]
                q_row.append(total)
            q_row = jnp.concatenate(q_row, 1)

    last = LAYERS - 1
    proj = [
        proj_a[s] + jnp.sum(hidden[last, s].astype(F32) * q_row, axis=1, keepdims=True) for s in range(4)
    ]
    tau = proj[0]
    sign_tau = sign_of(tau)
    abs_tau = jnp.abs(tau)
    grad_time = [units[k] * abs_tau + distance * sign_tau * proj[1 + k] for k in range(3)]
    square = grad_time[0] * grad_time[0] + grad_time[1] * grad_time[1] + grad_time[2] * grad_time[2]
    error = square - truth * truth
    total_err = jnp.sum(mask * jnp.abs(error), axis=0, keepdims=True)
    count = jnp.sum(mask, axis=0, keepdims=True)
    seed = mask * sign_of(error)
    g_time = [2.0 * grad_time[k] * seed for k in range(3)]
    g_tau = sign_tau * (units[0] * g_time[0] + units[1] * g_time[1] + units[2] * g_time[2])
    g_proj = [g_tau] + [distance * sign_tau * g_time[k] for k in range(3)]
    v_row = jnp.sum(
        sum(hidden[last, s].astype(F32) * g_proj[s] for s in range(4)), axis=0, keepdims=True
    )
    for tt in range(n_t):
        vsend[tt % 2, tt // 2] = jnp.broadcast_to(v_row[:, tt * cw : (tt + 1) * cw], (8, cw))
    vslot_g[me_near] = vsend[c, y]
    for (o, cc), d in zip(q_coords, q_devices):
        remote(vsend.at[cc, o // B], vslot_g.at[me_near], s_send.at[S_VNEAR], s_recv.at[S_VNEAR], d)

    def v_far():
        await_bytes(vslot_g.at[pl.ds(0, 2 * G - 1)], s_recv.at[S_VNEAR])
        vslot_z[a] = slot_sum(vslot_g, 2 * G)
        for d in z_devices:
            remote(vslot_z.at[a], vslot_z.at[a], s_send.at[S_VFAR], s_recv.at[S_VFAR], d)

    pieces = [(far[k], k) for k in reversed(range(A - 1))] + [(a, None)]

    def start_core(m, value):
        low = value.astype(BF16)
        for tt in range(n_t):
            block = low[:, tt * cw : (tt + 1) * cw].reshape(A, B, R, cw)
            for i in range(B):
                gsend[m, tt % 2, :, (tt // 2) * B + i] = block[:, i]
        return [
            remote(
                gsend.at[m, 1 - c, z], gcore.at[m, z], g_send.at[WC], gc_recv.at[m, j], core_device
            )
            for j, (z, k) in enumerate(pieces)
        ]

    def core_sum(m, j):
        z = pieces[j][0]
        flying[m][j].wait_recv()
        gone[m, z] = (gsend[m, c, z].astype(F32) + gcore[m, z].astype(F32)).astype(BF16)

    def start_near(m):
        for j, (z, kz) in enumerate(pieces):
            core_sum(m, j)
            for k in plain_near(m, g_turned):
                remote(
                    gone.at[m, z, near[k]],
                    gslot_n.at[m, j, k],
                    g_send.at[WX if m in g_turned else WN],
                    gn_recv.at[m, j],
                    g_devices[k],
                )
            if m in g_turned and kz is not None:
                remote(
                    gone.at[m, z, near[FARTHEST]],
                    tslot_z.at[m, kz],
                    g_send.at[WT],
                    gt_recv.at[m, 0],
                    z_devices[kz],
                )

    def start_far(m):
        count_of = len(plain_near(m, g_turned))
        for j, (z, k) in enumerate(pieces):
            if count_of:
                await_bytes(gslot_n.at[m, j, pl.ds(0, count_of)], gn_recv.at[m, j])
            total = slot_sum(gslot_n.at[m, j], count_of, gone[m, z, g].astype(F32))
            if k is None:
                gown[m] = total
            else:
                gtwo[m, k] = total.astype(BF16)
                remote(gtwo.at[m, k], gslot_z.at[m, k], g_send.at[WZ], gz_recv.at[m], z_devices[k])

    def start_turned(m):
        if m in g_turned:
            await_bytes(tslot_z.at[m], gt_recv.at[m, 0])
            total = slot_sum(tslot_z.at[m], A - 1, gone[m, a, near[FARTHEST]].astype(F32))
            tlow[m] = total.astype(BF16)
            remote(tlow.at[m], tslot_n.at[m], g_send.at[WP], gt_recv.at[m, 1], g_devices[FARTHEST])

    def finish(m):
        await_bytes(gslot_z.at[m], gz_recv.at[m])
        total = slot_sum(gslot_z.at[m], A - 1, gown[m])
        if m in g_turned:
            await_bytes(tslot_n.at[m], gt_recv.at[m, 1])
            total = total + tslot_n[m].astype(F32)
        return total

    flying = {}

    bias_in = [None] * LAYERS
    bias_out = [None] * LAYERS

    def back_last():
        z = pre[last, 0] + small_row(7 + last)
        e = jnp.exp(jnp.minimum(z, 0.0))
        slope = jnp.where(z > 0, 1.0, e)
        curve = jnp.where(z > 0, 0.0, e)
        mixed = g_proj[1] * pre[last, 1] + g_proj[2] * pre[last, 2] + g_proj[3] * pre[last, 3]
        gz = q_row * (g_proj[0] * slope + curve * mixed)
        bias_in[last] = jnp.sum(gz, axis=0, keepdims=True)
        gpre[0] = gz.astype(BF16)
        slope = slope * q_row
        for k in range(1, 4):
            gpre[k] = (g_proj[k] * slope).astype(BF16)

    def back_out(l):
        bias_out[l] = jnp.sum(grad[0], axis=0, keepdims=True)
        gb = gbranch[...].reshape(M, D)
        flying[2 * l + 1] = start_core(2 * l + 1, tn(gb, hidden[l].reshape(M, D)))

    def back_in(l):
        gb = gbranch[...].reshape(M, D)
        gh = nn(gb, weight(2 * l + 1)).reshape(4, Pn, D)
        z = pre[l, 0] + small_row(7 + l)
        e = jnp.exp(jnp.minimum(z, 0.0))
        slope = jnp.where(z > 0, 1.0, e)
        curve = jnp.where(z > 0, 0.0, e)
        gz = gh[0] * slope + curve * (gh[1] * pre[l, 1] + gh[2] * pre[l, 2] + gh[3] * pre[l, 3])
        bias_in[l] = jnp.sum(gz, axis=0, keepdims=True)
        gpre[0] = gz.astype(BF16)
        for k in range(1, 4):
            gpre[k] = (gh[k] * slope).astype(BF16)

    def back_weight(l):
        flying[2 * l] = start_core(2 * l, tn(acts[l].reshape(M, D), gpre[...].reshape(M, D)))

    def back_through(l):
        back = nt(gpre[...].reshape(M, D), weight(2 * l)).reshape(4, Pn, D)
        for s in range(4):
            value = (out_row * g_proj[s] if l == last else grad[s]) + back[s]
            grad[s] = value
            if l > 0:
                gbranch[s] = value.astype(BF16)

    back_last()
    back_weight(1)
    tau_sum = jnp.sum(g_proj[0], axis=0, keepdims=True)
    bias_out[last] = out_row * tau_sum
    g_out_row = bias_row * tau_sum + jnp.sum(
        streams[0] * g_proj[0] + streams[1] * g_proj[1] + streams[2] * g_proj[2] + streams[3] * g_proj[3],
        axis=0,
        keepdims=True,
    )
    back_through(1)
    back_out(0)
    start_near(2)
    back_in(0)
    back_weight(0)
    start_near(1)
    v_far()
    back_through(0)
    start_near(0)

    z0 = inner[...]
    e0 = jnp.exp(jnp.minimum(z0, 0.0))
    slope0 = jnp.where(z0 > 0, 1.0, e0)
    curve0 = jnp.where(z0 > 0, 0.0, e0)
    first_rows = [small_row(j) for j in range(6)]
    g_inner = grad[0] * slope0 + curve0 * (
        grad[1] * first_rows[3] + grad[2] * first_rows[4] + grad[3] * first_rows[5]
    )
    rows = [jnp.sum(xs[j] * g_inner, axis=0, keepdims=True) for j in range(6)]
    for k in range(3):
        rows[3 + k] = rows[3 + k] + jnp.sum(grad[1 + k] * slope0, axis=0, keepdims=True)
    rows.append(jnp.sum(g_inner, axis=0, keepdims=True))
    rows = rows + bias_in + bias_out + [g_out_row]

    lanes = lax.broadcasted_iota(jnp.int32, (1, cw), 1)
    weight_sq = jnp.zeros((1, cw), F32)
    for m in range(MATS):
        part = jnp.sum(master[m // 2, m % 2] * master[m // 2, m % 2], keepdims=True)
        weight_sq = jnp.where(lanes == m, part, weight_sq)
    own_small = spbuf[t]
    weight_sq = jnp.where(lanes == MATS, jnp.sum(own_small * own_small, keepdims=True) / (A * B), weight_sq)
    tail = [
        jnp.broadcast_to(total_err, (1, cw)),
        jnp.broadcast_to(count, (1, cw)),
        weight_sq,
        jnp.zeros((1, cw), F32),
    ]
    for tt in range(n_t):
        sgsend[tt % 2, tt // 2] = jnp.concatenate([r[:, tt * cw : (tt + 1) * cw] for r in rows] + tail, 0)
    sgslot_g[me_near] = sgsend[c, y]
    for (o, cc), d in zip(q_coords, q_devices):
        remote(sgsend.at[cc, o // B], sgslot_g.at[me_near], s_send.at[S_NEAR], s_recv.at[S_NEAR], d)

    await_bytes(vslot_z.at[fars], s_recv.at[S_VFAR])
    v_part = slot_sum(vslot_z, A)[0:1]
    product = jnp.sum(last_low * v_part, axis=1, keepdims=True)
    place = lax.broadcasted_iota(jnp.int32, (R, cw), 1) - lax.broadcasted_iota(jnp.int32, (R, cw), 0)
    product_row = jnp.sum(jnp.where(place == (dp * R) % cw, product, 0.0), axis=0, keepdims=True)
    psend[...] = jnp.broadcast_to(product_row, (8, cw))
    column = (dp * R) // cw
    mine_too = column == t
    slot = (dp % (cw // R)) * n_t + t
    pl.semaphore_wait(barrier, len(others))
    for k in range(1, A * B):
        remote(
            psend, pslot.at[slot], s_send.at[S_PROD], s_recv.at[S_PROD], (partner(dp, k, A * B), column)
        )

    @pl.when(mine_too)
    def _():
        pslot[slot] = psend[...]

    @pl.when(jnp.logical_not(mine_too))
    def _():
        remote(psend, pslot.at[slot], s_send.at[S_PROD], s_recv.at[S_PROD], (dp, column))

    def await_products(wait, ref, count_of, sems):
        @pl.when(mine_too)
        def _():
            wait(ref.at[pl.ds(0, count_of - 1)], sems.at[S_PROD])

        @pl.when(jnp.logical_not(mine_too))
        def _():
            wait(ref.at[pl.ds(0, count_of)], sems.at[S_PROD])

    start_far(2)
    start_turned(2)
    start_far(1)
    start_turned(1)
    start_far(0)
    start_turned(0)
    await_bytes(sgslot_g.at[pl.ds(0, 2 * G - 1)], s_recv.at[S_NEAR])
    sgtwo[...] = slot_sum(sgslot_g, 2 * G)
    sgslot_z[a] = sgtwo[...]
    for d in z_devices:
        remote(sgtwo, sgslot_z.at[a], s_send.at[S_FAR], s_recv.at[S_FAR], d)

    for copy in local[7:]:
        copy.wait()
    grad_b[last, 1] = out_column * v_part
    for m in (1, 2, 0):
        grad_b[m // 2, m % 2] = finish(m)
    await_bytes(sgslot_z.at[pl.ds(0, A - 1)], s_recv.at[S_FAR])
    sred[...] = slot_sum(sgslot_z, A)
    slots = (cw // R) * n_t
    await_products(await_bytes, pslot, slots, s_recv)
    head_row = sred[SMALL - 1 : SMALL]
    for i in range(slots):
        head_row = head_row + pslot[i, 0:1]
    sred[SMALL - 1 : SMALL] = head_row
    counted = sred[SMALL + 1 : SMALL + 2, 0:1]
    tile_rows = lax.broadcasted_iota(jnp.int32, (8, 128), 0)
    parts = jnp.zeros((8, 128), F32)

    def step(gradient, momentum):
        new = momentum_coef * momentum + gradient
        return new, gradient + momentum_coef * new

    for m in range(MATS):
        at = (m // 2, m % 2)
        gr = grad_b[at] / counted
        new, direction = step(gr, moment[at])
        grad_b[at] = gr
        moment_b[at] = new
        parts = jnp.where(tile_rows == m, jnp.sum(direction * direction, keepdims=True), parts)
    gr = sred[0:SMALL, :] / counted
    new, dir_small = step(gr, msmall[...])
    grad_s[...] = gr
    moment_s[...] = new
    parts = jnp.where(
        tile_rows == MATS, jnp.sum(dir_small * dir_small, keepdims=True) / (A * B), parts
    )
    me = (a * G + g) * 2 + c
    arslot[me] = parts
    for d in everyone:
        remote(arslot.at[me], arslot.at[me], s_send.at[S_ALL], s_recv.at[S_ALL], d)
    loss_b[...] = sred[SMALL : SMALL + 1, 0:1] / counted
    bias_b[...] = grad_s[7 : 7 + 2 * LAYERS, :]
    await_bytes(arslot.at[pl.ds(0, len(everyone))], s_recv.at[S_ALL])
    dir_sq = jnp.sum(arslot[...], axis=0)

    def rate_of(m):
        size = sred[SMALL + 2 : SMALL + 3, m : m + 1]
        return spread_rate * jnp.sqrt(size) / jnp.sqrt(dir_sq[m : m + 1, 0:1] + norm_epsilon)

    for m in range(MATS):
        at = (m // 2, m % 2)
        direction = grad_b[at] + momentum_coef * moment_b[at]
        new = master[at] - rate_of(m) * direction
        master_b[at] = new
        average_b[at] = average_decay * average[at] + (1.0 - average_decay) * new
        low_b[at] = new.astype(BF16)
    new = own_small - rate_of(MATS) * dir_small
    master_s[...] = new
    average_s[...] = average_decay * asmall[...] + (1.0 - average_decay) * new

    for sems, turned, passed in ((w_send, w_turned, A - 1), (g_send, g_turned, A)):
        few, many = pl.ds(0, len(turned)), pl.ds(0, MOVED - len(turned))
        all_passed = pl.ds(0, passed)
        await_sent(gone.at[:, fars, 0], sems.at[WZ])
        if len(turned) < MOVED:
            await_sent(gone.at[many, all_passed, nears], sems.at[WN])
        if turned:
            await_sent(gone.at[few, all_passed, pl.ds(0, G - 2)], sems.at[WX])
            await_sent(gone.at[few, fars, 0], sems.at[WT])
        await_sent(gone, sems.at[WC])
    await_sent(gone.at[:, 0, nears], w_send.at[WO])
    if g_turned:
        await_sent(gone.at[pl.ds(0, len(g_turned)), 0, 0], g_send.at[WP])
    await_sent(qslot_z.at[fars], s_send.at[S_QFAR])
    await_sent(vslot_z.at[fars], s_send.at[S_VFAR])
    await_sent(qslot_g.at[pl.ds(0, 2 * G - 1)], s_send.at[S_QNEAR])
    await_sent(vslot_g.at[pl.ds(0, 2 * G - 1)], s_send.at[S_VNEAR])
    await_sent(sgslot_g.at[pl.ds(0, 2 * G - 1)], s_send.at[S_NEAR])
    await_products(await_sent, pdone, A * B, s_send)
    await_sent(sgslot_z.at[fars], s_send.at[S_FAR])
    await_sent(arslot.at[pl.ds(0, len(everyone))], s_send.at[S_ALL])
    await_sent(spbuf.at[pl.ds(0, n_t - 1)], s_send.at[S_PAR])


def write_out(*refs):
    sems = refs[-1]
    count = (len(refs) - 1) // 2
    copies = [
        pltpu.make_async_copy(refs[i], refs[count + i], sems.at[i]) for i in range(count)
    ]
    for copy in copies:
        copy.start()
    for copy in copies:
        copy.wait()


def body(
    axes,
    coords,
    model_ids,
    cells,
    valid,
    slowness_grid,
    master_blocks,
    small_params,
    moment_blocks,
    moment_small,
    average_blocks,
    average_small,
):
    n_dp, n_t = axes
    A = 4 if n_dp % 4 == 0 else n_dp
    B = n_dp // A
    C = n_t // 2
    G = C * B
    R, cw = master_blocks.shape[2:]
    D = R * n_dp
    PB = coords.shape[1]
    Pn = PB // n_t
    dims = (A, B, C, R, cw, Pn, D)
    anywhere = pl.BlockSpec(memory_space=pltpu.HBM)
    vmem = pl.BlockSpec(memory_space=pltpu.VMEM)
    S = SMALL + 4
    args = (
        coords,
        model_ids,
        cells,
        valid,
        slowness_grid,
        master_blocks,
        small_params,
        moment_blocks,
        moment_small,
        average_blocks,
        average_small,
    )
    V = pltpu.VMEM
    DMA = pltpu.SemaphoreType.DMA
    block = (master_blocks.shape, F32)
    short = (small_params.shape, F32)
    shapes = [
        ((1, 1), F32),
        block,
        short,
        ((2 * LAYERS, cw), F32),
        block,
        short,
        block,
        short,
        block,
        short,
        (master_blocks.shape, BF16),
    ]
    results = pl.pallas_call(
        functools.partial(kernel, dims),
        out_shape=tuple(V(*shape) for shape in shapes),
        in_specs=[anywhere] * len(args),
        out_specs=(vmem,) * len(shapes),
        scratch_shapes=[
            V(coords.shape, F32),
            V((PB,), jnp.int32),
            V((PB,), jnp.int32),
            V((PB,), jnp.int32),
            V(slowness_grid.shape, F32),
            V(master_blocks.shape, F32),
            V(master_blocks.shape, F32),
            V(small_params.shape, F32),
            V(master_blocks.shape, F32),
            V(small_params.shape, F32),
            V((n_t, SMALL, cw), F32),
            V((PB, 128), F32),
            V((S, cw), F32),
            V((MOVED, 2, C, A, B, R, cw), BF16),
            V((4, Pn, D), F32),
            V((LAYERS, 4, Pn, D), BF16),
            V((LAYERS, 4, Pn, D), F32),
            V((LAYERS, 4, Pn, D), BF16),
            V((4, Pn, D), F32),
            V((4, Pn, D), BF16),
            V((4, Pn, D), BF16),
            V((Pn, D), F32),
            V((MOVED, 2, A, G, R, cw), BF16),
            V((MOVED, A, G, R, cw), BF16),
            V((MOVED, A, G, R, cw), BF16),
            V((MOVED, A, G - 1, R, cw), BF16),
            V((MOVED, A - 1, R, cw), BF16),
            V((MOVED, A - 1, R, cw), BF16),
            V((MOVED, R, cw), F32),
            V((MOVED, A - 1, R, cw), BF16),
            V((MOVED, R, cw), BF16),
            V((MOVED, R, cw), BF16),
            V((2, C, S, cw), F32),
            V((8, cw), F32),
            V(((cw // R) * n_t, 8, cw), F32),
            V((n_dp, 8, cw), F32),
            V((2 * G, S, cw), F32),
            V((S, cw), F32),
            V((A, S, cw), F32),
            V((2 * A * G, 8, 128), F32),
            V((A, 8, cw), F32),
            V((2 * G, 8, cw), F32),
            V((2, C, 8, cw), F32),
            V((2 * G, 8, cw), F32),
            V((A, 8, cw), F32),
            pltpu.SemaphoreType.DMA((len(args),)),
            DMA((7,)),
            DMA((MOVED, A - 1)),
            DMA((MOVED, G - 1)),
            DMA((MOVED,)),
            DMA((MOVED,)),
            DMA((7,)),
            DMA((MOVED,)),
            DMA((MOVED, A)),
            DMA((MOVED, 2)),
            DMA((MOVED, A)),
            DMA((9,)),
            DMA((9,)),
        ],
        compiler_params=pltpu.CompilerParams(
            collective_id=0, has_side_effects=True, vmem_limit_bytes=60 << 20
        ),
    )(*args)

    results = pl.pallas_call(
        write_out,
        out_shape=tuple(jax.ShapeDtypeStruct(*shape) for shape in shapes),
        in_specs=[vmem] * len(shapes),
        out_specs=(anywhere,) * len(shapes),
        scratch_shapes=[pltpu.SemaphoreType.DMA((len(shapes),))],
        compiler_params=pltpu.CompilerParams(vmem_limit_bytes=4 << 20),
    )(*results)
    return (results[0].reshape(()),) + tuple(results[1:])


def solution(mesh):
    blocks = P(None, None, "dp", "tensor")
    small = P(None, "tensor")
    in_specs = (
        P(None, "dp"),
        P("dp"),
        P("dp"),
        P("dp"),
        P(),
        blocks,
        small,
        blocks,
        small,
        blocks,
        small,
    )
    out_specs = (P(), blocks, small, small, blocks, small, blocks, small, blocks, small, blocks)
    axes = (mesh.shape["dp"], mesh.shape["tensor"])
    return jax.shard_map(
        functools.partial(body, axes), mesh=mesh, in_specs=in_specs, out_specs=out_specs, check_vma=False
    )
```

```python
import functools

import jax
import jax.numpy as jnp
from jax import lax
from jax.experimental import pallas as pl
from jax.experimental.pallas import tpu as pltpu
from jax.sharding import PartitionSpec as P

LAYERS = 2
MATS = 2 * LAYERS
SMALL = 12
MESH = pl.DeviceIdType.MESH
F32 = jnp.float32
BF16 = jnp.bfloat16

momentum_coef = 0.5
average_decay = 0.5
spread_rate = 0.5
norm_epsilon = 1e-12

MOVED = MATS - 1
W_TURNED = (0, 1)
G_TURNED = (2, 1, 0)


def partner(i, k, size):
    bit = 1
    while bit < size:
        if (k // bit) % 2:
            i = i + bit - 2 * bit * ((i // bit) % 2)
        bit *= 2
    return i


def nn(left, right):
    return lax.dot_general(left, right, (((1,), (0,)), ((), ())), preferred_element_type=F32)


def nt(left, right):
    return lax.dot_general(left, right, (((1,), (1,)), ((), ())), preferred_element_type=F32)


def tn(left, right):
    return lax.dot_general(left, right, (((0,), (0,)), ((), ())), preferred_element_type=F32)


def sign_of(v):
    return jnp.where(v > 0, 1.0, jnp.where(v < 0, -1.0, 0.0))


def kernel(
    dims,
    coords_hbm,
    model_hbm,
    cells_hbm,
    valid_hbm,
    grid_hbm,
    master_hbm,
    small_hbm,
    moment_hbm,
    msmall_hbm,
    average_hbm,
    asmall_hbm,
    loss_b,
    grad_b,
    grad_s,
    bias_b,
    moment_b,
    moment_s,
    master_b,
    master_s,
    average_b,
    average_s,
    low_b,
    coords,
    model,
    cells,
    valid,
    grid,
    master,
    moment,
    msmall,
    average,
    asmall,
    spbuf,
    columns,
    sred,
    wbuf,
    streams,
    acts,
    pre,
    hidden,
    grad,
    gbranch,
    gpre,
    inner,
    gsend,
    gcore,
    gone,
    gslot_n,
    gtwo,
    gslot_z,
    gown,
    tslot_z,
    tlow,
    tslot_n,
    sgsend,
    psend,
    pslot,
    pdone,
    sgslot_g,
    sgtwo,
    sgslot_z,
    arslot,
    qslot_z,
    qslot_g,
    vsend,
    vslot_g,
    vslot_z,
    in_sem,
    w_send,
    wz_recv,
    wn_recv,
    wt_recv,
    wc_recv,
    g_send,
    gz_recv,
    gn_recv,
    gt_recv,
    gc_recv,
    s_send,
    s_recv,
):
    A, B, C, R, cw, Pn, D = dims
    n_t = 2 * C
    G = C * B
    dp = lax.axis_index("dp")
    t = lax.axis_index("tensor")
    a, b = dp // B, dp % B
    y, c = t // 2, t % 2
    g = y * B + b

    def device(a_, g_, c_):
        return (a_ * B + g_ % B, (g_ // B) * 2 + c_)

    far = [partner(a, k, A) for k in range(1, A)]
    near = [partner(g, k, G) for k in range(1, G)]
    z_devices = [device(o, g, c) for o in far]
    g_devices = [device(a, o, c) for o in near]
    core_device = device(a, g, 1 - c)
    q_coords = [(partner(g, kg, G), partner(c, kc, 2)) for kg in range(G) for kc in range(2)][1:]
    q_devices = [device(a, o, cc) for o, cc in q_coords]
    steps = [(ka, kg, kc) for ka in range(A) for kg in range(G) for kc in range(2)][1:]
    steps.sort(key=lambda step: -(step[0] + bin(step[1]).count("1") + step[2] / 2))
    everyone = [device(partner(a, ka, A), partner(g, kg, G), partner(c, kc, 2)) for ka, kg, kc in steps]
    others = [d for d, step in zip(everyone, steps) if step[0] and (step[1] or step[2])]

    WZ, WO, WN, WX, WT, WP, WC = range(7)
    FARTHEST = G - 2
    w_turned = W_TURNED if G > 2 else ()
    g_turned = G_TURNED if G > 2 else ()

    def plain_near(m, turned):
        return range(G - 2 if m in turned else G - 1)

    S_PROD, S_NEAR, S_FAR, S_ALL, S_PAR, S_QFAR, S_QNEAR, S_VNEAR, S_VFAR = range(9)

    def remote(src, dst, ssem, rsem, device_id):
        copy = pltpu.make_async_remote_copy(
            src_ref=src,
            dst_ref=dst,
            send_sem=ssem,
            recv_sem=rsem,
            device_id=device_id,
            device_id_type=MESH,
        )
        copy.start()
        return copy

    def arrived(copies):
        for copy in copies:
            copy.wait_recv()

    nears, fars = pl.ds(0, G - 1), pl.ds(0, A - 1)

    local = []
    for i, (src, dst) in enumerate(
        [
            (master_hbm, master),
            (small_hbm, spbuf.at[t]),
            (coords_hbm, coords),
            (model_hbm, model),
            (cells_hbm, cells),
            (valid_hbm, valid),
            (grid_hbm, grid),
            (moment_hbm, moment),
            (msmall_hbm, msmall),
            (average_hbm, average),
            (asmall_hbm, asmall),
        ]
    ):
        copy = pltpu.make_async_copy(src, dst, in_sem.at[i])
        copy.start()
        local.append(copy)

    barrier = pltpu.get_barrier_semaphore()
    peers = z_devices + q_devices
    for d in peers:
        pl.semaphore_signal(barrier, inc=1, device_id=d, device_id_type=MESH)

    local[0].wait()
    for m in range(MOVED):
        wbuf[m, c, y, a, b] = master[m // 2, m % 2].astype(BF16)
    local[1].wait()
    pl.semaphore_wait(barrier, len(peers))

    def piece(m, o, z):
        return wbuf.at[m, c, o // B, z, o % B]

    def line(m, o):
        return wbuf.at[m, c, o // B, :, o % B]

    def plane(m, z):
        return wbuf.at[m, c, :, z]

    def await_bytes(ref, rsem):
        pltpu.make_async_remote_copy(
            src_ref=ref,
            dst_ref=ref,
            send_sem=s_send.at[0],
            recv_sem=rsem,
            device_id=core_device,
            device_id_type=MESH,
        ).wait_recv()

    def slot_sum(ref, count_of, value=None):
        for i in range(count_of):
            term = ref[i].astype(F32)
            value = term if value is None else value + term
        return value

    def await_sent(ref, ssem):
        pltpu.make_async_remote_copy(
            src_ref=ref,
            dst_ref=ref,
            send_sem=ssem,
            recv_sem=s_recv.at[0],
            device_id=core_device,
            device_id_type=MESH,
        ).wait_send()

    def w_far(m, ref):
        return [
            remote(ref, ref, w_send.at[WZ], wz_recv.at[m, k], d) for k, d in enumerate(z_devices)
        ]

    def w_near(m, ref, ks, ssem):
        for k in ks:
            remote(ref, ref, w_send.at[ssem], wn_recv.at[m, k], g_devices[k])

    def w_core(m, ref):
        remote(ref, ref, w_send.at[WC], wc_recv.at[m], core_device)

    for k in range(1, n_t):
        o = (t + k) % n_t
        remote(spbuf.at[t], spbuf.at[t], s_send.at[S_PAR], s_recv.at[S_PAR], (dp, o))
    first = {}
    for m in range(MOVED):
        first[m] = w_far(m, piece(m, g, a))
        w_near(m, piece(m, g, a), reversed(range(G - 1)), WO)

    for copy in local[2:7]:
        copy.wait()
    cols = grid.shape[2]
    shift = (cols - 1).bit_length()
    cell = cells[...].reshape(1, -1)
    row_id = model[...].reshape(1, -1) * grid.shape[1] + (cell >> shift)
    col_id = cell & (cols - 1)
    PB = row_id.shape[1]
    packed = jnp.concatenate(
        [
            coords[...],
            row_id.astype(F32),
            col_id.astype(F32),
            valid[...].reshape(1, -1).astype(F32),
            jnp.zeros((128 - 9, PB), F32),
        ],
        0,
    )
    columns[...] = packed.T
    mine = columns[pl.ds(pl.multiple_of(t * Pn, 8), Pn), :]
    xs = [mine[:, j : j + 1] for j in range(6)]
    mask = mine[:, 8:9]
    row_of = mine[:, 6:7].astype(jnp.int32)
    col_of = mine[:, 7:8].astype(jnp.int32)
    table = grid[...].reshape(-1, cols)
    onehot = (
        lax.broadcasted_iota(jnp.int32, (Pn, table.shape[0]), 1) == row_of
    ).astype(BF16)
    high = table.astype(BF16)
    rest = table - high.astype(F32)
    middle = rest.astype(BF16)
    lowest = (rest - middle.astype(F32)).astype(BF16)
    picked = nn(onehot, high) + nn(onehot, middle) + nn(onehot, lowest)
    lane = lax.broadcasted_iota(jnp.int32, (Pn, cols), 1)
    truth = jnp.sum(jnp.where(lane == col_of, picked, 0.0), 1, keepdims=True)
    seps = [xs[3 + k] - xs[k] for k in range(3)]
    distance = jnp.sqrt(seps[0] * seps[0] + seps[1] * seps[1] + seps[2] * seps[2])
    units = [s / distance for s in seps]

    await_bytes(spbuf.at[pl.ds(0, n_t - 1)], s_recv.at[S_PAR])

    def small_row(i):
        return jnp.concatenate([spbuf[tt, i : i + 1, :] for tt in range(n_t)], 1)

    out_row = small_row(7 + 2 * LAYERS)
    last_low = master[LAYERS - 1, 1].astype(BF16).astype(F32)
    feature = lax.broadcasted_iota(jnp.int32, (R, D), 1) - lax.broadcasted_iota(jnp.int32, (R, D), 0)
    out_column = jnp.sum(jnp.where(feature == dp * R, out_row, 0.0), axis=1, keepdims=True)
    q_part = jnp.sum(last_low * out_column, axis=0, keepdims=True)
    qslot_z[a] = jnp.broadcast_to(q_part, (8, cw))
    for d in z_devices:
        remote(qslot_z.at[a], qslot_z.at[a], s_send.at[S_QFAR], s_recv.at[S_QFAR], d)

    first_rows = [small_row(j) for j in range(6)]
    z0 = small_row(6) + xs[0] * first_rows[0]
    for j in range(1, 6):
        z0 = z0 + xs[j] * first_rows[j]
    inner[...] = z0
    e0 = jnp.exp(jnp.minimum(z0, 0.0))
    slope0 = jnp.where(z0 > 0, 1.0, e0)
    streams[0] = jnp.where(z0 > 0, z0, e0 - 1.0)
    acts[0, 0] = streams[0].astype(BF16)
    for k in range(3):
        streams[1 + k] = slope0 * first_rows[3 + k]
        acts[0, 1 + k] = streams[1 + k].astype(BF16)

    def pass_on(m):
        for k in range(A - 1):
            first[m][k].wait_recv()
            w_near(m, piece(m, g, far[k]), plain_near(m, w_turned), WX if m in w_turned else WN)
        w_core(m, line(m, g))
        if m in w_turned:
            o = near[FARTHEST]
            ref = piece(m, o, a)
            await_bytes(ref, wn_recv.at[m, FARTHEST])
            for d in z_devices:
                remote(ref, ref, w_send.at[WT], wt_recv.at[m], d)

    for m in range(MOVED):
        pass_on(m)
    me_near = g * 2 + c
    await_bytes(qslot_z.at[fars], s_recv.at[S_QFAR])
    qslot_g[me_near] = slot_sum(qslot_z, A)
    for d in q_devices:
        remote(qslot_g.at[me_near], qslot_g.at[me_near], s_send.at[S_QNEAR], s_recv.at[S_QNEAR], d)

    def weight(m):
        return jnp.concatenate([wbuf[m, tt % 2, tt // 2].reshape(D, cw) for tt in range(n_t)], 1)

    M = 4 * Pn

    def block_in(l):
        pre[l] = nn(acts[l].reshape(M, D), weight(2 * l)).reshape(4, Pn, D)
        z = pre[l, 0] + small_row(7 + l)
        e = jnp.exp(jnp.minimum(z, 0.0))
        slope = jnp.where(z > 0, 1.0, e)
        hidden[l, 0] = jnp.where(z > 0, z, e - 1.0).astype(BF16)
        for k in range(1, 4):
            hidden[l, k] = (slope * pre[l, k]).astype(BF16)

    def block_out(l):
        branch = nt(hidden[l].reshape(M, D), weight(2 * l + 1)).reshape(4, Pn, D)
        for s in range(4):
            new = streams[s] + branch[s]
            if s == 0:
                new = new + small_row(7 + LAYERS + l)
            streams[s] = new
            if l + 1 < LAYERS:
                acts[l + 1, s] = new.astype(BF16)

    def fetch(m):
        for k in range(G - 1):
            if m in w_turned and k == FARTHEST:
                await_bytes(wbuf.at[m, c, 0, fars, 0], wt_recv.at[m])
            else:
                await_bytes(line(m, near[k]), wn_recv.at[m, k])
            w_core(m, line(m, near[k]))

    def fetched(m):
        await_bytes(wbuf.at[m, c], wc_recv.at[m])

    for m in range(MOVED):
        fetch(m)
        fetched(m)
        if m == 0:
            for d in others:
                pl.semaphore_signal(barrier, inc=1, device_id=d, device_id_type=MESH)
        if m % 2 == 0:
            block_in(m // 2)
        else:
            block_out(m // 2)
        if m == MOVED - 2:
            proj_a = [jnp.sum(streams[s] * out_row, axis=1, keepdims=True) for s in range(4)]
            bias_row = small_row(6 + 2 * LAYERS)
            proj_a[0] = proj_a[0] + jnp.sum(bias_row * out_row, axis=1, keepdims=True)
            await_bytes(qslot_g.at[pl.ds(0, 2 * G - 1)], s_recv.at[S_QNEAR])
            q_row = []
            for tt in range(n_t):
                total = qslot_g[(tt // 2) * B * 2 + tt % 2, 0:1]
                for i in range(1, B):
                    total = total + qslot_g[((tt // 2) * B + i) * 2 + tt % 2, 0:1]
                q_row.append(total)
            q_row = jnp.concatenate(q_row, 1)

    last = LAYERS - 1
    proj = [
        proj_a[s] + jnp.sum(hidden[last, s].astype(F32) * q_row, axis=1, keepdims=True) for s in range(4)
    ]
    tau = proj[0]
    sign_tau = sign_of(tau)
    abs_tau = jnp.abs(tau)
    grad_time = [units[k] * abs_tau + distance * sign_tau * proj[1 + k] for k in range(3)]
    square = grad_time[0] * grad_time[0] + grad_time[1] * grad_time[1] + grad_time[2] * grad_time[2]
    error = square - truth * truth
    total_err = jnp.sum(mask * jnp.abs(error), axis=0, keepdims=True)
    count = jnp.sum(mask, axis=0, keepdims=True)
    seed = mask * sign_of(error)
    g_time = [2.0 * grad_time[k] * seed for k in range(3)]
    g_tau = sign_tau * (units[0] * g_time[0] + units[1] * g_time[1] + units[2] * g_time[2])
    g_proj = [g_tau] + [distance * sign_tau * g_time[k] for k in range(3)]
    v_row = jnp.sum(
        sum(hidden[last, s].astype(F32) * g_proj[s] for s in range(4)), axis=0, keepdims=True
    )
    for tt in range(n_t):
        vsend[tt % 2, tt // 2] = jnp.broadcast_to(v_row[:, tt * cw : (tt + 1) * cw], (8, cw))
    vslot_g[me_near] = vsend[c, y]
    for (o, cc), d in zip(q_coords, q_devices):
        remote(vsend.at[cc, o // B], vslot_g.at[me_near], s_send.at[S_VNEAR], s_recv.at[S_VNEAR], d)

    def v_far():
        await_bytes(vslot_g.at[pl.ds(0, 2 * G - 1)], s_recv.at[S_VNEAR])
        vslot_z[a] = slot_sum(vslot_g, 2 * G)
        for d in z_devices:
            remote(vslot_z.at[a], vslot_z.at[a], s_send.at[S_VFAR], s_recv.at[S_VFAR], d)

    pieces = [(far[k], k) for k in reversed(range(A - 1))] + [(a, None)]

    def start_core(m, value):
        low = value.astype(BF16)
        for tt in range(n_t):
            block = low[:, tt * cw : (tt + 1) * cw].reshape(A, B, R, cw)
            for i in range(B):
                gsend[m, tt % 2, :, (tt // 2) * B + i] = block[:, i]
        return [
            remote(
                gsend.at[m, 1 - c, z], gcore.at[m, z], g_send.at[WC], gc_recv.at[m, j], core_device
            )
            for j, (z, k) in enumerate(pieces)
        ]

    def core_sum(m, j):
        z = pieces[j][0]
        flying[m][j].wait_recv()
        gone[m, z] = (gsend[m, c, z].astype(F32) + gcore[m, z].astype(F32)).astype(BF16)

    def start_near(m):
        for j, (z, kz) in enumerate(pieces):
            core_sum(m, j)
            for k in plain_near(m, g_turned):
                remote(
                    gone.at[m, z, near[k]],
                    gslot_n.at[m, j, k],
                    g_send.at[WX if m in g_turned else WN],
                    gn_recv.at[m, j],
                    g_devices[k],
                )
            if m in g_turned and kz is not None:
                remote(
                    gone.at[m, z, near[FARTHEST]],
                    tslot_z.at[m, kz],
                    g_send.at[WT],
                    gt_recv.at[m, 0],
                    z_devices[kz],
                )

    def start_far(m):
        count_of = len(plain_near(m, g_turned))
        for j, (z, k) in enumerate(pieces):
            if count_of:
                await_bytes(gslot_n.at[m, j, pl.ds(0, count_of)], gn_recv.at[m, j])
            total = slot_sum(gslot_n.at[m, j], count_of, gone[m, z, g].astype(F32))
            if k is None:
                gown[m] = total
            else:
                gtwo[m, k] = total.astype(BF16)
                remote(gtwo.at[m, k], gslot_z.at[m, k], g_send.at[WZ], gz_recv.at[m], z_devices[k])

    def start_turned(m):
        if m in g_turned:
            await_bytes(tslot_z.at[m], gt_recv.at[m, 0])
            total = slot_sum(tslot_z.at[m], A - 1, gone[m, a, near[FARTHEST]].astype(F32))
            tlow[m] = total.astype(BF16)
            remote(tlow.at[m], tslot_n.at[m], g_send.at[WP], gt_recv.at[m, 1], g_devices[FARTHEST])

    def finish(m):
        await_bytes(gslot_z.at[m], gz_recv.at[m])
        total = slot_sum(gslot_z.at[m], A - 1, gown[m])
        if m in g_turned:
            await_bytes(tslot_n.at[m], gt_recv.at[m, 1])
            total = total + tslot_n[m].astype(F32)
        return total

    flying = {}

    bias_in = [None] * LAYERS
    bias_out = [None] * LAYERS

    def back_last():
        z = pre[last, 0] + small_row(7 + last)
        e = jnp.exp(jnp.minimum(z, 0.0))
        slope = jnp.where(z > 0, 1.0, e)
        curve = jnp.where(z > 0, 0.0, e)
        mixed = g_proj[1] * pre[last, 1] + g_proj[2] * pre[last, 2] + g_proj[3] * pre[last, 3]
        gz = q_row * (g_proj[0] * slope + curve * mixed)
        bias_in[last] = jnp.sum(gz, axis=0, keepdims=True)
        gpre[0] = gz.astype(BF16)
        slope = slope * q_row
        for k in range(1, 4):
            gpre[k] = (g_proj[k] * slope).astype(BF16)

    def back_out(l):
        bias_out[l] = jnp.sum(grad[0], axis=0, keepdims=True)
        gb = gbranch[...].reshape(M, D)
        flying[2 * l + 1] = start_core(2 * l + 1, tn(gb, hidden[l].reshape(M, D)))

    def back_in(l):
        gb = gbranch[...].reshape(M, D)
        gh = nn(gb, weight(2 * l + 1)).reshape(4, Pn, D)
        z = pre[l, 0] + small_row(7 + l)
        e = jnp.exp(jnp.minimum(z, 0.0))
        slope = jnp.where(z > 0, 1.0, e)
        curve = jnp.where(z > 0, 0.0, e)
        gz = gh[0] * slope + curve * (gh[1] * pre[l, 1] + gh[2] * pre[l, 2] + gh[3] * pre[l, 3])
        bias_in[l] = jnp.sum(gz, axis=0, keepdims=True)
        gpre[0] = gz.astype(BF16)
        for k in range(1, 4):
            gpre[k] = (gh[k] * slope).astype(BF16)

    def back_weight(l):
        flying[2 * l] = start_core(2 * l, tn(acts[l].reshape(M, D), gpre[...].reshape(M, D)))

    def back_through(l):
        back = nt(gpre[...].reshape(M, D), weight(2 * l)).reshape(4, Pn, D)
        for s in range(4):
            value = (out_row * g_proj[s] if l == last else grad[s]) + back[s]
            grad[s] = value
            if l > 0:
                gbranch[s] = value.astype(BF16)

    back_last()
    back_weight(1)
    tau_sum = jnp.sum(g_proj[0], axis=0, keepdims=True)
    bias_out[last] = out_row * tau_sum
    g_out_row = bias_row * tau_sum + jnp.sum(
        streams[0] * g_proj[0] + streams[1] * g_proj[1] + streams[2] * g_proj[2] + streams[3] * g_proj[3],
        axis=0,
        keepdims=True,
    )
    back_through(1)
    back_out(0)
    start_near(2)
    back_in(0)
    back_weight(0)
    start_near(1)
    back_through(0)
    v_far()
    start_near(0)

    z0 = inner[...]
    e0 = jnp.exp(jnp.minimum(z0, 0.0))
    slope0 = jnp.where(z0 > 0, 1.0, e0)
    curve0 = jnp.where(z0 > 0, 0.0, e0)
    first_rows = [small_row(j) for j in range(6)]
    g_inner = grad[0] * slope0 + curve0 * (
        grad[1] * first_rows[3] + grad[2] * first_rows[4] + grad[3] * first_rows[5]
    )
    rows = [jnp.sum(xs[j] * g_inner, axis=0, keepdims=True) for j in range(6)]
    for k in range(3):
        rows[3 + k] = rows[3 + k] + jnp.sum(grad[1 + k] * slope0, axis=0, keepdims=True)
    rows.append(jnp.sum(g_inner, axis=0, keepdims=True))
    rows = rows + bias_in + bias_out + [g_out_row]

    lanes = lax.broadcasted_iota(jnp.int32, (1, cw), 1)
    weight_sq = jnp.zeros((1, cw), F32)
    for m in range(MATS):
        part = jnp.sum(master[m // 2, m % 2] * master[m // 2, m % 2], keepdims=True)
        weight_sq = jnp.where(lanes == m, part, weight_sq)
    own_small = spbuf[t]
    weight_sq = jnp.where(lanes == MATS, jnp.sum(own_small * own_small, keepdims=True) / (A * B), weight_sq)
    tail = [
        jnp.broadcast_to(total_err, (1, cw)),
        jnp.broadcast_to(count, (1, cw)),
        weight_sq,
        jnp.zeros((1, cw), F32),
    ]
    for tt in range(n_t):
        sgsend[tt % 2, tt // 2] = jnp.concatenate([r[:, tt * cw : (tt + 1) * cw] for r in rows] + tail, 0)
    sgslot_g[me_near] = sgsend[c, y]
    for (o, cc), d in zip(q_coords, q_devices):
        remote(sgsend.at[cc, o // B], sgslot_g.at[me_near], s_send.at[S_NEAR], s_recv.at[S_NEAR], d)

    await_bytes(vslot_z.at[fars], s_recv.at[S_VFAR])
    v_part = slot_sum(vslot_z, A)[0:1]
    product = jnp.sum(last_low * v_part, axis=1, keepdims=True)
    place = lax.broadcasted_iota(jnp.int32, (R, cw), 1) - lax.broadcasted_iota(jnp.int32, (R, cw), 0)
    product_row = jnp.sum(jnp.where(place == (dp * R) % cw, product, 0.0), axis=0, keepdims=True)
    psend[...] = jnp.broadcast_to(product_row, (8, cw))
    column = (dp * R) // cw
    mine_too = column == t
    slot = (dp % (cw // R)) * n_t + t
    pl.semaphore_wait(barrier, len(others))
    for k in range(1, A * B):
        remote(
            psend, pslot.at[slot], s_send.at[S_PROD], s_recv.at[S_PROD], (partner(dp, k, A * B), column)
        )

    @pl.when(mine_too)
    def _():
        pslot[slot] = psend[...]

    @pl.when(jnp.logical_not(mine_too))
    def _():
        remote(psend, pslot.at[slot], s_send.at[S_PROD], s_recv.at[S_PROD], (dp, column))

    def await_products(wait, ref, count_of, sems):
        @pl.when(mine_too)
        def _():
            wait(ref.at[pl.ds(0, count_of - 1)], sems.at[S_PROD])

        @pl.when(jnp.logical_not(mine_too))
        def _():
            wait(ref.at[pl.ds(0, count_of)], sems.at[S_PROD])

    start_far(2)
    start_turned(2)
    start_far(1)
    start_turned(1)
    start_far(0)
    start_turned(0)
    await_bytes(sgslot_g.at[pl.ds(0, 2 * G - 1)], s_recv.at[S_NEAR])
    sgtwo[...] = slot_sum(sgslot_g, 2 * G)
    sgslot_z[a] = sgtwo[...]
    for d in z_devices:
        remote(sgtwo, sgslot_z.at[a], s_send.at[S_FAR], s_recv.at[S_FAR], d)

    for copy in local[7:]:
        copy.wait()
    grad_b[last, 1] = out_column * v_part
    for m in (1, 2, 0):
        grad_b[m // 2, m % 2] = finish(m)
    await_bytes(sgslot_z.at[pl.ds(0, A - 1)], s_recv.at[S_FAR])
    sred[...] = slot_sum(sgslot_z, A)
    slots = (cw // R) * n_t
    await_products(await_bytes, pslot, slots, s_recv)
    head_row = sred[SMALL - 1 : SMALL]
    for i in range(slots):
        head_row = head_row + pslot[i, 0:1]
    sred[SMALL - 1 : SMALL] = head_row
    counted = sred[SMALL + 1 : SMALL + 2, 0:1]
    tile_rows = lax.broadcasted_iota(jnp.int32, (8, 128), 0)
    parts = jnp.zeros((8, 128), F32)

    def step(gradient, momentum):
        new = momentum_coef * momentum + gradient
        return new, gradient + momentum_coef * new

    for m in range(MATS):
        at = (m // 2, m % 2)
        gr = grad_b[at] / counted
        new, direction = step(gr, moment[at])
        grad_b[at] = gr
        moment_b[at] = new
        parts = jnp.where(tile_rows == m, jnp.sum(direction * direction, keepdims=True), parts)
    gr = sred[0:SMALL, :] / counted
    new, dir_small = step(gr, msmall[...])
    grad_s[...] = gr
    moment_s[...] = new
    parts = jnp.where(
        tile_rows == MATS, jnp.sum(dir_small * dir_small, keepdims=True) / (A * B), parts
    )
    me = (a * G + g) * 2 + c
    arslot[me] = parts
    for d in everyone:
        remote(arslot.at[me], arslot.at[me], s_send.at[S_ALL], s_recv.at[S_ALL], d)
    loss_b[...] = sred[SMALL : SMALL + 1, 0:1] / counted
    bias_b[...] = grad_s[7 : 7 + 2 * LAYERS, :]
    await_bytes(arslot.at[pl.ds(0, len(everyone))], s_recv.at[S_ALL])
    dir_sq = jnp.sum(arslot[...], axis=0)

    def rate_of(m):
        size = sred[SMALL + 2 : SMALL + 3, m : m + 1]
        return spread_rate * jnp.sqrt(size) / jnp.sqrt(dir_sq[m : m + 1, 0:1] + norm_epsilon)

    for m in range(MATS):
        at = (m // 2, m % 2)
        direction = grad_b[at] + momentum_coef * moment_b[at]
        new = master[at] - rate_of(m) * direction
        master_b[at] = new
        average_b[at] = average_decay * average[at] + (1.0 - average_decay) * new
        low_b[at] = new.astype(BF16)
    new = own_small - rate_of(MATS) * dir_small
    master_s[...] = new
    average_s[...] = average_decay * asmall[...] + (1.0 - average_decay) * new

    for sems, turned, passed in ((w_send, w_turned, A - 1), (g_send, g_turned, A)):
        few, many = pl.ds(0, len(turned)), pl.ds(0, MOVED - len(turned))
        all_passed = pl.ds(0, passed)
        await_sent(gone.at[:, fars, 0], sems.at[WZ])
        if len(turned) < MOVED:
            await_sent(gone.at[many, all_passed, nears], sems.at[WN])
        if turned:
            await_sent(gone.at[few, all_passed, pl.ds(0, G - 2)], sems.at[WX])
            await_sent(gone.at[few, fars, 0], sems.at[WT])
        await_sent(gone, sems.at[WC])
    await_sent(gone.at[:, 0, nears], w_send.at[WO])
    if g_turned:
        await_sent(gone.at[pl.ds(0, len(g_turned)), 0, 0], g_send.at[WP])
    await_sent(qslot_z.at[fars], s_send.at[S_QFAR])
    await_sent(vslot_z.at[fars], s_send.at[S_VFAR])
    await_sent(qslot_g.at[pl.ds(0, 2 * G - 1)], s_send.at[S_QNEAR])
    await_sent(vslot_g.at[pl.ds(0, 2 * G - 1)], s_send.at[S_VNEAR])
    await_sent(sgslot_g.at[pl.ds(0, 2 * G - 1)], s_send.at[S_NEAR])
    await_products(await_sent, pdone, A * B, s_send)
    await_sent(sgslot_z.at[fars], s_send.at[S_FAR])
    await_sent(arslot.at[pl.ds(0, len(everyone))], s_send.at[S_ALL])
    await_sent(spbuf.at[pl.ds(0, n_t - 1)], s_send.at[S_PAR])


def write_out(*refs):
    sems = refs[-1]
    count = (len(refs) - 1) // 2
    copies = [
        pltpu.make_async_copy(refs[i], refs[count + i], sems.at[i]) for i in range(count)
    ]
    for copy in copies:
        copy.start()
    for copy in copies:
        copy.wait()


def body(
    axes,
    coords,
    model_ids,
    cells,
    valid,
    slowness_grid,
    master_blocks,
    small_params,
    moment_blocks,
    moment_small,
    average_blocks,
    average_small,
):
    n_dp, n_t = axes
    A = 4 if n_dp % 4 == 0 else n_dp
    B = n_dp // A
    C = n_t // 2
    G = C * B
    R, cw = master_blocks.shape[2:]
    D = R * n_dp
    PB = coords.shape[1]
    Pn = PB // n_t
    dims = (A, B, C, R, cw, Pn, D)
    anywhere = pl.BlockSpec(memory_space=pltpu.HBM)
    vmem = pl.BlockSpec(memory_space=pltpu.VMEM)
    S = SMALL + 4
    args = (
        coords,
        model_ids,
        cells,
        valid,
        slowness_grid,
        master_blocks,
        small_params,
        moment_blocks,
        moment_small,
        average_blocks,
        average_small,
    )
    V = pltpu.VMEM
    DMA = pltpu.SemaphoreType.DMA
    block = (master_blocks.shape, F32)
    short = (small_params.shape, F32)
    shapes = [
        ((1, 1), F32),
        block,
        short,
        ((2 * LAYERS, cw), F32),
        block,
        short,
        block,
        short,
        block,
        short,
        (master_blocks.shape, BF16),
    ]
    results = pl.pallas_call(
        functools.partial(kernel, dims),
        out_shape=tuple(V(*shape) for shape in shapes),
        in_specs=[anywhere] * len(args),
        out_specs=(vmem,) * len(shapes),
        scratch_shapes=[
            V(coords.shape, F32),
            V((PB,), jnp.int32),
            V((PB,), jnp.int32),
            V((PB,), jnp.int32),
            V(slowness_grid.shape, F32),
            V(master_blocks.shape, F32),
            V(master_blocks.shape, F32),
            V(small_params.shape, F32),
            V(master_blocks.shape, F32),
            V(small_params.shape, F32),
            V((n_t, SMALL, cw), F32),
            V((PB, 128), F32),
            V((S, cw), F32),
            V((MOVED, 2, C, A, B, R, cw), BF16),
            V((4, Pn, D), F32),
            V((LAYERS, 4, Pn, D), BF16),
            V((LAYERS, 4, Pn, D), F32),
            V((LAYERS, 4, Pn, D), BF16),
            V((4, Pn, D), F32),
            V((4, Pn, D), BF16),
            V((4, Pn, D), BF16),
            V((Pn, D), F32),
            V((MOVED, 2, A, G, R, cw), BF16),
            V((MOVED, A, G, R, cw), BF16),
            V((MOVED, A, G, R, cw), BF16),
            V((MOVED, A, G - 1, R, cw), BF16),
            V((MOVED, A - 1, R, cw), BF16),
            V((MOVED, A - 1, R, cw), BF16),
            V((MOVED, R, cw), F32),
            V((MOVED, A - 1, R, cw), BF16),
            V((MOVED, R, cw), BF16),
            V((MOVED, R, cw), BF16),
            V((2, C, S, cw), F32),
            V((8, cw), F32),
            V(((cw // R) * n_t, 8, cw), F32),
            V((n_dp, 8, cw), F32),
            V((2 * G, S, cw), F32),
            V((S, cw), F32),
            V((A, S, cw), F32),
            V((2 * A * G, 8, 128), F32),
            V((A, 8, cw), F32),
            V((2 * G, 8, cw), F32),
            V((2, C, 8, cw), F32),
            V((2 * G, 8, cw), F32),
            V((A, 8, cw), F32),
            pltpu.SemaphoreType.DMA((len(args),)),
            DMA((7,)),
            DMA((MOVED, A - 1)),
            DMA((MOVED, G - 1)),
            DMA((MOVED,)),
            DMA((MOVED,)),
            DMA((7,)),
            DMA((MOVED,)),
            DMA((MOVED, A)),
            DMA((MOVED, 2)),
            DMA((MOVED, A)),
            DMA((9,)),
            DMA((9,)),
        ],
        compiler_params=pltpu.CompilerParams(
            collective_id=0, has_side_effects=True, vmem_limit_bytes=60 << 20
        ),
    )(*args)

    results = pl.pallas_call(
        write_out,
        out_shape=tuple(jax.ShapeDtypeStruct(*shape) for shape in shapes),
        in_specs=[vmem] * len(shapes),
        out_specs=(anywhere,) * len(shapes),
        scratch_shapes=[pltpu.SemaphoreType.DMA((len(shapes),))],
        compiler_params=pltpu.CompilerParams(vmem_limit_bytes=4 << 20),
    )(*results)
    return (results[0].reshape(()),) + tuple(results[1:])


def solution(mesh):
    blocks = P(None, None, "dp", "tensor")
    small = P(None, "tensor")
    in_specs = (
        P(None, "dp"),
        P("dp"),
        P("dp"),
        P("dp"),
        P(),
        blocks,
        small,
        blocks,
        small,
        blocks,
        small,
    )
    out_specs = (P(), blocks, small, small, blocks, small, blocks, small, blocks, small, blocks)
    axes = (mesh.shape["dp"], mesh.shape["tensor"])
    return jax.shard_map(
        functools.partial(body, axes), mesh=mesh, in_specs=in_specs, out_specs=out_specs, check_vma=False
    )
```

```python
import functools

import jax
import jax.numpy as jnp
from jax import lax
from jax.experimental import pallas as pl
from jax.experimental.pallas import tpu as pltpu
from jax.sharding import PartitionSpec as P

LAYERS = 2
MATS = 2 * LAYERS
SMALL = 12
MESH = pl.DeviceIdType.MESH
F32 = jnp.float32
BF16 = jnp.bfloat16

momentum_coef = 0.5
average_decay = 0.5
spread_rate = 0.5
norm_epsilon = 1e-12

MOVED = MATS - 1
W_TURNED = (0, 1)
G_TURNED = (2, 1, 0)


def partner(i, k, size):
    bit = 1
    while bit < size:
        if (k // bit) % 2:
            i = i + bit - 2 * bit * ((i // bit) % 2)
        bit *= 2
    return i


def nn(left, right):
    return lax.dot_general(left, right, (((1,), (0,)), ((), ())), preferred_element_type=F32)


def nt(left, right):
    return lax.dot_general(left, right, (((1,), (1,)), ((), ())), preferred_element_type=F32)


def tn(left, right):
    return lax.dot_general(left, right, (((0,), (0,)), ((), ())), preferred_element_type=F32)


def sign_of(v):
    return jnp.where(v > 0, 1.0, jnp.where(v < 0, -1.0, 0.0))


def kernel(
    dims,
    coords_hbm,
    model_hbm,
    cells_hbm,
    valid_hbm,
    grid_hbm,
    master_hbm,
    small_hbm,
    moment_hbm,
    msmall_hbm,
    average_hbm,
    asmall_hbm,
    loss_b,
    grad_b,
    grad_s,
    bias_b,
    moment_b,
    moment_s,
    master_b,
    master_s,
    average_b,
    average_s,
    low_b,
    coords,
    model,
    cells,
    valid,
    grid,
    master,
    moment,
    msmall,
    average,
    asmall,
    spbuf,
    columns,
    sred,
    wbuf,
    streams,
    acts,
    pre,
    hidden,
    grad,
    gbranch,
    gpre,
    inner,
    gsend,
    gcore,
    gone,
    gslot_n,
    gtwo,
    gslot_z,
    gown,
    tslot_z,
    tlow,
    tslot_n,
    sgsend,
    psend,
    pslot,
    pdone,
    sized,
    sgslot_g,
    sgtwo,
    sgslot_z,
    arslot,
    qslot_z,
    qslot_g,
    vsend,
    vslot_g,
    vslot_z,
    in_sem,
    w_send,
    wz_recv,
    wn_recv,
    wt_recv,
    wc_recv,
    g_send,
    gz_recv,
    gn_recv,
    gt_recv,
    gc_recv,
    s_send,
    s_recv,
):
    A, B, C, R, cw, Pn, D = dims
    n_t = 2 * C
    G = C * B
    dp = lax.axis_index("dp")
    t = lax.axis_index("tensor")
    a, b = dp // B, dp % B
    y, c = t // 2, t % 2
    g = y * B + b

    def device(a_, g_, c_):
        return (a_ * B + g_ % B, (g_ // B) * 2 + c_)

    far = [partner(a, k, A) for k in range(1, A)]
    near = [partner(g, k, G) for k in range(1, G)]
    z_devices = [device(o, g, c) for o in far]
    g_devices = [device(a, o, c) for o in near]
    core_device = device(a, g, 1 - c)
    q_coords = [(partner(g, kg, G), partner(c, kc, 2)) for kg in range(G) for kc in range(2)][1:]
    q_devices = [device(a, o, cc) for o, cc in q_coords]
    steps = [(ka, kg, kc) for ka in range(A) for kg in range(G) for kc in range(2)][1:]
    steps.sort(key=lambda step: -(step[0] + bin(step[1]).count("1") + step[2] / 2))
    everyone = [device(partner(a, ka, A), partner(g, kg, G), partner(c, kc, 2)) for ka, kg, kc in steps]
    others = [d for d, step in zip(everyone, steps) if step[0] and (step[1] or step[2])]

    FARTHEST = G - 2
    w_turned = W_TURNED if G > 2 else ()
    g_turned = G_TURNED if G > 2 else ()

    def plain_near(m, turned):
        return range(G - 2 if m in turned else G - 1)

    S_PROD, S_NEAR, S_FAR, S_ALL, S_PAR, S_QFAR, S_QNEAR, S_VNEAR, S_VFAR = range(9)

    def remote(src, dst, ssem, rsem, device_id):
        copy = pltpu.make_async_remote_copy(
            src_ref=src,
            dst_ref=dst,
            send_sem=ssem,
            recv_sem=rsem,
            device_id=device_id,
            device_id_type=MESH,
        )
        copy.start()
        return copy

    def arrived(copies):
        for copy in copies:
            copy.wait_recv()

    nears, fars = pl.ds(0, G - 1), pl.ds(0, A - 1)

    local = []
    for i, (src, dst) in enumerate(
        [
            (master_hbm, master),
            (small_hbm, spbuf.at[t]),
            (coords_hbm, coords),
            (model_hbm, model),
            (cells_hbm, cells),
            (valid_hbm, valid),
            (grid_hbm, grid),
            (moment_hbm, moment),
            (msmall_hbm, msmall),
            (average_hbm, average),
            (asmall_hbm, asmall),
        ]
    ):
        copy = pltpu.make_async_copy(src, dst, in_sem.at[i])
        copy.start()
        local.append(copy)

    barrier = pltpu.get_barrier_semaphore()
    peers = z_devices + q_devices
    for d in peers:
        pl.semaphore_signal(barrier, inc=1, device_id=d, device_id_type=MESH)

    local[0].wait()
    for m in range(MOVED):
        wbuf[m, c, y, a, b] = master[m // 2, m % 2].astype(BF16)
    local[1].wait()
    pl.semaphore_wait(barrier, len(peers))

    def piece(m, o, z):
        return wbuf.at[m, c, o // B, z, o % B]

    def line(m, o):
        return wbuf.at[m, c, o // B, :, o % B]

    def plane(m, z):
        return wbuf.at[m, c, :, z]

    def await_bytes(ref, rsem):
        pltpu.make_async_remote_copy(
            src_ref=ref,
            dst_ref=ref,
            send_sem=s_send.at[0],
            recv_sem=rsem,
            device_id=core_device,
            device_id_type=MESH,
        ).wait_recv()

    def slot_sum(ref, count_of, value=None):
        for i in range(count_of):
            term = ref[i].astype(F32)
            value = term if value is None else value + term
        return value

    def await_sent(ref, ssem):
        pltpu.make_async_remote_copy(
            src_ref=ref,
            dst_ref=ref,
            send_sem=ssem,
            recv_sem=s_recv.at[0],
            device_id=core_device,
            device_id_type=MESH,
        ).wait_send()

    def w_far(m, ref):
        return [
            remote(ref, ref, w_send.at[0], wz_recv.at[m, k], d) for k, d in enumerate(z_devices)
        ]

    def w_near(m, ref, ks):
        for k in ks:
            remote(ref, ref, w_send.at[0], wn_recv.at[m, k], g_devices[k])

    def w_core(m, ref):
        remote(ref, ref, w_send.at[0], wc_recv.at[m], core_device)

    for k in range(1, n_t):
        o = (t + k) % n_t
        remote(spbuf.at[t], spbuf.at[t], s_send.at[S_PAR], s_recv.at[S_PAR], (dp, o))
    first = {}
    for m in range(MOVED):
        first[m] = w_far(m, piece(m, g, a))
        w_near(m, piece(m, g, a), reversed(range(G - 1)))

    for copy in local[2:7]:
        copy.wait()
    cols = grid.shape[2]
    shift = (cols - 1).bit_length()
    cell = cells[...].reshape(1, -1)
    row_id = model[...].reshape(1, -1) * grid.shape[1] + (cell >> shift)
    col_id = cell & (cols - 1)
    PB = row_id.shape[1]
    packed = jnp.concatenate(
        [
            coords[...],
            row_id.astype(F32),
            col_id.astype(F32),
            valid[...].reshape(1, -1).astype(F32),
            jnp.zeros((128 - 9, PB), F32),
        ],
        0,
    )
    columns[...] = packed.T
    mine = columns[pl.ds(pl.multiple_of(t * Pn, 8), Pn), :]
    xs = [mine[:, j : j + 1] for j in range(6)]
    mask = mine[:, 8:9]
    row_of = mine[:, 6:7].astype(jnp.int32)
    col_of = mine[:, 7:8].astype(jnp.int32)
    table = grid[...].reshape(-1, cols)
    onehot = (
        lax.broadcasted_iota(jnp.int32, (Pn, table.shape[0]), 1) == row_of
    ).astype(BF16)
    high = table.astype(BF16)
    rest = table - high.astype(F32)
    middle = rest.astype(BF16)
    lowest = (rest - middle.astype(F32)).astype(BF16)
    picked = nn(onehot, high) + nn(onehot, middle) + nn(onehot, lowest)
    lane = lax.broadcasted_iota(jnp.int32, (Pn, cols), 1)
    truth = jnp.sum(jnp.where(lane == col_of, picked, 0.0), 1, keepdims=True)
    seps = [xs[3 + k] - xs[k] for k in range(3)]
    distance = jnp.sqrt(seps[0] * seps[0] + seps[1] * seps[1] + seps[2] * seps[2])
    units = [s / distance for s in seps]

    await_bytes(spbuf.at[pl.ds(0, n_t - 1)], s_recv.at[S_PAR])

    def small_row(i):
        return jnp.concatenate([spbuf[tt, i : i + 1, :] for tt in range(n_t)], 1)

    out_row = small_row(7 + 2 * LAYERS)
    last_low = master[LAYERS - 1, 1].astype(BF16).astype(F32)
    feature = lax.broadcasted_iota(jnp.int32, (R, D), 1) - lax.broadcasted_iota(jnp.int32, (R, D), 0)
    out_column = jnp.sum(jnp.where(feature == dp * R, out_row, 0.0), axis=1, keepdims=True)
    q_part = jnp.sum(last_low * out_column, axis=0, keepdims=True)
    count = jnp.sum(mask, axis=0, keepdims=True)
    row_of_8 = lax.broadcasted_iota(jnp.int32, (8, cw), 0)
    qslot_z[a] = jnp.where(row_of_8 == 0, q_part, count)
    for d in z_devices:
        remote(qslot_z.at[a], qslot_z.at[a], s_send.at[S_QFAR], s_recv.at[S_QFAR], d)

    first_rows = [small_row(j) for j in range(6)]
    z0 = small_row(6) + xs[0] * first_rows[0]
    for j in range(1, 6):
        z0 = z0 + xs[j] * first_rows[j]
    inner[...] = z0
    e0 = jnp.exp(jnp.minimum(z0, 0.0))
    slope0 = jnp.where(z0 > 0, 1.0, e0)
    streams[0] = jnp.where(z0 > 0, z0, e0 - 1.0)
    acts[0, 0] = streams[0].astype(BF16)
    for k in range(3):
        streams[1 + k] = slope0 * first_rows[3 + k]
        acts[0, 1 + k] = streams[1 + k].astype(BF16)

    def pass_on(m):
        for k in range(A - 1):
            first[m][k].wait_recv()
            w_near(m, piece(m, g, far[k]), plain_near(m, w_turned))
        w_core(m, line(m, g))
        if m in w_turned:
            o = near[FARTHEST]
            ref = piece(m, o, a)
            await_bytes(ref, wn_recv.at[m, FARTHEST])
            for d in z_devices:
                remote(ref, ref, w_send.at[0], wt_recv.at[m], d)

    for m in range(MOVED):
        pass_on(m)
    me_near = g * 2 + c
    await_bytes(qslot_z.at[fars], s_recv.at[S_QFAR])
    qslot_g[me_near] = slot_sum(qslot_z, A)
    for d in q_devices:
        remote(qslot_g.at[me_near], qslot_g.at[me_near], s_send.at[S_QNEAR], s_recv.at[S_QNEAR], d)

    def weight(m):
        return jnp.concatenate([wbuf[m, tt % 2, tt // 2].reshape(D, cw) for tt in range(n_t)], 1)

    M = 4 * Pn

    def block_in(l):
        pre[l] = nn(acts[l].reshape(M, D), weight(2 * l)).reshape(4, Pn, D)
        z = pre[l, 0] + small_row(7 + l)
        e = jnp.exp(jnp.minimum(z, 0.0))
        slope = jnp.where(z > 0, 1.0, e)
        hidden[l, 0] = jnp.where(z > 0, z, e - 1.0).astype(BF16)
        for k in range(1, 4):
            hidden[l, k] = (slope * pre[l, k]).astype(BF16)

    def block_out(l):
        branch = nt(hidden[l].reshape(M, D), weight(2 * l + 1)).reshape(4, Pn, D)
        for s in range(4):
            new = streams[s] + branch[s]
            if s == 0:
                new = new + small_row(7 + LAYERS + l)
            streams[s] = new
            if l + 1 < LAYERS:
                acts[l + 1, s] = new.astype(BF16)

    def fetch(m):
        for k in range(G - 1):
            if m in w_turned and k == FARTHEST:
                await_bytes(wbuf.at[m, c, 0, fars, 0], wt_recv.at[m])
            else:
                await_bytes(line(m, near[k]), wn_recv.at[m, k])
            w_core(m, line(m, near[k]))

    def fetched(m):
        await_bytes(wbuf.at[m, c], wc_recv.at[m])

    for m in range(MOVED):
        fetch(m)
        fetched(m)
        if m == 0:
            for d in others:
                pl.semaphore_signal(barrier, inc=1, device_id=d, device_id_type=MESH)
        if m % 2 == 0:
            block_in(m // 2)
        else:
            block_out(m // 2)
        if m == MOVED - 2:
            proj_a = [jnp.sum(streams[s] * out_row, axis=1, keepdims=True) for s in range(4)]
            bias_row = small_row(6 + 2 * LAYERS)
            proj_a[0] = proj_a[0] + jnp.sum(bias_row * out_row, axis=1, keepdims=True)
            await_bytes(qslot_g.at[pl.ds(0, 2 * G - 1)], s_recv.at[S_QNEAR])
            q_row = []
            for tt in range(n_t):
                total = qslot_g[(tt // 2) * B * 2 + tt % 2, 0:1]
                for i in range(1, B):
                    total = total + qslot_g[((tt // 2) * B + i) * 2 + tt % 2, 0:1]
                q_row.append(total)
            q_row = jnp.concatenate(q_row, 1)
            counted = slot_sum(qslot_g, 2 * G)[1:2, 0:1]

    last = LAYERS - 1
    proj = [
        proj_a[s] + jnp.sum(hidden[last, s].astype(F32) * q_row, axis=1, keepdims=True) for s in range(4)
    ]
    tau = proj[0]
    sign_tau = sign_of(tau)
    abs_tau = jnp.abs(tau)
    grad_time = [units[k] * abs_tau + distance * sign_tau * proj[1 + k] for k in range(3)]
    square = grad_time[0] * grad_time[0] + grad_time[1] * grad_time[1] + grad_time[2] * grad_time[2]
    error = square - truth * truth
    total_err = jnp.sum(mask * jnp.abs(error), axis=0, keepdims=True)
    seed = mask * sign_of(error)
    g_time = [2.0 * grad_time[k] * seed for k in range(3)]
    g_tau = sign_tau * (units[0] * g_time[0] + units[1] * g_time[1] + units[2] * g_time[2])
    g_proj = [g_tau] + [distance * sign_tau * g_time[k] for k in range(3)]
    v_row = jnp.sum(
        sum(hidden[last, s].astype(F32) * g_proj[s] for s in range(4)), axis=0, keepdims=True
    )
    for tt in range(n_t):
        vsend[tt % 2, tt // 2] = jnp.broadcast_to(v_row[:, tt * cw : (tt + 1) * cw], (8, cw))
    vslot_g[me_near] = vsend[c, y]
    for (o, cc), d in zip(q_coords, q_devices):
        remote(vsend.at[cc, o // B], vslot_g.at[me_near], s_send.at[S_VNEAR], s_recv.at[S_VNEAR], d)

    def v_far():
        await_bytes(vslot_g.at[pl.ds(0, 2 * G - 1)], s_recv.at[S_VNEAR])
        vslot_z[a] = slot_sum(vslot_g, 2 * G)
        for d in z_devices:
            remote(vslot_z.at[a], vslot_z.at[a], s_send.at[S_VFAR], s_recv.at[S_VFAR], d)

    pieces = [(far[k], k) for k in reversed(range(A - 1))] + [(a, None)]

    def start_core(m, value):
        low = value.astype(BF16)
        for tt in range(n_t):
            block = low[:, tt * cw : (tt + 1) * cw].reshape(A, B, R, cw)
            for i in range(B):
                gsend[m, tt % 2, :, (tt // 2) * B + i] = block[:, i]
        for z, _ in pieces:
            remote(gsend.at[m, 1 - c, z], gcore.at[m, z], g_send.at[0], gc_recv.at[m], core_device)

    def core_sum(m, j):
        z = pieces[j][0]
        gone[m, z] = (gsend[m, c, z].astype(F32) + gcore[m, z].astype(F32)).astype(BF16)

    def start_near(m):
        await_bytes(gcore.at[m], gc_recv.at[m])
        for j, (z, kz) in enumerate(pieces):
            core_sum(m, j)
            for k in plain_near(m, g_turned):
                remote(
                    gone.at[m, z, near[k]],
                    gslot_n.at[m, j, k],
                    g_send.at[0],
                    gn_recv.at[m, j],
                    g_devices[k],
                )
            if m in g_turned and kz is not None:
                remote(
                    gone.at[m, z, near[FARTHEST]],
                    tslot_z.at[m, kz],
                    g_send.at[0],
                    gt_recv.at[m, 0],
                    z_devices[kz],
                )

    def start_far(m):
        count_of = len(plain_near(m, g_turned))
        for j, (z, k) in enumerate(pieces):
            if count_of:
                await_bytes(gslot_n.at[m, j, pl.ds(0, count_of)], gn_recv.at[m, j])
            total = slot_sum(gslot_n.at[m, j], count_of, gone[m, z, g].astype(F32))
            if k is None:
                gown[m] = total
            else:
                gtwo[m, k] = total.astype(BF16)
                remote(gtwo.at[m, k], gslot_z.at[m, k], g_send.at[0], gz_recv.at[m], z_devices[k])

    def start_turned(m):
        if m in g_turned:
            await_bytes(tslot_z.at[m], gt_recv.at[m, 0])
            total = slot_sum(tslot_z.at[m], A - 1, gone[m, a, near[FARTHEST]].astype(F32))
            tlow[m] = total.astype(BF16)
            remote(tlow.at[m], tslot_n.at[m], g_send.at[0], gt_recv.at[m, 1], g_devices[FARTHEST])

    def finish(m):
        await_bytes(gslot_z.at[m], gz_recv.at[m])
        total = slot_sum(gslot_z.at[m], A - 1, gown[m])
        if m in g_turned:
            await_bytes(tslot_n.at[m], gt_recv.at[m, 1])
            total = total + tslot_n[m].astype(F32)
        return total

    bias_in = [None] * LAYERS
    bias_out = [None] * LAYERS

    def back_last():
        z = pre[last, 0] + small_row(7 + last)
        e = jnp.exp(jnp.minimum(z, 0.0))
        slope = jnp.where(z > 0, 1.0, e)
        curve = jnp.where(z > 0, 0.0, e)
        mixed = g_proj[1] * pre[last, 1] + g_proj[2] * pre[last, 2] + g_proj[3] * pre[last, 3]
        gz = q_row * (g_proj[0] * slope + curve * mixed)
        bias_in[last] = jnp.sum(gz, axis=0, keepdims=True)
        gpre[0] = gz.astype(BF16)
        slope = slope * q_row
        for k in range(1, 4):
            gpre[k] = (g_proj[k] * slope).astype(BF16)

    def back_out(l):
        bias_out[l] = jnp.sum(grad[0], axis=0, keepdims=True)
        gb = gbranch[...].reshape(M, D)
        start_core(2 * l + 1, tn(gb, hidden[l].reshape(M, D)))

    def back_in(l):
        gb = gbranch[...].reshape(M, D)
        gh = nn(gb, weight(2 * l + 1)).reshape(4, Pn, D)
        z = pre[l, 0] + small_row(7 + l)
        e = jnp.exp(jnp.minimum(z, 0.0))
        slope = jnp.where(z > 0, 1.0, e)
        curve = jnp.where(z > 0, 0.0, e)
        gz = gh[0] * slope + curve * (gh[1] * pre[l, 1] + gh[2] * pre[l, 2] + gh[3] * pre[l, 3])
        bias_in[l] = jnp.sum(gz, axis=0, keepdims=True)
        gpre[0] = gz.astype(BF16)
        for k in range(1, 4):
            gpre[k] = (gh[k] * slope).astype(BF16)

    def back_weight(l):
        start_core(2 * l, tn(acts[l].reshape(M, D), gpre[...].reshape(M, D)))

    def back_through(l):
        back = nt(gpre[...].reshape(M, D), weight(2 * l)).reshape(4, Pn, D)
        for s in range(4):
            value = (out_row * g_proj[s] if l == last else grad[s]) + back[s]
            grad[s] = value
            if l > 0:
                gbranch[s] = value.astype(BF16)

    back_last()
    back_weight(1)
    tau_sum = jnp.sum(g_proj[0], axis=0, keepdims=True)
    bias_out[last] = out_row * tau_sum
    g_out_row = bias_row * tau_sum + jnp.sum(
        streams[0] * g_proj[0] + streams[1] * g_proj[1] + streams[2] * g_proj[2] + streams[3] * g_proj[3],
        axis=0,
        keepdims=True,
    )
    back_through(1)
    back_out(0)
    start_near(2)
    back_in(0)
    back_weight(0)
    start_near(1)
    back_through(0)
    v_far()

    z0 = inner[...]
    e0 = jnp.exp(jnp.minimum(z0, 0.0))
    slope0 = jnp.where(z0 > 0, 1.0, e0)
    curve0 = jnp.where(z0 > 0, 0.0, e0)
    first_rows = [small_row(j) for j in range(6)]
    g_inner = grad[0] * slope0 + curve0 * (
        grad[1] * first_rows[3] + grad[2] * first_rows[4] + grad[3] * first_rows[5]
    )
    rows = [jnp.sum(xs[j] * g_inner, axis=0, keepdims=True) for j in range(6)]
    for k in range(3):
        rows[3 + k] = rows[3 + k] + jnp.sum(grad[1 + k] * slope0, axis=0, keepdims=True)
    rows.append(jnp.sum(g_inner, axis=0, keepdims=True))
    rows = rows + bias_in + bias_out + [g_out_row]

    lanes = lax.broadcasted_iota(jnp.int32, (1, cw), 1)
    weight_sq = jnp.zeros((1, cw), F32)
    for m in range(MATS):
        part = jnp.sum(master[m // 2, m % 2] * master[m // 2, m % 2], keepdims=True)
        weight_sq = jnp.where(lanes == m, part, weight_sq)
    own_small = spbuf[t]
    weight_sq = jnp.where(lanes == MATS, jnp.sum(own_small * own_small, keepdims=True) / (A * B), weight_sq)
    tail = [
        jnp.broadcast_to(total_err, (1, cw)),
        weight_sq,
        jnp.zeros((2, cw), F32),
    ]
    for tt in range(n_t):
        sgsend[tt % 2, tt // 2] = jnp.concatenate([r[:, tt * cw : (tt + 1) * cw] for r in rows] + tail, 0)
    sgslot_g[me_near] = sgsend[c, y]
    for (o, cc), d in zip(q_coords, q_devices):
        remote(sgsend.at[cc, o // B], sgslot_g.at[me_near], s_send.at[S_NEAR], s_recv.at[S_NEAR], d)
    start_near(0)

    for copy in local[7:]:
        copy.wait()
    tile_rows = lax.broadcasted_iota(jnp.int32, (8, 128), 0)

    def step(gradient, momentum):
        new = momentum_coef * momentum + gradient
        return new, gradient + momentum_coef * new

    def settle(m, total):
        at = (m // 2, m % 2)
        gr = total / counted
        new, direction = step(gr, moment[at])
        grad_b[at] = gr
        moment_b[at] = new
        return jnp.where(tile_rows == m, jnp.sum(direction * direction, keepdims=True), 0.0)

    start_far(2)
    start_turned(2)
    start_far(1)
    start_turned(1)

    await_bytes(vslot_z.at[fars], s_recv.at[S_VFAR])
    v_part = slot_sum(vslot_z, A)[0:1]
    product = jnp.sum(last_low * v_part, axis=1, keepdims=True)
    place = lax.broadcasted_iota(jnp.int32, (R, cw), 1) - lax.broadcasted_iota(jnp.int32, (R, cw), 0)
    product_row = jnp.sum(jnp.where(place == (dp * R) % cw, product, 0.0), axis=0, keepdims=True)
    psend[...] = jnp.broadcast_to(product_row, (8, cw))
    column = (dp * R) // cw
    mine_too = column == t
    slot = (dp % (cw // R)) * n_t + t
    pl.semaphore_wait(barrier, len(others))
    for k in range(1, A * B):
        remote(
            psend, pslot.at[slot], s_send.at[S_PROD], s_recv.at[S_PROD], (partner(dp, k, A * B), column)
        )

    @pl.when(mine_too)
    def _():
        pslot[slot] = psend[...]

    @pl.when(jnp.logical_not(mine_too))
    def _():
        remote(psend, pslot.at[slot], s_send.at[S_PROD], s_recv.at[S_PROD], (dp, column))

    def await_products(wait, ref, count_of, sems):
        @pl.when(mine_too)
        def _():
            wait(ref.at[pl.ds(0, count_of - 1)], sems.at[S_PROD])

        @pl.when(jnp.logical_not(mine_too))
        def _():
            wait(ref.at[pl.ds(0, count_of)], sems.at[S_PROD])

    start_far(0)
    start_turned(0)
    await_bytes(sgslot_g.at[pl.ds(0, 2 * G - 1)], s_recv.at[S_NEAR])
    sgtwo[...] = slot_sum(sgslot_g, 2 * G)
    sgslot_z[a] = sgtwo[...]
    for d in z_devices:
        remote(sgtwo, sgslot_z.at[a], s_send.at[S_FAR], s_recv.at[S_FAR], d)

    parts = settle(MATS - 1, out_column * v_part)
    for m in (2, 1, 0):
        parts = parts + settle(m, finish(m))
    slots = (cw // R) * n_t
    await_products(await_bytes, pslot, slots, s_recv)
    await_bytes(sgslot_z.at[fars], s_recv.at[S_FAR])
    sred[...] = slot_sum(sgslot_z, A)
    head_row = sred[SMALL - 1 : SMALL]
    for i in range(slots):
        head_row = head_row + pslot[i, 0:1]
    sred[SMALL - 1 : SMALL] = head_row
    gr = sred[0:SMALL, :] / counted
    new, dir_small = step(gr, msmall[...])
    grad_s[...] = gr
    moment_s[...] = new
    parts = parts + jnp.where(
        tile_rows == MATS, jnp.sum(dir_small * dir_small, keepdims=True) / (A * B), 0.0
    )
    me = (a * G + g) * 2 + c
    arslot[me] = parts
    for d in everyone:
        remote(arslot.at[me], arslot.at[me], s_send.at[S_ALL], s_recv.at[S_ALL], d)
    loss_b[...] = sred[SMALL : SMALL + 1, 0:1] / counted
    bias_b[...] = grad_s[7 : 7 + 2 * LAYERS, :]
    await_bytes(arslot.at[pl.ds(0, len(everyone))], s_recv.at[S_ALL])
    dir_sq = jnp.sum(arslot[...], axis=0)

    def rate_of(m):
        size = sred[SMALL + 1 : SMALL + 2, m : m + 1]
        return spread_rate * jnp.sqrt(size) / jnp.sqrt(dir_sq[m : m + 1, 0:1] + norm_epsilon)

    for m in range(MATS):
        at = (m // 2, m % 2)
        direction = grad_b[at] + momentum_coef * moment_b[at]
        new = master[at] - rate_of(m) * direction
        master_b[at] = new
        average_b[at] = average_decay * average[at] + (1.0 - average_decay) * new
        low_b[at] = new.astype(BF16)
    new = own_small - rate_of(MATS) * dir_small
    master_s[...] = new
    average_s[...] = average_decay * asmall[...] + (1.0 - average_decay) * new

    n_w, n_g = len(w_turned), len(g_turned)
    gathered = MOVED * (A - 1 + G - 1 + A * G) + (A - 1) * (MOVED * (G - 1) - n_w) + n_w * (A - 1)
    scattered = MOVED * (A - 1 + A * G) + A * (MOVED * (G - 1) - n_g) + n_g * A
    await_sent(sized.at[pl.ds(0, gathered)], w_send.at[0])
    await_sent(sized.at[pl.ds(0, scattered)], g_send.at[0])
    await_sent(qslot_z.at[fars], s_send.at[S_QFAR])
    await_sent(vslot_z.at[fars], s_send.at[S_VFAR])
    await_sent(qslot_g.at[pl.ds(0, 2 * G - 1)], s_send.at[S_QNEAR])
    await_sent(vslot_g.at[pl.ds(0, 2 * G - 1)], s_send.at[S_VNEAR])
    await_sent(sgslot_g.at[pl.ds(0, 2 * G - 1)], s_send.at[S_NEAR])
    await_products(await_sent, pdone, A * B, s_send)
    await_sent(sgslot_z.at[fars], s_send.at[S_FAR])
    await_sent(arslot.at[pl.ds(0, len(everyone))], s_send.at[S_ALL])
    await_sent(spbuf.at[pl.ds(0, n_t - 1)], s_send.at[S_PAR])


def write_out(*refs):
    sems = refs[-1]
    count = (len(refs) - 1) // 2
    copies = [
        pltpu.make_async_copy(refs[i], refs[count + i], sems.at[i]) for i in range(count)
    ]
    for copy in copies:
        copy.start()
    for copy in copies:
        copy.wait()


def body(
    axes,
    coords,
    model_ids,
    cells,
    valid,
    slowness_grid,
    master_blocks,
    small_params,
    moment_blocks,
    moment_small,
    average_blocks,
    average_small,
):
    n_dp, n_t = axes
    A = 4 if n_dp % 4 == 0 else n_dp
    B = n_dp // A
    C = n_t // 2
    G = C * B
    R, cw = master_blocks.shape[2:]
    D = R * n_dp
    PB = coords.shape[1]
    Pn = PB // n_t
    dims = (A, B, C, R, cw, Pn, D)
    anywhere = pl.BlockSpec(memory_space=pltpu.HBM)
    vmem = pl.BlockSpec(memory_space=pltpu.VMEM)
    S = SMALL + 4
    args = (
        coords,
        model_ids,
        cells,
        valid,
        slowness_grid,
        master_blocks,
        small_params,
        moment_blocks,
        moment_small,
        average_blocks,
        average_small,
    )
    V = pltpu.VMEM
    DMA = pltpu.SemaphoreType.DMA
    block = (master_blocks.shape, F32)
    short = (small_params.shape, F32)
    shapes = [
        ((1, 1), F32),
        block,
        short,
        ((2 * LAYERS, cw), F32),
        block,
        short,
        block,
        short,
        block,
        short,
        (master_blocks.shape, BF16),
    ]
    results = pl.pallas_call(
        functools.partial(kernel, dims),
        out_shape=tuple(V(*shape) for shape in shapes),
        in_specs=[anywhere] * len(args),
        out_specs=(vmem,) * len(shapes),
        scratch_shapes=[
            V(coords.shape, F32),
            V((PB,), jnp.int32),
            V((PB,), jnp.int32),
            V((PB,), jnp.int32),
            V(slowness_grid.shape, F32),
            V(master_blocks.shape, F32),
            V(master_blocks.shape, F32),
            V(small_params.shape, F32),
            V(master_blocks.shape, F32),
            V(small_params.shape, F32),
            V((n_t, SMALL, cw), F32),
            V((PB, 128), F32),
            V((S, cw), F32),
            V((MOVED, 2, C, A, B, R, cw), BF16),
            V((4, Pn, D), F32),
            V((LAYERS, 4, Pn, D), BF16),
            V((LAYERS, 4, Pn, D), F32),
            V((LAYERS, 4, Pn, D), BF16),
            V((4, Pn, D), F32),
            V((4, Pn, D), BF16),
            V((4, Pn, D), BF16),
            V((Pn, D), F32),
            V((MOVED, 2, A, G, R, cw), BF16),
            V((MOVED, A, G, R, cw), BF16),
            V((MOVED, A, G, R, cw), BF16),
            V((MOVED, A, G - 1, R, cw), BF16),
            V((MOVED, A - 1, R, cw), BF16),
            V((MOVED, A - 1, R, cw), BF16),
            V((MOVED, R, cw), F32),
            V((MOVED, A - 1, R, cw), BF16),
            V((MOVED, R, cw), BF16),
            V((MOVED, R, cw), BF16),
            V((2, C, S, cw), F32),
            V((8, cw), F32),
            V(((cw // R) * n_t, 8, cw), F32),
            V((n_dp, 8, cw), F32),
            V((MOVED * A * (2 * G + 1), R, cw), BF16),
            V((2 * G, S, cw), F32),
            V((S, cw), F32),
            V((A, S, cw), F32),
            V((2 * A * G, 8, 128), F32),
            V((A, 8, cw), F32),
            V((2 * G, 8, cw), F32),
            V((2, C, 8, cw), F32),
            V((2 * G, 8, cw), F32),
            V((A, 8, cw), F32),
            pltpu.SemaphoreType.DMA((len(args),)),
            DMA((1,)),
            DMA((MOVED, A - 1)),
            DMA((MOVED, G - 1)),
            DMA((MOVED,)),
            DMA((MOVED,)),
            DMA((1,)),
            DMA((MOVED,)),
            DMA((MOVED, A)),
            DMA((MOVED, 2)),
            DMA((MOVED,)),
            DMA((9,)),
            DMA((9,)),
        ],
        compiler_params=pltpu.CompilerParams(
            collective_id=0, has_side_effects=True, vmem_limit_bytes=60 << 20
        ),
    )(*args)

    results = pl.pallas_call(
        write_out,
        out_shape=tuple(jax.ShapeDtypeStruct(*shape) for shape in shapes),
        in_specs=[vmem] * len(shapes),
        out_specs=(anywhere,) * len(shapes),
        scratch_shapes=[pltpu.SemaphoreType.DMA((len(shapes),))],
        compiler_params=pltpu.CompilerParams(vmem_limit_bytes=4 << 20),
    )(*results)
    return (results[0].reshape(()),) + tuple(results[1:])


def solution(mesh):
    blocks = P(None, None, "dp", "tensor")
    small = P(None, "tensor")
    in_specs = (
        P(None, "dp"),
        P("dp"),
        P("dp"),
        P("dp"),
        P(),
        blocks,
        small,
        blocks,
        small,
        blocks,
        small,
    )
    out_specs = (P(), blocks, small, small, blocks, small, blocks, small, blocks, small, blocks)
    axes = (mesh.shape["dp"], mesh.shape["tensor"])
    return jax.shard_map(
        functools.partial(body, axes), mesh=mesh, in_specs=in_specs, out_specs=out_specs, check_vma=False
    )
```

```python
import functools

import jax
import jax.numpy as jnp
from jax import lax
from jax.experimental import pallas as pl
from jax.experimental.pallas import tpu as pltpu
from jax.sharding import PartitionSpec as P

LAYERS = 2
MATS = 2 * LAYERS
SMALL = 12
MESH = pl.DeviceIdType.MESH
F32 = jnp.float32
BF16 = jnp.bfloat16

momentum_coef = 0.5
average_decay = 0.5
spread_rate = 0.5
norm_epsilon = 1e-12

MOVED = MATS - 1
W_TURNED = (0, 1)
G_TURNED = (2, 1, 0)


def partner(i, k, size):
    bit = 1
    while bit < size:
        if (k // bit) % 2:
            i = i + bit - 2 * bit * ((i // bit) % 2)
        bit *= 2
    return i


def nn(left, right):
    return lax.dot_general(left, right, (((1,), (0,)), ((), ())), preferred_element_type=F32)


def nt(left, right):
    return lax.dot_general(left, right, (((1,), (1,)), ((), ())), preferred_element_type=F32)


def tn(left, right):
    return lax.dot_general(left, right, (((0,), (0,)), ((), ())), preferred_element_type=F32)


def sign_of(v):
    return jnp.where(v > 0, 1.0, jnp.where(v < 0, -1.0, 0.0))


def kernel(
    dims,
    coords_hbm,
    model_hbm,
    cells_hbm,
    valid_hbm,
    grid_hbm,
    master_hbm,
    small_hbm,
    moment_hbm,
    msmall_hbm,
    average_hbm,
    asmall_hbm,
    loss_b,
    grad_b,
    grad_s,
    bias_b,
    moment_b,
    moment_s,
    master_b,
    master_s,
    average_b,
    average_s,
    low_b,
    coords,
    model,
    cells,
    valid,
    grid,
    master,
    moment,
    msmall,
    average,
    asmall,
    spbuf,
    columns,
    sred,
    wbuf,
    streams,
    acts,
    pre,
    hidden,
    grad,
    gbranch,
    gpre,
    inner,
    gsend,
    gcore,
    gone,
    gslot_n,
    gtwo,
    gslot_z,
    gown,
    tslot_z,
    tlow,
    tslot_n,
    sgsend,
    psend,
    pslot,
    pdone,
    sized,
    sgslot_g,
    sgtwo,
    sgslot_z,
    arslot,
    qslot_z,
    qslot_g,
    vsend,
    vslot_g,
    vslot_z,
    in_sem,
    w_send,
    wz_recv,
    wn_recv,
    wt_recv,
    wc_recv,
    g_send,
    gz_recv,
    gn_recv,
    gt_recv,
    gc_recv,
    s_send,
    s_recv,
):
    A, B, C, R, cw, Pn, D = dims
    n_t = 2 * C
    G = C * B
    dp = lax.axis_index("dp")
    t = lax.axis_index("tensor")
    a, b = dp // B, dp % B
    y, c = t // 2, t % 2
    g = y * B + b

    def device(a_, g_, c_):
        return (a_ * B + g_ % B, (g_ // B) * 2 + c_)

    far = [partner(a, k, A) for k in range(1, A)]
    near = [partner(g, k, G) for k in range(1, G)]
    z_devices = [device(o, g, c) for o in far]
    g_devices = [device(a, o, c) for o in near]
    core_device = device(a, g, 1 - c)
    q_steps = [(kg, kc) for kg in range(G) for kc in range(2)][1:]
    q_steps.sort(key=lambda step: -(bin(step[0]).count("1") + step[1] / 2))
    q_coords = [(partner(g, kg, G), partner(c, kc, 2)) for kg, kc in q_steps]
    q_devices = [device(a, o, cc) for o, cc in q_coords]
    steps = [(ka, kg, kc) for ka in range(A) for kg in range(G) for kc in range(2)][1:]
    steps.sort(key=lambda step: -(step[0] + bin(step[1]).count("1") + step[2] / 2))
    everyone = [device(partner(a, ka, A), partner(g, kg, G), partner(c, kc, 2)) for ka, kg, kc in steps]
    others = [d for d, step in zip(everyone, steps) if step[0] and (step[1] or step[2])]

    FARTHEST = G - 2
    w_turned = W_TURNED if G > 2 else ()
    g_turned = G_TURNED if G > 2 else ()

    def plain_near(m, turned):
        return range(G - 2 if m in turned else G - 1)

    S_PROD, S_NEAR, S_FAR, S_ALL, S_PAR, S_QFAR, S_QNEAR, S_VNEAR, S_VFAR = range(9)

    def remote(src, dst, ssem, rsem, device_id):
        copy = pltpu.make_async_remote_copy(
            src_ref=src,
            dst_ref=dst,
            send_sem=ssem,
            recv_sem=rsem,
            device_id=device_id,
            device_id_type=MESH,
        )
        copy.start()
        return copy

    def arrived(copies):
        for copy in copies:
            copy.wait_recv()

    nears, fars = pl.ds(0, G - 1), pl.ds(0, A - 1)

    local = []
    for i, (src, dst) in enumerate(
        [
            (master_hbm, master),
            (small_hbm, spbuf.at[t]),
            (coords_hbm, coords),
            (model_hbm, model),
            (cells_hbm, cells),
            (valid_hbm, valid),
            (grid_hbm, grid),
            (moment_hbm, moment),
            (msmall_hbm, msmall),
            (average_hbm, average),
            (asmall_hbm, asmall),
        ]
    ):
        copy = pltpu.make_async_copy(src, dst, in_sem.at[i])
        copy.start()
        local.append(copy)

    barrier = pltpu.get_barrier_semaphore()
    peers = z_devices + q_devices
    for d in peers:
        pl.semaphore_signal(barrier, inc=1, device_id=d, device_id_type=MESH)

    local[0].wait()
    for m in range(MOVED):
        wbuf[m, c, y, a, b] = master[m // 2, m % 2].astype(BF16)
    local[1].wait()
    pl.semaphore_wait(barrier, len(peers))

    def piece(m, o, z):
        return wbuf.at[m, c, o // B, z, o % B]

    def line(m, o):
        return wbuf.at[m, c, o // B, :, o % B]

    def plane(m, z):
        return wbuf.at[m, c, :, z]

    def await_bytes(ref, rsem):
        pltpu.make_async_remote_copy(
            src_ref=ref,
            dst_ref=ref,
            send_sem=s_send.at[0],
            recv_sem=rsem,
            device_id=core_device,
            device_id_type=MESH,
        ).wait_recv()

    def slot_sum(ref, count_of, value=None):
        for i in range(count_of):
            term = ref[i].astype(F32)
            value = term if value is None else value + term
        return value

    def await_sent(ref, ssem):
        pltpu.make_async_remote_copy(
            src_ref=ref,
            dst_ref=ref,
            send_sem=ssem,
            recv_sem=s_recv.at[0],
            device_id=core_device,
            device_id_type=MESH,
        ).wait_send()

    def w_far(m, ref):
        return [
            remote(ref, ref, w_send.at[0], wz_recv.at[m, k], z_devices[k]) for k in reversed(range(A - 1))
        ][::-1]

    def w_near(m, ref, ks):
        for k in ks:
            remote(ref, ref, w_send.at[0], wn_recv.at[m, k], g_devices[k])

    def w_core(m, ref):
        remote(ref, ref, w_send.at[0], wc_recv.at[m], core_device)

    for k in range(1, n_t):
        o = (t + k) % n_t
        remote(spbuf.at[t], spbuf.at[t], s_send.at[S_PAR], s_recv.at[S_PAR], (dp, o))
    first = {}
    for m in range(MOVED):
        first[m] = w_far(m, piece(m, g, a))
        w_near(m, piece(m, g, a), reversed(range(G - 1)))

    for copy in local[2:7]:
        copy.wait()
    cols = grid.shape[2]
    shift = (cols - 1).bit_length()
    cell = cells[...].reshape(1, -1)
    row_id = model[...].reshape(1, -1) * grid.shape[1] + (cell >> shift)
    col_id = cell & (cols - 1)
    PB = row_id.shape[1]
    packed = jnp.concatenate(
        [
            coords[...],
            row_id.astype(F32),
            col_id.astype(F32),
            valid[...].reshape(1, -1).astype(F32),
            jnp.zeros((128 - 9, PB), F32),
        ],
        0,
    )
    columns[...] = packed.T
    mine = columns[pl.ds(pl.multiple_of(t * Pn, 8), Pn), :]
    xs = [mine[:, j : j + 1] for j in range(6)]
    mask = mine[:, 8:9]
    row_of = mine[:, 6:7].astype(jnp.int32)
    col_of = mine[:, 7:8].astype(jnp.int32)
    table = grid[...].reshape(-1, cols)
    onehot = (
        lax.broadcasted_iota(jnp.int32, (Pn, table.shape[0]), 1) == row_of
    ).astype(BF16)
    high = table.astype(BF16)
    rest = table - high.astype(F32)
    middle = rest.astype(BF16)
    lowest = (rest - middle.astype(F32)).astype(BF16)
    picked = nn(onehot, high) + nn(onehot, middle) + nn(onehot, lowest)
    lane = lax.broadcasted_iota(jnp.int32, (Pn, cols), 1)
    truth = jnp.sum(jnp.where(lane == col_of, picked, 0.0), 1, keepdims=True)
    seps = [xs[3 + k] - xs[k] for k in range(3)]
    distance = jnp.sqrt(seps[0] * seps[0] + seps[1] * seps[1] + seps[2] * seps[2])
    units = [s / distance for s in seps]

    await_bytes(spbuf.at[pl.ds(0, n_t - 1)], s_recv.at[S_PAR])

    def small_row(i):
        return jnp.concatenate([spbuf[tt, i : i + 1, :] for tt in range(n_t)], 1)

    out_row = small_row(7 + 2 * LAYERS)
    last_low = master[LAYERS - 1, 1].astype(BF16).astype(F32)
    feature = lax.broadcasted_iota(jnp.int32, (R, D), 1) - lax.broadcasted_iota(jnp.int32, (R, D), 0)
    out_column = jnp.sum(jnp.where(feature == dp * R, out_row, 0.0), axis=1, keepdims=True)
    q_part = jnp.sum(last_low * out_column, axis=0, keepdims=True)
    count = jnp.sum(mask, axis=0, keepdims=True)
    row_of_8 = lax.broadcasted_iota(jnp.int32, (8, cw), 0)
    qslot_z[a] = jnp.where(row_of_8 == 0, q_part, count)
    for d in reversed(z_devices):
        remote(qslot_z.at[a], qslot_z.at[a], s_send.at[S_QFAR], s_recv.at[S_QFAR], d)

    first_rows = [small_row(j) for j in range(6)]
    z0 = small_row(6) + xs[0] * first_rows[0]
    for j in range(1, 6):
        z0 = z0 + xs[j] * first_rows[j]
    inner[...] = z0
    e0 = jnp.exp(jnp.minimum(z0, 0.0))
    slope0 = jnp.where(z0 > 0, 1.0, e0)
    streams[0] = jnp.where(z0 > 0, z0, e0 - 1.0)
    acts[0, 0] = streams[0].astype(BF16)
    for k in range(3):
        streams[1 + k] = slope0 * first_rows[3 + k]
        acts[0, 1 + k] = streams[1 + k].astype(BF16)

    def pass_on(m):
        for k in range(A - 1):
            first[m][k].wait_recv()
            w_near(m, piece(m, g, far[k]), plain_near(m, w_turned))
        w_core(m, line(m, g))
        if m in w_turned:
            o = near[FARTHEST]
            ref = piece(m, o, a)
            await_bytes(ref, wn_recv.at[m, FARTHEST])
            for d in reversed(z_devices):
                remote(ref, ref, w_send.at[0], wt_recv.at[m], d)

    for m in range(MOVED):
        pass_on(m)
    me_near = g * 2 + c
    await_bytes(qslot_z.at[fars], s_recv.at[S_QFAR])
    qslot_g[me_near] = slot_sum(qslot_z, A)
    for d in q_devices:
        remote(qslot_g.at[me_near], qslot_g.at[me_near], s_send.at[S_QNEAR], s_recv.at[S_QNEAR], d)

    def weight(m):
        return jnp.concatenate([wbuf[m, tt % 2, tt // 2].reshape(D, cw) for tt in range(n_t)], 1)

    M = 4 * Pn

    def block_in(l):
        pre[l] = nn(acts[l].reshape(M, D), weight(2 * l)).reshape(4, Pn, D)
        z = pre[l, 0] + small_row(7 + l)
        e = jnp.exp(jnp.minimum(z, 0.0))
        slope = jnp.where(z > 0, 1.0, e)
        hidden[l, 0] = jnp.where(z > 0, z, e - 1.0).astype(BF16)
        for k in range(1, 4):
            hidden[l, k] = (slope * pre[l, k]).astype(BF16)

    def block_out(l):
        branch = nt(hidden[l].reshape(M, D), weight(2 * l + 1)).reshape(4, Pn, D)
        for s in range(4):
            new = streams[s] + branch[s]
            if s == 0:
                new = new + small_row(7 + LAYERS + l)
            streams[s] = new
            if l + 1 < LAYERS:
                acts[l + 1, s] = new.astype(BF16)

    def fetch(m):
        for k in range(G - 1):
            if m in w_turned and k == FARTHEST:
                await_bytes(wbuf.at[m, c, 0, fars, 0], wt_recv.at[m])
            else:
                await_bytes(line(m, near[k]), wn_recv.at[m, k])
            w_core(m, line(m, near[k]))

    def fetched(m):
        await_bytes(wbuf.at[m, c], wc_recv.at[m])

    for m in range(MOVED):
        fetch(m)
        fetched(m)
        if m == 0:
            for d in others:
                pl.semaphore_signal(barrier, inc=1, device_id=d, device_id_type=MESH)
        if m % 2 == 0:
            block_in(m // 2)
        else:
            block_out(m // 2)
        if m == MOVED - 2:
            proj_a = [jnp.sum(streams[s] * out_row, axis=1, keepdims=True) for s in range(4)]
            bias_row = small_row(6 + 2 * LAYERS)
            proj_a[0] = proj_a[0] + jnp.sum(bias_row * out_row, axis=1, keepdims=True)
            await_bytes(qslot_g.at[pl.ds(0, 2 * G - 1)], s_recv.at[S_QNEAR])
            q_row = []
            for tt in range(n_t):
                total = qslot_g[(tt // 2) * B * 2 + tt % 2, 0:1]
                for i in range(1, B):
                    total = total + qslot_g[((tt // 2) * B + i) * 2 + tt % 2, 0:1]
                q_row.append(total)
            q_row = jnp.concatenate(q_row, 1)
            counted = slot_sum(qslot_g, 2 * G)[1:2, 0:1]

    last = LAYERS - 1
    proj = [
        proj_a[s] + jnp.sum(hidden[last, s].astype(F32) * q_row, axis=1, keepdims=True) for s in range(4)
    ]
    tau = proj[0]
    sign_tau = sign_of(tau)
    abs_tau = jnp.abs(tau)
    grad_time = [units[k] * abs_tau + distance * sign_tau * proj[1 + k] for k in range(3)]
    square = grad_time[0] * grad_time[0] + grad_time[1] * grad_time[1] + grad_time[2] * grad_time[2]
    error = square - truth * truth
    total_err = jnp.sum(mask * jnp.abs(error), axis=0, keepdims=True)
    seed = mask * sign_of(error)
    g_time = [2.0 * grad_time[k] * seed for k in range(3)]
    g_tau = sign_tau * (units[0] * g_time[0] + units[1] * g_time[1] + units[2] * g_time[2])
    g_proj = [g_tau] + [distance * sign_tau * g_time[k] for k in range(3)]
    v_row = jnp.sum(
        sum(hidden[last, s].astype(F32) * g_proj[s] for s in range(4)), axis=0, keepdims=True
    )
    for tt in range(n_t):
        vsend[tt % 2, tt // 2] = jnp.broadcast_to(v_row[:, tt * cw : (tt + 1) * cw], (8, cw))
    vslot_g[me_near] = vsend[c, y]
    for (o, cc), d in zip(q_coords, q_devices):
        remote(vsend.at[cc, o // B], vslot_g.at[me_near], s_send.at[S_VNEAR], s_recv.at[S_VNEAR], d)

    def v_far():
        await_bytes(vslot_g.at[pl.ds(0, 2 * G - 1)], s_recv.at[S_VNEAR])
        vslot_z[a] = slot_sum(vslot_g, 2 * G)
        for d in reversed(z_devices):
            remote(vslot_z.at[a], vslot_z.at[a], s_send.at[S_VFAR], s_recv.at[S_VFAR], d)

    pieces = [(far[k], k) for k in reversed(range(A - 1))] + [(a, None)]

    def start_core(m, value):
        low = value.astype(BF16)
        for tt in range(n_t):
            block = low[:, tt * cw : (tt + 1) * cw].reshape(A, B, R, cw)
            for i in range(B):
                gsend[m, tt % 2, :, (tt // 2) * B + i] = block[:, i]
        for z, _ in pieces:
            remote(gsend.at[m, 1 - c, z], gcore.at[m, z], g_send.at[0], gc_recv.at[m], core_device)

    def core_sum(m, j):
        z = pieces[j][0]
        gone[m, z] = (gsend[m, c, z].astype(F32) + gcore[m, z].astype(F32)).astype(BF16)

    def start_near(m):
        await_bytes(gcore.at[m], gc_recv.at[m])
        for j, (z, kz) in enumerate(pieces):
            core_sum(m, j)
            for k in plain_near(m, g_turned):
                remote(
                    gone.at[m, z, near[k]],
                    gslot_n.at[m, j, k],
                    g_send.at[0],
                    gn_recv.at[m, j],
                    g_devices[k],
                )
            if m in g_turned and kz is not None:
                remote(
                    gone.at[m, z, near[FARTHEST]],
                    tslot_z.at[m, kz],
                    g_send.at[0],
                    gt_recv.at[m, 0],
                    z_devices[kz],
                )

    def start_far(m):
        count_of = len(plain_near(m, g_turned))
        for j, (z, k) in enumerate(pieces):
            if count_of:
                await_bytes(gslot_n.at[m, j, pl.ds(0, count_of)], gn_recv.at[m, j])
            total = slot_sum(gslot_n.at[m, j], count_of, gone[m, z, g].astype(F32))
            if k is None:
                gown[m] = total
            else:
                gtwo[m, k] = total.astype(BF16)
                remote(gtwo.at[m, k], gslot_z.at[m, k], g_send.at[0], gz_recv.at[m], z_devices[k])

    def start_turned(m):
        if m in g_turned:
            await_bytes(tslot_z.at[m], gt_recv.at[m, 0])
            total = slot_sum(tslot_z.at[m], A - 1, gone[m, a, near[FARTHEST]].astype(F32))
            tlow[m] = total.astype(BF16)
            remote(tlow.at[m], tslot_n.at[m], g_send.at[0], gt_recv.at[m, 1], g_devices[FARTHEST])

    def finish(m):
        await_bytes(gslot_z.at[m], gz_recv.at[m])
        total = slot_sum(gslot_z.at[m], A - 1, gown[m])
        if m in g_turned:
            await_bytes(tslot_n.at[m], gt_recv.at[m, 1])
            total = total + tslot_n[m].astype(F32)
        return total

    bias_in = [None] * LAYERS
    bias_out = [None] * LAYERS

    def back_last():
        z = pre[last, 0] + small_row(7 + last)
        e = jnp.exp(jnp.minimum(z, 0.0))
        slope = jnp.where(z > 0, 1.0, e)
        curve = jnp.where(z > 0, 0.0, e)
        mixed = g_proj[1] * pre[last, 1] + g_proj[2] * pre[last, 2] + g_proj[3] * pre[last, 3]
        gz = q_row * (g_proj[0] * slope + curve * mixed)
        bias_in[last] = jnp.sum(gz, axis=0, keepdims=True)
        gpre[0] = gz.astype(BF16)
        slope = slope * q_row
        for k in range(1, 4):
            gpre[k] = (g_proj[k] * slope).astype(BF16)

    def back_out(l):
        bias_out[l] = jnp.sum(grad[0], axis=0, keepdims=True)
        gb = gbranch[...].reshape(M, D)
        start_core(2 * l + 1, tn(gb, hidden[l].reshape(M, D)))

    def back_in(l):
        gb = gbranch[...].reshape(M, D)
        gh = nn(gb, weight(2 * l + 1)).reshape(4, Pn, D)
        z = pre[l, 0] + small_row(7 + l)
        e = jnp.exp(jnp.minimum(z, 0.0))
        slope = jnp.where(z > 0, 1.0, e)
        curve = jnp.where(z > 0, 0.0, e)
        gz = gh[0] * slope + curve * (gh[1] * pre[l, 1] + gh[2] * pre[l, 2] + gh[3] * pre[l, 3])
        bias_in[l] = jnp.sum(gz, axis=0, keepdims=True)
        gpre[0] = gz.astype(BF16)
        for k in range(1, 4):
            gpre[k] = (gh[k] * slope).astype(BF16)

    def back_weight(l):
        start_core(2 * l, tn(acts[l].reshape(M, D), gpre[...].reshape(M, D)))

    def back_through(l):
        back = nt(gpre[...].reshape(M, D), weight(2 * l)).reshape(4, Pn, D)
        for s in range(4):
            value = (out_row * g_proj[s] if l == last else grad[s]) + back[s]
            grad[s] = value
            if l > 0:
                gbranch[s] = value.astype(BF16)

    back_last()
    back_weight(1)
    tau_sum = jnp.sum(g_proj[0], axis=0, keepdims=True)
    bias_out[last] = out_row * tau_sum
    g_out_row = bias_row * tau_sum + jnp.sum(
        streams[0] * g_proj[0] + streams[1] * g_proj[1] + streams[2] * g_proj[2] + streams[3] * g_proj[3],
        axis=0,
        keepdims=True,
    )
    back_through(1)
    back_out(0)
    start_near(2)
    back_in(0)
    back_weight(0)
    start_near(1)
    back_through(0)
    v_far()

    z0 = inner[...]
    e0 = jnp.exp(jnp.minimum(z0, 0.0))
    slope0 = jnp.where(z0 > 0, 1.0, e0)
    curve0 = jnp.where(z0 > 0, 0.0, e0)
    first_rows = [small_row(j) for j in range(6)]
    g_inner = grad[0] * slope0 + curve0 * (
        grad[1] * first_rows[3] + grad[2] * first_rows[4] + grad[3] * first_rows[5]
    )
    rows = [jnp.sum(xs[j] * g_inner, axis=0, keepdims=True) for j in range(6)]
    for k in range(3):
        rows[3 + k] = rows[3 + k] + jnp.sum(grad[1 + k] * slope0, axis=0, keepdims=True)
    rows.append(jnp.sum(g_inner, axis=0, keepdims=True))
    rows = rows + bias_in + bias_out + [g_out_row]

    lanes = lax.broadcasted_iota(jnp.int32, (1, cw), 1)
    weight_sq = jnp.zeros((1, cw), F32)
    for m in range(MATS):
        part = jnp.sum(master[m // 2, m % 2] * master[m // 2, m % 2], keepdims=True)
        weight_sq = jnp.where(lanes == m, part, weight_sq)
    own_small = spbuf[t]
    weight_sq = jnp.where(lanes == MATS, jnp.sum(own_small * own_small, keepdims=True) / (A * B), weight_sq)
    tail = [
        jnp.broadcast_to(total_err, (1, cw)),
        weight_sq,
        jnp.zeros((2, cw), F32),
    ]
    for tt in range(n_t):
        sgsend[tt % 2, tt // 2] = jnp.concatenate([r[:, tt * cw : (tt + 1) * cw] for r in rows] + tail, 0)
    sgslot_g[me_near] = sgsend[c, y]
    for (o, cc), d in zip(q_coords, q_devices):
        remote(sgsend.at[cc, o // B], sgslot_g.at[me_near], s_send.at[S_NEAR], s_recv.at[S_NEAR], d)
    start_near(0)

    for copy in local[7:]:
        copy.wait()
    tile_rows = lax.broadcasted_iota(jnp.int32, (8, 128), 0)

    def step(gradient, momentum):
        new = momentum_coef * momentum + gradient
        return new, gradient + momentum_coef * new

    def settle(m, total):
        at = (m // 2, m % 2)
        gr = total / counted
        new, direction = step(gr, moment[at])
        grad_b[at] = gr
        moment_b[at] = new
        return jnp.where(tile_rows == m, jnp.sum(direction * direction, keepdims=True), 0.0)

    start_far(2)
    start_turned(2)
    start_far(1)
    start_turned(1)

    await_bytes(vslot_z.at[fars], s_recv.at[S_VFAR])
    v_part = slot_sum(vslot_z, A)[0:1]
    product = jnp.sum(last_low * v_part, axis=1, keepdims=True)
    place = lax.broadcasted_iota(jnp.int32, (R, cw), 1) - lax.broadcasted_iota(jnp.int32, (R, cw), 0)
    product_row = jnp.sum(jnp.where(place == (dp * R) % cw, product, 0.0), axis=0, keepdims=True)
    psend[...] = jnp.broadcast_to(product_row, (8, cw))
    column = (dp * R) // cw
    mine_too = column == t
    slot = (dp % (cw // R)) * n_t + t
    pl.semaphore_wait(barrier, len(others))
    for k in reversed(range(1, A * B)):
        remote(
            psend, pslot.at[slot], s_send.at[S_PROD], s_recv.at[S_PROD], (partner(dp, k, A * B), column)
        )

    @pl.when(mine_too)
    def _():
        pslot[slot] = psend[...]

    @pl.when(jnp.logical_not(mine_too))
    def _():
        remote(psend, pslot.at[slot], s_send.at[S_PROD], s_recv.at[S_PROD], (dp, column))

    def await_products(wait, ref, count_of, sems):
        @pl.when(mine_too)
        def _():
            wait(ref.at[pl.ds(0, count_of - 1)], sems.at[S_PROD])

        @pl.when(jnp.logical_not(mine_too))
        def _():
            wait(ref.at[pl.ds(0, count_of)], sems.at[S_PROD])

    start_far(0)
    start_turned(0)
    await_bytes(sgslot_g.at[pl.ds(0, 2 * G - 1)], s_recv.at[S_NEAR])
    sgtwo[...] = slot_sum(sgslot_g, 2 * G)
    sgslot_z[a] = sgtwo[...]
    for d in reversed(z_devices):
        remote(sgtwo, sgslot_z.at[a], s_send.at[S_FAR], s_recv.at[S_FAR], d)

    parts = settle(MATS - 1, out_column * v_part)
    for m in (2, 1, 0):
        parts = parts + settle(m, finish(m))
    slots = (cw // R) * n_t
    await_products(await_bytes, pslot, slots, s_recv)
    await_bytes(sgslot_z.at[fars], s_recv.at[S_FAR])
    sred[...] = slot_sum(sgslot_z, A)
    head_row = sred[SMALL - 1 : SMALL]
    for i in range(slots):
        head_row = head_row + pslot[i, 0:1]
    sred[SMALL - 1 : SMALL] = head_row
    gr = sred[0:SMALL, :] / counted
    new, dir_small = step(gr, msmall[...])
    grad_s[...] = gr
    moment_s[...] = new
    parts = parts + jnp.where(
        tile_rows == MATS, jnp.sum(dir_small * dir_small, keepdims=True) / (A * B), 0.0
    )
    me = (a * G + g) * 2 + c
    arslot[me] = parts
    for d in everyone:
        remote(arslot.at[me], arslot.at[me], s_send.at[S_ALL], s_recv.at[S_ALL], d)
    loss_b[...] = sred[SMALL : SMALL + 1, 0:1] / counted
    bias_b[...] = grad_s[7 : 7 + 2 * LAYERS, :]
    await_bytes(arslot.at[pl.ds(0, len(everyone))], s_recv.at[S_ALL])
    dir_sq = jnp.sum(arslot[...], axis=0)

    def rate_of(m):
        size = sred[SMALL + 1 : SMALL + 2, m : m + 1]
        return spread_rate * jnp.sqrt(size) / jnp.sqrt(dir_sq[m : m + 1, 0:1] + norm_epsilon)

    for m in range(MATS):
        at = (m // 2, m % 2)
        direction = grad_b[at] + momentum_coef * moment_b[at]
        new = master[at] - rate_of(m) * direction
        master_b[at] = new
        average_b[at] = average_decay * average[at] + (1.0 - average_decay) * new
        low_b[at] = new.astype(BF16)
    new = own_small - rate_of(MATS) * dir_small
    master_s[...] = new
    average_s[...] = average_decay * asmall[...] + (1.0 - average_decay) * new

    n_w, n_g = len(w_turned), len(g_turned)
    gathered = MOVED * (A - 1 + G - 1 + A * G) + (A - 1) * (MOVED * (G - 1) - n_w) + n_w * (A - 1)
    scattered = MOVED * (A - 1 + A * G) + A * (MOVED * (G - 1) - n_g) + n_g * A
    await_sent(sized.at[pl.ds(0, gathered)], w_send.at[0])
    await_sent(sized.at[pl.ds(0, scattered)], g_send.at[0])
    await_sent(qslot_z.at[fars], s_send.at[S_QFAR])
    await_sent(vslot_z.at[fars], s_send.at[S_VFAR])
    await_sent(qslot_g.at[pl.ds(0, 2 * G - 1)], s_send.at[S_QNEAR])
    await_sent(vslot_g.at[pl.ds(0, 2 * G - 1)], s_send.at[S_VNEAR])
    await_sent(sgslot_g.at[pl.ds(0, 2 * G - 1)], s_send.at[S_NEAR])
    await_products(await_sent, pdone, A * B, s_send)
    await_sent(sgslot_z.at[fars], s_send.at[S_FAR])
    await_sent(arslot.at[pl.ds(0, len(everyone))], s_send.at[S_ALL])
    await_sent(spbuf.at[pl.ds(0, n_t - 1)], s_send.at[S_PAR])


def write_out(*refs):
    sems = refs[-1]
    count = (len(refs) - 1) // 2
    copies = [
        pltpu.make_async_copy(refs[i], refs[count + i], sems.at[i]) for i in range(count)
    ]
    for copy in copies:
        copy.start()
    for copy in copies:
        copy.wait()


def body(
    axes,
    coords,
    model_ids,
    cells,
    valid,
    slowness_grid,
    master_blocks,
    small_params,
    moment_blocks,
    moment_small,
    average_blocks,
    average_small,
):
    n_dp, n_t = axes
    A = 4 if n_dp % 4 == 0 else n_dp
    B = n_dp // A
    C = n_t // 2
    G = C * B
    R, cw = master_blocks.shape[2:]
    D = R * n_dp
    PB = coords.shape[1]
    Pn = PB // n_t
    dims = (A, B, C, R, cw, Pn, D)
    anywhere = pl.BlockSpec(memory_space=pltpu.HBM)
    vmem = pl.BlockSpec(memory_space=pltpu.VMEM)
    S = SMALL + 4
    args = (
        coords,
        model_ids,
        cells,
        valid,
        slowness_grid,
        master_blocks,
        small_params,
        moment_blocks,
        moment_small,
        average_blocks,
        average_small,
    )
    V = pltpu.VMEM
    DMA = pltpu.SemaphoreType.DMA
    block = (master_blocks.shape, F32)
    short = (small_params.shape, F32)
    shapes = [
        ((1, 1), F32),
        block,
        short,
        ((2 * LAYERS, cw), F32),
        block,
        short,
        block,
        short,
        block,
        short,
        (master_blocks.shape, BF16),
    ]
    results = pl.pallas_call(
        functools.partial(kernel, dims),
        out_shape=tuple(V(*shape) for shape in shapes),
        in_specs=[anywhere] * len(args),
        out_specs=(vmem,) * len(shapes),
        scratch_shapes=[
            V(coords.shape, F32),
            V((PB,), jnp.int32),
            V((PB,), jnp.int32),
            V((PB,), jnp.int32),
            V(slowness_grid.shape, F32),
            V(master_blocks.shape, F32),
            V(master_blocks.shape, F32),
            V(small_params.shape, F32),
            V(master_blocks.shape, F32),
            V(small_params.shape, F32),
            V((n_t, SMALL, cw), F32),
            V((PB, 128), F32),
            V((S, cw), F32),
            V((MOVED, 2, C, A, B, R, cw), BF16),
            V((4, Pn, D), F32),
            V((LAYERS, 4, Pn, D), BF16),
            V((LAYERS, 4, Pn, D), F32),
            V((LAYERS, 4, Pn, D), BF16),
            V((4, Pn, D), F32),
            V((4, Pn, D), BF16),
            V((4, Pn, D), BF16),
            V((Pn, D), F32),
            V((MOVED, 2, A, G, R, cw), BF16),
            V((MOVED, A, G, R, cw), BF16),
            V((MOVED, A, G, R, cw), BF16),
            V((MOVED, A, G - 1, R, cw), BF16),
            V((MOVED, A - 1, R, cw), BF16),
            V((MOVED, A - 1, R, cw), BF16),
            V((MOVED, R, cw), F32),
            V((MOVED, A - 1, R, cw), BF16),
            V((MOVED, R, cw), BF16),
            V((MOVED, R, cw), BF16),
            V((2, C, S, cw), F32),
            V((8, cw), F32),
            V(((cw // R) * n_t, 8, cw), F32),
            V((n_dp, 8, cw), F32),
            V((MOVED * A * (2 * G + 1), R, cw), BF16),
            V((2 * G, S, cw), F32),
            V((S, cw), F32),
            V((A, S, cw), F32),
            V((2 * A * G, 8, 128), F32),
            V((A, 8, cw), F32),
            V((2 * G, 8, cw), F32),
            V((2, C, 8, cw), F32),
            V((2 * G, 8, cw), F32),
            V((A, 8, cw), F32),
            pltpu.SemaphoreType.DMA((len(args),)),
            DMA((1,)),
            DMA((MOVED, A - 1)),
            DMA((MOVED, G - 1)),
            DMA((MOVED,)),
            DMA((MOVED,)),
            DMA((1,)),
            DMA((MOVED,)),
            DMA((MOVED, A)),
            DMA((MOVED, 2)),
            DMA((MOVED,)),
            DMA((9,)),
            DMA((9,)),
        ],
        compiler_params=pltpu.CompilerParams(
            collective_id=0, has_side_effects=True, vmem_limit_bytes=60 << 20
        ),
    )(*args)

    results = pl.pallas_call(
        write_out,
        out_shape=tuple(jax.ShapeDtypeStruct(*shape) for shape in shapes),
        in_specs=[vmem] * len(shapes),
        out_specs=(anywhere,) * len(shapes),
        scratch_shapes=[pltpu.SemaphoreType.DMA((len(shapes),))],
        compiler_params=pltpu.CompilerParams(vmem_limit_bytes=4 << 20),
    )(*results)
    return (results[0].reshape(()),) + tuple(results[1:])


def solution(mesh):
    blocks = P(None, None, "dp", "tensor")
    small = P(None, "tensor")
    in_specs = (
        P(None, "dp"),
        P("dp"),
        P("dp"),
        P("dp"),
        P(),
        blocks,
        small,
        blocks,
        small,
        blocks,
        small,
    )
    out_specs = (P(), blocks, small, small, blocks, small, blocks, small, blocks, small, blocks)
    axes = (mesh.shape["dp"], mesh.shape["tensor"])
    return jax.shard_map(
        functools.partial(body, axes), mesh=mesh, in_specs=in_specs, out_specs=out_specs, check_vma=False
    )
```

```python
import functools

import jax
import jax.numpy as jnp
from jax import lax
from jax.experimental import pallas as pl
from jax.experimental.pallas import tpu as pltpu
from jax.sharding import PartitionSpec as P

LAYERS = 2
MATS = 2 * LAYERS
SMALL = 12
MESH = pl.DeviceIdType.MESH
F32 = jnp.float32
BF16 = jnp.bfloat16

momentum_coef = 0.5
average_decay = 0.5
spread_rate = 0.5
norm_epsilon = 1e-12

MOVED = MATS - 1
W_TURNED = (0, 1)
G_TURNED = (2, 1, 0)


def partners(i, size):
    values, bit = [i], 1
    while bit < size:
        change = bit - 2 * bit * lax.rem(lax.div(i, bit), 2)
        values = values + [value + change for value in values]
        bit *= 2
    return values


def nn(left, right):
    return lax.dot_general(left, right, (((1,), (0,)), ((), ())), preferred_element_type=F32)


def nt(left, right):
    return lax.dot_general(left, right, (((1,), (1,)), ((), ())), preferred_element_type=F32)


def tn(left, right):
    return lax.dot_general(left, right, (((0,), (0,)), ((), ())), preferred_element_type=F32)


def sign_of(v):
    return jnp.where(v > 0, 1.0, jnp.where(v < 0, -1.0, 0.0))


def kernel(
    dims,
    coords_hbm,
    model_hbm,
    cells_hbm,
    valid_hbm,
    grid_hbm,
    master_hbm,
    small_hbm,
    moment_hbm,
    msmall_hbm,
    average_hbm,
    asmall_hbm,
    loss_b,
    grad_b,
    grad_s,
    bias_b,
    moment_b,
    moment_s,
    master_b,
    master_s,
    average_b,
    average_s,
    low_b,
    coords,
    model,
    cells,
    valid,
    grid,
    master,
    moment,
    msmall,
    average,
    asmall,
    spbuf,
    columns,
    sred,
    wbuf,
    streams,
    acts,
    pre,
    hidden,
    grad,
    gbranch,
    gpre,
    inner,
    gsend,
    gcore,
    gone,
    gslot_n,
    gtwo,
    gslot_z,
    gown,
    tslot_z,
    tlow,
    tslot_n,
    sgsend,
    psend,
    pslot,
    pdone,
    sized,
    sgslot_g,
    sgtwo,
    sgslot_z,
    arslot,
    qslot_z,
    qslot_g,
    vsend,
    vslot_g,
    vslot_z,
    in_sem,
    w_send,
    wz_recv,
    wn_recv,
    wt_recv,
    wc_recv,
    g_send,
    gz_recv,
    gn_recv,
    gt_recv,
    gc_recv,
    s_send,
    s_recv,
):
    A, B, C, R, cw, Pn, D = dims
    n_t = 2 * C
    G = C * B
    dp = lax.axis_index("dp")
    t = lax.axis_index("tensor")
    a, b = lax.div(dp, B), lax.rem(dp, B)
    y, c = lax.div(t, 2), lax.rem(t, 2)
    g = y * B + b
    in_a, in_g, in_c, in_dp = partners(a, A), partners(g, G), partners(c, 2), partners(dp, A * B)

    def device(a_, g_, c_):
        return (a_ * B + lax.rem(g_, B), lax.div(g_, B) * 2 + c_)

    far = [in_a[k] for k in range(1, A)]
    near = [in_g[k] for k in range(1, G)]
    z_devices = [device(o, g, c) for o in far]
    g_devices = [device(a, o, c) for o in near]
    core_device = device(a, g, 1 - c)
    q_steps = [(kg, kc) for kg in range(G) for kc in range(2)][1:]
    q_steps.sort(key=lambda step: -(bin(step[0]).count("1") + step[1] / 2))
    q_coords = [(in_g[kg], in_c[kc]) for kg, kc in q_steps]
    q_devices = [device(a, o, cc) for o, cc in q_coords]
    steps = [(ka, kg, kc) for ka in range(A) for kg in range(G) for kc in range(2)][1:]
    steps.sort(key=lambda step: -(step[0] + bin(step[1]).count("1") + step[2] / 2))
    everyone = [device(in_a[ka], in_g[kg], in_c[kc]) for ka, kg, kc in steps]
    others = [d for d, step in zip(everyone, steps) if step[0] and (step[1] or step[2])]

    FARTHEST = G - 2
    w_turned = W_TURNED if G > 2 else ()
    g_turned = G_TURNED if G > 2 else ()

    def plain_near(m, turned):
        return range(G - 2 if m in turned else G - 1)

    S_PROD, S_NEAR, S_FAR, S_ALL, S_PAR, S_QFAR, S_QNEAR, S_VNEAR, S_VFAR = range(9)

    def remote(src, dst, ssem, rsem, device_id):
        copy = pltpu.make_async_remote_copy(
            src_ref=src,
            dst_ref=dst,
            send_sem=ssem,
            recv_sem=rsem,
            device_id=device_id,
            device_id_type=MESH,
        )
        copy.start()
        return copy

    def arrived(copies):
        for copy in copies:
            copy.wait_recv()

    nears, fars = pl.ds(0, G - 1), pl.ds(0, A - 1)

    local = []
    for i, (src, dst) in enumerate(
        [
            (master_hbm, master),
            (small_hbm, spbuf.at[t]),
            (coords_hbm, coords),
            (model_hbm, model),
            (cells_hbm, cells),
            (valid_hbm, valid),
            (grid_hbm, grid),
            (moment_hbm, moment),
            (msmall_hbm, msmall),
            (average_hbm, average),
            (asmall_hbm, asmall),
        ]
    ):
        copy = pltpu.make_async_copy(src, dst, in_sem.at[i])
        copy.start()
        local.append(copy)

    barrier = pltpu.get_barrier_semaphore()
    peers = z_devices + q_devices
    for d in peers:
        pl.semaphore_signal(barrier, inc=1, device_id=d, device_id_type=MESH)

    local[0].wait()
    for m in range(MOVED):
        wbuf[m, c, y, a, b] = master[m // 2, m % 2].astype(BF16)
    local[1].wait()
    pl.semaphore_wait(barrier, len(peers))

    def piece(m, o, z):
        return wbuf.at[m, c, lax.div(o, B), z, lax.rem(o, B)]

    def line(m, o):
        return wbuf.at[m, c, lax.div(o, B), :, lax.rem(o, B)]

    def plane(m, z):
        return wbuf.at[m, c, :, z]

    def await_bytes(ref, rsem):
        pltpu.make_async_remote_copy(
            src_ref=ref,
            dst_ref=ref,
            send_sem=s_send.at[0],
            recv_sem=rsem,
            device_id=core_device,
            device_id_type=MESH,
        ).wait_recv()

    def slot_sum(ref, count_of, value=None):
        for i in range(count_of):
            term = ref[i].astype(F32)
            value = term if value is None else value + term
        return value

    def await_sent(ref, ssem):
        pltpu.make_async_remote_copy(
            src_ref=ref,
            dst_ref=ref,
            send_sem=ssem,
            recv_sem=s_recv.at[0],
            device_id=core_device,
            device_id_type=MESH,
        ).wait_send()

    def w_far(m, ref):
        return [
            remote(ref, ref, w_send.at[0], wz_recv.at[m, k], z_devices[k]) for k in reversed(range(A - 1))
        ][::-1]

    def w_near(m, ref, ks):
        for k in ks:
            remote(ref, ref, w_send.at[0], wn_recv.at[m, k], g_devices[k])

    def w_core(m, ref):
        remote(ref, ref, w_send.at[0], wc_recv.at[m], core_device)

    for k in range(1, n_t):
        o = (t + k) % n_t
        remote(spbuf.at[t], spbuf.at[t], s_send.at[S_PAR], s_recv.at[S_PAR], (dp, o))
    first = {}
    for m in range(MOVED):
        first[m] = w_far(m, piece(m, g, a))
        w_near(m, piece(m, g, a), reversed(range(G - 1)))

    for copy in local[2:7]:
        copy.wait()
    cols = grid.shape[2]
    shift = (cols - 1).bit_length()
    cell = cells[...].reshape(1, -1)
    row_id = model[...].reshape(1, -1) * grid.shape[1] + (cell >> shift)
    col_id = cell & (cols - 1)
    PB = row_id.shape[1]
    packed = jnp.concatenate(
        [
            coords[...],
            row_id.astype(F32),
            col_id.astype(F32),
            valid[...].reshape(1, -1).astype(F32),
            jnp.zeros((128 - 9, PB), F32),
        ],
        0,
    )
    columns[...] = packed.T
    mine = columns[pl.ds(pl.multiple_of(t * Pn, 8), Pn), :]
    xs = [mine[:, j : j + 1] for j in range(6)]
    mask = mine[:, 8:9]
    row_of = mine[:, 6:7].astype(jnp.int32)
    col_of = mine[:, 7:8].astype(jnp.int32)
    table = grid[...].reshape(-1, cols)
    onehot = (
        lax.broadcasted_iota(jnp.int32, (Pn, table.shape[0]), 1) == row_of
    ).astype(BF16)
    high = table.astype(BF16)
    rest = table - high.astype(F32)
    middle = rest.astype(BF16)
    lowest = (rest - middle.astype(F32)).astype(BF16)
    picked = nn(onehot, high) + nn(onehot, middle) + nn(onehot, lowest)
    lane = lax.broadcasted_iota(jnp.int32, (Pn, cols), 1)
    truth = jnp.sum(jnp.where(lane == col_of, picked, 0.0), 1, keepdims=True)
    seps = [xs[3 + k] - xs[k] for k in range(3)]
    distance = jnp.sqrt(seps[0] * seps[0] + seps[1] * seps[1] + seps[2] * seps[2])
    units = [s / distance for s in seps]

    await_bytes(spbuf.at[pl.ds(0, n_t - 1)], s_recv.at[S_PAR])

    def small_row(i):
        return jnp.concatenate([spbuf[tt, i : i + 1, :] for tt in range(n_t)], 1)

    out_row = small_row(7 + 2 * LAYERS)
    last_low = master[LAYERS - 1, 1].astype(BF16).astype(F32)
    feature = lax.broadcasted_iota(jnp.int32, (R, D), 1) - lax.broadcasted_iota(jnp.int32, (R, D), 0)
    out_column = jnp.sum(jnp.where(feature == dp * R, out_row, 0.0), axis=1, keepdims=True)
    q_part = jnp.sum(last_low * out_column, axis=0, keepdims=True)
    count = jnp.sum(mask, axis=0, keepdims=True)
    row_of_8 = lax.broadcasted_iota(jnp.int32, (8, cw), 0)
    qslot_z[a] = jnp.where(row_of_8 == 0, q_part, count)
    for d in reversed(z_devices):
        remote(qslot_z.at[a], qslot_z.at[a], s_send.at[S_QFAR], s_recv.at[S_QFAR], d)

    first_rows = [small_row(j) for j in range(6)]
    z0 = small_row(6) + xs[0] * first_rows[0]
    for j in range(1, 6):
        z0 = z0 + xs[j] * first_rows[j]
    inner[...] = z0
    e0 = jnp.exp(jnp.minimum(z0, 0.0))
    slope0 = jnp.where(z0 > 0, 1.0, e0)
    streams[0] = jnp.where(z0 > 0, z0, e0 - 1.0)
    acts[0, 0] = streams[0].astype(BF16)
    for k in range(3):
        streams[1 + k] = slope0 * first_rows[3 + k]
        acts[0, 1 + k] = streams[1 + k].astype(BF16)

    def pass_on(m):
        for k in range(A - 1):
            first[m][k].wait_recv()
            w_near(m, piece(m, g, far[k]), plain_near(m, w_turned))
        w_core(m, line(m, g))
        if m in w_turned:
            o = near[FARTHEST]
            ref = piece(m, o, a)
            await_bytes(ref, wn_recv.at[m, FARTHEST])
            for d in reversed(z_devices):
                remote(ref, ref, w_send.at[0], wt_recv.at[m], d)

    for m in range(MOVED):
        pass_on(m)
    me_near = g * 2 + c
    await_bytes(qslot_z.at[fars], s_recv.at[S_QFAR])
    qslot_g[me_near] = slot_sum(qslot_z, A)
    for d in q_devices:
        remote(qslot_g.at[me_near], qslot_g.at[me_near], s_send.at[S_QNEAR], s_recv.at[S_QNEAR], d)

    def weight(m):
        return jnp.concatenate([wbuf[m, tt % 2, tt // 2].reshape(D, cw) for tt in range(n_t)], 1)

    M = 4 * Pn

    def block_in(l):
        pre[l] = nn(acts[l].reshape(M, D), weight(2 * l)).reshape(4, Pn, D)
        z = pre[l, 0] + small_row(7 + l)
        e = jnp.exp(jnp.minimum(z, 0.0))
        slope = jnp.where(z > 0, 1.0, e)
        hidden[l, 0] = jnp.where(z > 0, z, e - 1.0).astype(BF16)
        for k in range(1, 4):
            hidden[l, k] = (slope * pre[l, k]).astype(BF16)

    def block_out(l):
        branch = nt(hidden[l].reshape(M, D), weight(2 * l + 1)).reshape(4, Pn, D)
        for s in range(4):
            new = streams[s] + branch[s]
            if s == 0:
                new = new + small_row(7 + LAYERS + l)
            streams[s] = new
            if l + 1 < LAYERS:
                acts[l + 1, s] = new.astype(BF16)

    def fetch(m):
        for k in range(G - 1):
            if m in w_turned and k == FARTHEST:
                await_bytes(wbuf.at[m, c, 0, fars, 0], wt_recv.at[m])
            else:
                await_bytes(line(m, near[k]), wn_recv.at[m, k])
            w_core(m, line(m, near[k]))

    def fetched(m):
        await_bytes(wbuf.at[m, c], wc_recv.at[m])

    for m in range(MOVED):
        fetch(m)
        fetched(m)
        if m == 0:
            for d in others:
                pl.semaphore_signal(barrier, inc=1, device_id=d, device_id_type=MESH)
        if m % 2 == 0:
            block_in(m // 2)
        else:
            block_out(m // 2)
        if m == MOVED - 2:
            proj_a = [jnp.sum(streams[s] * out_row, axis=1, keepdims=True) for s in range(4)]
            bias_row = small_row(6 + 2 * LAYERS)
            proj_a[0] = proj_a[0] + jnp.sum(bias_row * out_row, axis=1, keepdims=True)
            await_bytes(qslot_g.at[pl.ds(0, 2 * G - 1)], s_recv.at[S_QNEAR])
            q_row = []
            for tt in range(n_t):
                total = qslot_g[(tt // 2) * B * 2 + tt % 2, 0:1]
                for i in range(1, B):
                    total = total + qslot_g[((tt // 2) * B + i) * 2 + tt % 2, 0:1]
                q_row.append(total)
            q_row = jnp.concatenate(q_row, 1)
            counted = slot_sum(qslot_g, 2 * G)[1:2, 0:1]

    last = LAYERS - 1
    proj = [
        proj_a[s] + jnp.sum(hidden[last, s].astype(F32) * q_row, axis=1, keepdims=True) for s in range(4)
    ]
    tau = proj[0]
    sign_tau = sign_of(tau)
    abs_tau = jnp.abs(tau)
    grad_time = [units[k] * abs_tau + distance * sign_tau * proj[1 + k] for k in range(3)]
    square = grad_time[0] * grad_time[0] + grad_time[1] * grad_time[1] + grad_time[2] * grad_time[2]
    error = square - truth * truth
    total_err = jnp.sum(mask * jnp.abs(error), axis=0, keepdims=True)
    seed = mask * sign_of(error)
    g_time = [2.0 * grad_time[k] * seed for k in range(3)]
    g_tau = sign_tau * (units[0] * g_time[0] + units[1] * g_time[1] + units[2] * g_time[2])
    g_proj = [g_tau] + [distance * sign_tau * g_time[k] for k in range(3)]
    v_row = jnp.sum(
        sum(hidden[last, s].astype(F32) * g_proj[s] for s in range(4)), axis=0, keepdims=True
    )
    for tt in range(n_t):
        vsend[tt % 2, tt // 2] = jnp.broadcast_to(v_row[:, tt * cw : (tt + 1) * cw], (8, cw))
    vslot_g[me_near] = vsend[c, y]
    for (o, cc), d in zip(q_coords, q_devices):
        remote(vsend.at[cc, lax.div(o, B)], vslot_g.at[me_near], s_send.at[S_VNEAR], s_recv.at[S_VNEAR], d)

    def v_far():
        await_bytes(vslot_g.at[pl.ds(0, 2 * G - 1)], s_recv.at[S_VNEAR])
        vslot_z[a] = slot_sum(vslot_g, 2 * G)
        for d in reversed(z_devices):
            remote(vslot_z.at[a], vslot_z.at[a], s_send.at[S_VFAR], s_recv.at[S_VFAR], d)

    pieces = [(far[k], k) for k in reversed(range(A - 1))] + [(a, None)]

    def start_core(m, value):
        low = value.astype(BF16)
        for tt in range(n_t):
            block = low[:, tt * cw : (tt + 1) * cw].reshape(A, B, R, cw)
            for i in range(B):
                gsend[m, tt % 2, :, (tt // 2) * B + i] = block[:, i]
        for z, _ in pieces:
            remote(gsend.at[m, 1 - c, z], gcore.at[m, z], g_send.at[0], gc_recv.at[m], core_device)

    def core_sum(m, j):
        z = pieces[j][0]
        gone[m, z] = (gsend[m, c, z].astype(F32) + gcore[m, z].astype(F32)).astype(BF16)

    def start_near(m):
        await_bytes(gcore.at[m], gc_recv.at[m])
        for j, (z, kz) in enumerate(pieces):
            core_sum(m, j)
            for k in plain_near(m, g_turned):
                remote(
                    gone.at[m, z, near[k]],
                    gslot_n.at[m, j, k],
                    g_send.at[0],
                    gn_recv.at[m, j],
                    g_devices[k],
                )
            if m in g_turned and kz is not None:
                remote(
                    gone.at[m, z, near[FARTHEST]],
                    tslot_z.at[m, kz],
                    g_send.at[0],
                    gt_recv.at[m, 0],
                    z_devices[kz],
                )

    def start_far(m):
        count_of = len(plain_near(m, g_turned))
        for j, (z, k) in enumerate(pieces):
            if count_of:
                await_bytes(gslot_n.at[m, j, pl.ds(0, count_of)], gn_recv.at[m, j])
            total = slot_sum(gslot_n.at[m, j], count_of, gone[m, z, g].astype(F32))
            if k is None:
                gown[m] = total
            else:
                gtwo[m, k] = total.astype(BF16)
                remote(gtwo.at[m, k], gslot_z.at[m, k], g_send.at[0], gz_recv.at[m], z_devices[k])

    def start_turned(m):
        if m in g_turned:
            await_bytes(tslot_z.at[m], gt_recv.at[m, 0])
            total = slot_sum(tslot_z.at[m], A - 1, gone[m, a, near[FARTHEST]].astype(F32))
            tlow[m] = total.astype(BF16)
            remote(tlow.at[m], tslot_n.at[m], g_send.at[0], gt_recv.at[m, 1], g_devices[FARTHEST])

    def finish(m):
        await_bytes(gslot_z.at[m], gz_recv.at[m])
        total = slot_sum(gslot_z.at[m], A - 1, gown[m])
        if m in g_turned:
            await_bytes(tslot_n.at[m], gt_recv.at[m, 1])
            total = total + tslot_n[m].astype(F32)
        return total

    bias_in = [None] * LAYERS
    bias_out = [None] * LAYERS

    def back_last():
        z = pre[last, 0] + small_row(7 + last)
        e = jnp.exp(jnp.minimum(z, 0.0))
        slope = jnp.where(z > 0, 1.0, e)
        curve = jnp.where(z > 0, 0.0, e)
        mixed = g_proj[1] * pre[last, 1] + g_proj[2] * pre[last, 2] + g_proj[3] * pre[last, 3]
        gz = q_row * (g_proj[0] * slope + curve * mixed)
        bias_in[last] = jnp.sum(gz, axis=0, keepdims=True)
        gpre[0] = gz.astype(BF16)
        slope = slope * q_row
        for k in range(1, 4):
            gpre[k] = (g_proj[k] * slope).astype(BF16)

    def back_out(l):
        bias_out[l] = jnp.sum(grad[0], axis=0, keepdims=True)
        gb = gbranch[...].reshape(M, D)
        start_core(2 * l + 1, tn(gb, hidden[l].reshape(M, D)))

    def back_in(l):
        gb = gbranch[...].reshape(M, D)
        gh = nn(gb, weight(2 * l + 1)).reshape(4, Pn, D)
        z = pre[l, 0] + small_row(7 + l)
        e = jnp.exp(jnp.minimum(z, 0.0))
        slope = jnp.where(z > 0, 1.0, e)
        curve = jnp.where(z > 0, 0.0, e)
        gz = gh[0] * slope + curve * (gh[1] * pre[l, 1] + gh[2] * pre[l, 2] + gh[3] * pre[l, 3])
        bias_in[l] = jnp.sum(gz, axis=0, keepdims=True)
        gpre[0] = gz.astype(BF16)
        for k in range(1, 4):
            gpre[k] = (gh[k] * slope).astype(BF16)

    def back_weight(l):
        start_core(2 * l, tn(acts[l].reshape(M, D), gpre[...].reshape(M, D)))

    def back_through(l):
        back = nt(gpre[...].reshape(M, D), weight(2 * l)).reshape(4, Pn, D)
        for s in range(4):
            value = (out_row * g_proj[s] if l == last else grad[s]) + back[s]
            grad[s] = value
            if l > 0:
                gbranch[s] = value.astype(BF16)

    back_last()
    back_weight(1)
    tau_sum = jnp.sum(g_proj[0], axis=0, keepdims=True)
    bias_out[last] = out_row * tau_sum
    g_out_row = bias_row * tau_sum + jnp.sum(
        streams[0] * g_proj[0] + streams[1] * g_proj[1] + streams[2] * g_proj[2] + streams[3] * g_proj[3],
        axis=0,
        keepdims=True,
    )
    back_through(1)
    back_out(0)
    start_near(2)
    back_in(0)
    back_weight(0)
    start_near(1)
    back_through(0)
    v_far()

    z0 = inner[...]
    e0 = jnp.exp(jnp.minimum(z0, 0.0))
    slope0 = jnp.where(z0 > 0, 1.0, e0)
    curve0 = jnp.where(z0 > 0, 0.0, e0)
    first_rows = [small_row(j) for j in range(6)]
    g_inner = grad[0] * slope0 + curve0 * (
        grad[1] * first_rows[3] + grad[2] * first_rows[4] + grad[3] * first_rows[5]
    )
    rows = [jnp.sum(xs[j] * g_inner, axis=0, keepdims=True) for j in range(6)]
    for k in range(3):
        rows[3 + k] = rows[3 + k] + jnp.sum(grad[1 + k] * slope0, axis=0, keepdims=True)
    rows.append(jnp.sum(g_inner, axis=0, keepdims=True))
    rows = rows + bias_in + bias_out + [g_out_row]

    lanes = lax.broadcasted_iota(jnp.int32, (1, cw), 1)
    weight_sq = jnp.zeros((1, cw), F32)
    for m in range(MATS):
        part = jnp.sum(master[m // 2, m % 2] * master[m // 2, m % 2], keepdims=True)
        weight_sq = jnp.where(lanes == m, part, weight_sq)
    own_small = spbuf[t]
    weight_sq = jnp.where(lanes == MATS, jnp.sum(own_small * own_small, keepdims=True) / (A * B), weight_sq)
    tail = [
        jnp.broadcast_to(total_err, (1, cw)),
        weight_sq,
        jnp.zeros((2, cw), F32),
    ]
    for tt in range(n_t):
        sgsend[tt % 2, tt // 2] = jnp.concatenate([r[:, tt * cw : (tt + 1) * cw] for r in rows] + tail, 0)
    sgslot_g[me_near] = sgsend[c, y]
    for (o, cc), d in zip(q_coords, q_devices):
        remote(sgsend.at[cc, lax.div(o, B)], sgslot_g.at[me_near], s_send.at[S_NEAR], s_recv.at[S_NEAR], d)
    start_near(0)

    for copy in local[7:]:
        copy.wait()
    tile_rows = lax.broadcasted_iota(jnp.int32, (8, 128), 0)

    def step(gradient, momentum):
        new = momentum_coef * momentum + gradient
        return new, gradient + momentum_coef * new

    def settle(m, total):
        at = (m // 2, m % 2)
        gr = total / counted
        new, direction = step(gr, moment[at])
        grad_b[at] = gr
        moment_b[at] = new
        return jnp.where(tile_rows == m, jnp.sum(direction * direction, keepdims=True), 0.0)

    start_far(2)
    start_turned(2)
    start_far(1)
    start_turned(1)

    await_bytes(vslot_z.at[fars], s_recv.at[S_VFAR])
    v_part = slot_sum(vslot_z, A)[0:1]
    product = jnp.sum(last_low * v_part, axis=1, keepdims=True)
    place = lax.broadcasted_iota(jnp.int32, (R, cw), 1) - lax.broadcasted_iota(jnp.int32, (R, cw), 0)
    product_row = jnp.sum(jnp.where(place == (dp * R) % cw, product, 0.0), axis=0, keepdims=True)
    psend[...] = jnp.broadcast_to(product_row, (8, cw))
    column = (dp * R) // cw
    mine_too = column == t
    slot = (dp % (cw // R)) * n_t + t
    pl.semaphore_wait(barrier, len(others))
    for k in reversed(range(1, A * B)):
        remote(
            psend, pslot.at[slot], s_send.at[S_PROD], s_recv.at[S_PROD], (in_dp[k], column)
        )

    @pl.when(mine_too)
    def _():
        pslot[slot] = psend[...]

    @pl.when(jnp.logical_not(mine_too))
    def _():
        remote(psend, pslot.at[slot], s_send.at[S_PROD], s_recv.at[S_PROD], (dp, column))

    def await_products(wait, ref, count_of, sems):
        @pl.when(mine_too)
        def _():
            wait(ref.at[pl.ds(0, count_of - 1)], sems.at[S_PROD])

        @pl.when(jnp.logical_not(mine_too))
        def _():
            wait(ref.at[pl.ds(0, count_of)], sems.at[S_PROD])

    start_far(0)
    start_turned(0)
    await_bytes(sgslot_g.at[pl.ds(0, 2 * G - 1)], s_recv.at[S_NEAR])
    sgtwo[...] = slot_sum(sgslot_g, 2 * G)
    sgslot_z[a] = sgtwo[...]
    for d in reversed(z_devices):
        remote(sgtwo, sgslot_z.at[a], s_send.at[S_FAR], s_recv.at[S_FAR], d)

    parts = settle(MATS - 1, out_column * v_part)
    for m in (2, 1, 0):
        parts = parts + settle(m, finish(m))
    slots = (cw // R) * n_t
    await_products(await_bytes, pslot, slots, s_recv)
    await_bytes(sgslot_z.at[fars], s_recv.at[S_FAR])
    sred[...] = slot_sum(sgslot_z, A)
    head_row = sred[SMALL - 1 : SMALL]
    for i in range(slots):
        head_row = head_row + pslot[i, 0:1]
    sred[SMALL - 1 : SMALL] = head_row
    gr = sred[0:SMALL, :] / counted
    new, dir_small = step(gr, msmall[...])
    grad_s[...] = gr
    moment_s[...] = new
    parts = parts + jnp.where(
        tile_rows == MATS, jnp.sum(dir_small * dir_small, keepdims=True) / (A * B), 0.0
    )
    me = (a * G + g) * 2 + c
    arslot[me] = parts
    for d in everyone:
        remote(arslot.at[me], arslot.at[me], s_send.at[S_ALL], s_recv.at[S_ALL], d)
    loss_b[...] = sred[SMALL : SMALL + 1, 0:1] / counted
    bias_b[...] = grad_s[7 : 7 + 2 * LAYERS, :]
    await_bytes(arslot.at[pl.ds(0, len(everyone))], s_recv.at[S_ALL])
    dir_sq = jnp.sum(arslot[...], axis=0)

    def rate_of(m):
        size = sred[SMALL + 1 : SMALL + 2, m : m + 1]
        return spread_rate * jnp.sqrt(size) / jnp.sqrt(dir_sq[m : m + 1, 0:1] + norm_epsilon)

    for m in range(MATS):
        at = (m // 2, m % 2)
        direction = grad_b[at] + momentum_coef * moment_b[at]
        new = master[at] - rate_of(m) * direction
        master_b[at] = new
        average_b[at] = average_decay * average[at] + (1.0 - average_decay) * new
        low_b[at] = new.astype(BF16)
    new = own_small - rate_of(MATS) * dir_small
    master_s[...] = new
    average_s[...] = average_decay * asmall[...] + (1.0 - average_decay) * new

    n_w, n_g = len(w_turned), len(g_turned)
    gathered = MOVED * (A - 1 + G - 1 + A * G) + (A - 1) * (MOVED * (G - 1) - n_w) + n_w * (A - 1)
    scattered = MOVED * (A - 1 + A * G) + A * (MOVED * (G - 1) - n_g) + n_g * A
    await_sent(sized.at[pl.ds(0, gathered)], w_send.at[0])
    await_sent(sized.at[pl.ds(0, scattered)], g_send.at[0])
    await_sent(qslot_z.at[fars], s_send.at[S_QFAR])
    await_sent(vslot_z.at[fars], s_send.at[S_VFAR])
    await_sent(qslot_g.at[pl.ds(0, 2 * G - 1)], s_send.at[S_QNEAR])
    await_sent(vslot_g.at[pl.ds(0, 2 * G - 1)], s_send.at[S_VNEAR])
    await_sent(sgslot_g.at[pl.ds(0, 2 * G - 1)], s_send.at[S_NEAR])
    await_products(await_sent, pdone, A * B, s_send)
    await_sent(sgslot_z.at[fars], s_send.at[S_FAR])
    await_sent(arslot.at[pl.ds(0, len(everyone))], s_send.at[S_ALL])
    await_sent(spbuf.at[pl.ds(0, n_t - 1)], s_send.at[S_PAR])


def write_out(*refs):
    sems = refs[-1]
    count = (len(refs) - 1) // 2
    copies = [
        pltpu.make_async_copy(refs[i], refs[count + i], sems.at[i]) for i in range(count)
    ]
    for copy in copies:
        copy.start()
    for copy in copies:
        copy.wait()


def body(
    axes,
    coords,
    model_ids,
    cells,
    valid,
    slowness_grid,
    master_blocks,
    small_params,
    moment_blocks,
    moment_small,
    average_blocks,
    average_small,
):
    n_dp, n_t = axes
    A = 4 if n_dp % 4 == 0 else n_dp
    B = n_dp // A
    C = n_t // 2
    G = C * B
    R, cw = master_blocks.shape[2:]
    D = R * n_dp
    PB = coords.shape[1]
    Pn = PB // n_t
    dims = (A, B, C, R, cw, Pn, D)
    anywhere = pl.BlockSpec(memory_space=pltpu.HBM)
    vmem = pl.BlockSpec(memory_space=pltpu.VMEM)
    S = SMALL + 4
    args = (
        coords,
        model_ids,
        cells,
        valid,
        slowness_grid,
        master_blocks,
        small_params,
        moment_blocks,
        moment_small,
        average_blocks,
        average_small,
    )
    V = pltpu.VMEM
    DMA = pltpu.SemaphoreType.DMA
    block = (master_blocks.shape, F32)
    short = (small_params.shape, F32)
    shapes = [
        ((1, 1), F32),
        block,
        short,
        ((2 * LAYERS, cw), F32),
        block,
        short,
        block,
        short,
        block,
        short,
        (master_blocks.shape, BF16),
    ]
    results = pl.pallas_call(
        functools.partial(kernel, dims),
        out_shape=tuple(V(*shape) for shape in shapes),
        in_specs=[anywhere] * len(args),
        out_specs=(vmem,) * len(shapes),
        scratch_shapes=[
            V(coords.shape, F32),
            V((PB,), jnp.int32),
            V((PB,), jnp.int32),
            V((PB,), jnp.int32),
            V(slowness_grid.shape, F32),
            V(master_blocks.shape, F32),
            V(master_blocks.shape, F32),
            V(small_params.shape, F32),
            V(master_blocks.shape, F32),
            V(small_params.shape, F32),
            V((n_t, SMALL, cw), F32),
            V((PB, 128), F32),
            V((S, cw), F32),
            V((MOVED, 2, C, A, B, R, cw), BF16),
            V((4, Pn, D), F32),
            V((LAYERS, 4, Pn, D), BF16),
            V((LAYERS, 4, Pn, D), F32),
            V((LAYERS, 4, Pn, D), BF16),
            V((4, Pn, D), F32),
            V((4, Pn, D), BF16),
            V((4, Pn, D), BF16),
            V((Pn, D), F32),
            V((MOVED, 2, A, G, R, cw), BF16),
            V((MOVED, A, G, R, cw), BF16),
            V((MOVED, A, G, R, cw), BF16),
            V((MOVED, A, G - 1, R, cw), BF16),
            V((MOVED, A - 1, R, cw), BF16),
            V((MOVED, A - 1, R, cw), BF16),
            V((MOVED, R, cw), F32),
            V((MOVED, A - 1, R, cw), BF16),
            V((MOVED, R, cw), BF16),
            V((MOVED, R, cw), BF16),
            V((2, C, S, cw), F32),
            V((8, cw), F32),
            V(((cw // R) * n_t, 8, cw), F32),
            V((n_dp, 8, cw), F32),
            V((MOVED * A * (2 * G + 1), R, cw), BF16),
            V((2 * G, S, cw), F32),
            V((S, cw), F32),
            V((A, S, cw), F32),
            V((2 * A * G, 8, 128), F32),
            V((A, 8, cw), F32),
            V((2 * G, 8, cw), F32),
            V((2, C, 8, cw), F32),
            V((2 * G, 8, cw), F32),
            V((A, 8, cw), F32),
            pltpu.SemaphoreType.DMA((len(args),)),
            DMA((1,)),
            DMA((MOVED, A - 1)),
            DMA((MOVED, G - 1)),
            DMA((MOVED,)),
            DMA((MOVED,)),
            DMA((1,)),
            DMA((MOVED,)),
            DMA((MOVED, A)),
            DMA((MOVED, 2)),
            DMA((MOVED,)),
            DMA((9,)),
            DMA((9,)),
        ],
        compiler_params=pltpu.CompilerParams(
            collective_id=0, has_side_effects=True, vmem_limit_bytes=60 << 20
        ),
    )(*args)

    results = pl.pallas_call(
        write_out,
        out_shape=tuple(jax.ShapeDtypeStruct(*shape) for shape in shapes),
        in_specs=[vmem] * len(shapes),
        out_specs=(anywhere,) * len(shapes),
        scratch_shapes=[pltpu.SemaphoreType.DMA((len(shapes),))],
        compiler_params=pltpu.CompilerParams(vmem_limit_bytes=4 << 20),
    )(*results)
    return (results[0].reshape(()),) + tuple(results[1:])


def solution(mesh):
    blocks = P(None, None, "dp", "tensor")
    small = P(None, "tensor")
    in_specs = (
        P(None, "dp"),
        P("dp"),
        P("dp"),
        P("dp"),
        P(),
        blocks,
        small,
        blocks,
        small,
        blocks,
        small,
    )
    out_specs = (P(), blocks, small, small, blocks, small, blocks, small, blocks, small, blocks)
    axes = (mesh.shape["dp"], mesh.shape["tensor"])
    return jax.shard_map(
        functools.partial(body, axes), mesh=mesh, in_specs=in_specs, out_specs=out_specs, check_vma=False
    )
```

```python
import functools

import jax
import jax.numpy as jnp
from jax import lax
from jax.experimental import pallas as pl
from jax.experimental.pallas import tpu as pltpu
from jax.sharding import PartitionSpec as P

LAYERS = 2
MATS = 2 * LAYERS
SMALL = 12
MESH = pl.DeviceIdType.MESH
F32 = jnp.float32
BF16 = jnp.bfloat16

momentum_coef = 0.5
average_decay = 0.5
spread_rate = 0.5
norm_epsilon = 1e-12

MOVED = MATS - 1
W_TURNED = (0, 1)
G_TURNED = (2, 1, 0)


def partners(i, size):
    values, bit = [i], 1
    while bit < size:
        change = bit - 2 * bit * lax.rem(lax.div(i, bit), 2)
        values = values + [value + change for value in values]
        bit *= 2
    return values


def nn(left, right):
    return lax.dot_general(left, right, (((1,), (0,)), ((), ())), preferred_element_type=F32)


def nt(left, right):
    return lax.dot_general(left, right, (((1,), (1,)), ((), ())), preferred_element_type=F32)


def tn(left, right):
    return lax.dot_general(left, right, (((0,), (0,)), ((), ())), preferred_element_type=F32)


def sign_of(v):
    return jnp.where(v > 0, 1.0, jnp.where(v < 0, -1.0, 0.0))


def kernel(
    dims,
    coords_hbm,
    model_hbm,
    cells_hbm,
    valid_hbm,
    grid_hbm,
    master_hbm,
    small_hbm,
    moment_hbm,
    msmall_hbm,
    average_hbm,
    asmall_hbm,
    loss_b,
    grad_b,
    grad_s,
    bias_b,
    moment_b,
    moment_s,
    master_b,
    master_s,
    average_b,
    average_s,
    low_b,
    coords,
    model,
    cells,
    valid,
    grid,
    master,
    moment,
    msmall,
    average,
    asmall,
    spbuf,
    columns,
    sred,
    wbuf,
    streams,
    acts,
    pre,
    hidden,
    grad,
    gbranch,
    gpre,
    inner,
    gsend,
    gcore,
    gone,
    gslot_n,
    gtwo,
    gslot_z,
    gown,
    tslot_z,
    tlow,
    tslot_n,
    sgsend,
    psend,
    pslot,
    pdone,
    sized,
    sgslot_g,
    sgtwo,
    sgslot_z,
    arslot,
    qslot_z,
    qslot_g,
    vsend,
    vslot_g,
    vslot_z,
    in_sem,
    w_send,
    wz_recv,
    wn_recv,
    wt_recv,
    wc_recv,
    g_send,
    gz_recv,
    gn_recv,
    gt_recv,
    gc_recv,
    s_send,
    s_recv,
):
    A, B, C, R, cw, Pn, D = dims
    n_t = 2 * C
    G = C * B
    dp = lax.axis_index("dp")
    t = lax.axis_index("tensor")
    a, b = lax.div(dp, B), lax.rem(dp, B)
    y, c = lax.div(t, 2), lax.rem(t, 2)
    g = y * B + b
    in_a, in_g, in_c, in_dp = partners(a, A), partners(g, G), partners(c, 2), partners(dp, A * B)

    def device(a_, g_, c_):
        return (a_ * B + lax.rem(g_, B), lax.div(g_, B) * 2 + c_)

    far = [in_a[k] for k in range(1, A)]
    near = [in_g[k] for k in range(1, G)]
    z_devices = [device(o, g, c) for o in far]
    g_devices = [device(a, o, c) for o in near]
    core_device = device(a, g, 1 - c)
    q_steps = [(kg, kc) for kg in range(G) for kc in range(2)][1:]
    q_steps.sort(key=lambda step: -(bin(step[0]).count("1") + step[1] / 2))
    q_coords = [(in_g[kg], in_c[kc]) for kg, kc in q_steps]
    q_devices = [device(a, o, cc) for o, cc in q_coords]
    steps = [(ka, kg, kc) for ka in range(A) for kg in range(G) for kc in range(2)][1:]
    steps.sort(key=lambda step: -(step[0] + bin(step[1]).count("1") + step[2] / 2))
    everyone = [device(in_a[ka], in_g[kg], in_c[kc]) for ka, kg, kc in steps]
    others = [d for d, step in zip(everyone, steps) if step[0] and (step[1] or step[2])]

    FARTHEST = G - 2
    w_turned = W_TURNED if G > 2 else ()
    g_turned = G_TURNED if G > 2 else ()

    def plain_near(m, turned):
        return range(G - 2 if m in turned else G - 1)

    S_PROD, S_NEAR, S_FAR, S_ALL, S_PAR, S_QFAR, S_QNEAR, S_VNEAR, S_VFAR = range(9)

    def remote(src, dst, ssem, rsem, device_id):
        copy = pltpu.make_async_remote_copy(
            src_ref=src,
            dst_ref=dst,
            send_sem=ssem,
            recv_sem=rsem,
            device_id=device_id,
            device_id_type=MESH,
        )
        copy.start()
        return copy

    def arrived(copies):
        for copy in copies:
            copy.wait_recv()

    nears, fars = pl.ds(0, G - 1), pl.ds(0, A - 1)

    local = []
    for i, (src, dst) in enumerate(
        [
            (master_hbm, master),
            (small_hbm, spbuf.at[t]),
            (coords_hbm, coords),
            (model_hbm, model),
            (cells_hbm, cells),
            (valid_hbm, valid),
            (grid_hbm, grid),
            (moment_hbm, moment),
            (msmall_hbm, msmall),
            (average_hbm, average),
            (asmall_hbm, asmall),
        ]
    ):
        copy = pltpu.make_async_copy(src, dst, in_sem.at[i])
        copy.start()
        local.append(copy)

    barrier = pltpu.get_barrier_semaphore()
    peers = z_devices + q_devices
    for d in peers:
        pl.semaphore_signal(barrier, inc=1, device_id=d, device_id_type=MESH)

    local[0].wait()
    for m in range(MOVED):
        wbuf[m, c, y, a, b] = master[m // 2, m % 2].astype(BF16)
    local[1].wait()
    pl.semaphore_wait(barrier, len(peers))

    def piece(m, o, z):
        return wbuf.at[m, c, lax.div(o, B), z, lax.rem(o, B)]

    def line(m, o):
        return wbuf.at[m, c, lax.div(o, B), :, lax.rem(o, B)]

    def plane(m, z):
        return wbuf.at[m, c, :, z]

    def await_bytes(ref, rsem):
        pltpu.make_async_remote_copy(
            src_ref=ref,
            dst_ref=ref,
            send_sem=s_send.at[0],
            recv_sem=rsem,
            device_id=core_device,
            device_id_type=MESH,
        ).wait_recv()

    def slot_sum(ref, count_of, value=None):
        for i in range(count_of):
            term = ref[i].astype(F32)
            value = term if value is None else value + term
        return value

    def await_sent(ref, ssem):
        pltpu.make_async_remote_copy(
            src_ref=ref,
            dst_ref=ref,
            send_sem=ssem,
            recv_sem=s_recv.at[0],
            device_id=core_device,
            device_id_type=MESH,
        ).wait_send()

    def w_far(m, ref):
        return [
            remote(ref, ref, w_send.at[0], wz_recv.at[m, k], z_devices[k]) for k in reversed(range(A - 1))
        ][::-1]

    def w_near(m, ref, ks):
        for k in ks:
            remote(ref, ref, w_send.at[0], wn_recv.at[m, k], g_devices[k])

    def w_core(m, ref):
        remote(ref, ref, w_send.at[0], wc_recv.at[m], core_device)

    for k in range(1, n_t):
        o = (t + k) % n_t
        remote(spbuf.at[t], spbuf.at[t], s_send.at[S_PAR], s_recv.at[S_PAR], (dp, o))
    first = {}
    for m in range(MOVED):
        first[m] = w_far(m, piece(m, g, a))
    for m in range(MOVED):
        w_near(m, piece(m, g, a), reversed(range(G - 1)))

    for copy in local[2:7]:
        copy.wait()
    cols = grid.shape[2]
    shift = (cols - 1).bit_length()
    cell = cells[...].reshape(1, -1)
    row_id = model[...].reshape(1, -1) * grid.shape[1] + (cell >> shift)
    col_id = cell & (cols - 1)
    PB = row_id.shape[1]
    packed = jnp.concatenate(
        [
            coords[...],
            row_id.astype(F32),
            col_id.astype(F32),
            valid[...].reshape(1, -1).astype(F32),
            jnp.zeros((128 - 9, PB), F32),
        ],
        0,
    )
    columns[...] = packed.T
    mine = columns[pl.ds(pl.multiple_of(t * Pn, 8), Pn), :]
    xs = [mine[:, j : j + 1] for j in range(6)]
    mask = mine[:, 8:9]
    row_of = mine[:, 6:7].astype(jnp.int32)
    col_of = mine[:, 7:8].astype(jnp.int32)
    table = grid[...].reshape(-1, cols)
    onehot = (
        lax.broadcasted_iota(jnp.int32, (Pn, table.shape[0]), 1) == row_of
    ).astype(BF16)
    high = table.astype(BF16)
    rest = table - high.astype(F32)
    middle = rest.astype(BF16)
    lowest = (rest - middle.astype(F32)).astype(BF16)
    picked = nn(onehot, high) + nn(onehot, middle) + nn(onehot, lowest)
    lane = lax.broadcasted_iota(jnp.int32, (Pn, cols), 1)
    truth = jnp.sum(jnp.where(lane == col_of, picked, 0.0), 1, keepdims=True)
    seps = [xs[3 + k] - xs[k] for k in range(3)]
    distance = jnp.sqrt(seps[0] * seps[0] + seps[1] * seps[1] + seps[2] * seps[2])
    units = [s / distance for s in seps]

    await_bytes(spbuf.at[pl.ds(0, n_t - 1)], s_recv.at[S_PAR])

    def small_row(i):
        return jnp.concatenate([spbuf[tt, i : i + 1, :] for tt in range(n_t)], 1)

    out_row = small_row(7 + 2 * LAYERS)
    last_low = master[LAYERS - 1, 1].astype(BF16).astype(F32)
    feature = lax.broadcasted_iota(jnp.int32, (R, D), 1) - lax.broadcasted_iota(jnp.int32, (R, D), 0)
    out_column = jnp.sum(jnp.where(feature == dp * R, out_row, 0.0), axis=1, keepdims=True)
    q_part = jnp.sum(last_low * out_column, axis=0, keepdims=True)
    count = jnp.sum(mask, axis=0, keepdims=True)
    row_of_8 = lax.broadcasted_iota(jnp.int32, (8, cw), 0)
    qslot_z[a] = jnp.where(row_of_8 == 0, q_part, count)
    for d in reversed(z_devices):
        remote(qslot_z.at[a], qslot_z.at[a], s_send.at[S_QFAR], s_recv.at[S_QFAR], d)

    first_rows = [small_row(j) for j in range(6)]
    z0 = small_row(6) + xs[0] * first_rows[0]
    for j in range(1, 6):
        z0 = z0 + xs[j] * first_rows[j]
    inner[...] = z0
    e0 = jnp.exp(jnp.minimum(z0, 0.0))
    slope0 = jnp.where(z0 > 0, 1.0, e0)
    streams[0] = jnp.where(z0 > 0, z0, e0 - 1.0)
    acts[0, 0] = streams[0].astype(BF16)
    for k in range(3):
        streams[1 + k] = slope0 * first_rows[3 + k]
        acts[0, 1 + k] = streams[1 + k].astype(BF16)

    def pass_on(m):
        for k in range(A - 1):
            first[m][k].wait_recv()
            w_near(m, piece(m, g, far[k]), plain_near(m, w_turned))
        w_core(m, line(m, g))
        if m in w_turned:
            o = near[FARTHEST]
            ref = piece(m, o, a)
            await_bytes(ref, wn_recv.at[m, FARTHEST])
            for d in reversed(z_devices):
                remote(ref, ref, w_send.at[0], wt_recv.at[m], d)

    for m in range(MOVED):
        pass_on(m)
    me_near = g * 2 + c
    await_bytes(qslot_z.at[fars], s_recv.at[S_QFAR])
    qslot_g[me_near] = slot_sum(qslot_z, A)
    for d in q_devices:
        remote(qslot_g.at[me_near], qslot_g.at[me_near], s_send.at[S_QNEAR], s_recv.at[S_QNEAR], d)

    def weight(m):
        return jnp.concatenate([wbuf[m, tt % 2, tt // 2].reshape(D, cw) for tt in range(n_t)], 1)

    M = 4 * Pn

    def block_in(l):
        pre[l] = nn(acts[l].reshape(M, D), weight(2 * l)).reshape(4, Pn, D)
        z = pre[l, 0] + small_row(7 + l)
        e = jnp.exp(jnp.minimum(z, 0.0))
        slope = jnp.where(z > 0, 1.0, e)
        hidden[l, 0] = jnp.where(z > 0, z, e - 1.0).astype(BF16)
        for k in range(1, 4):
            hidden[l, k] = (slope * pre[l, k]).astype(BF16)

    def block_out(l):
        branch = nt(hidden[l].reshape(M, D), weight(2 * l + 1)).reshape(4, Pn, D)
        for s in range(4):
            new = streams[s] + branch[s]
            if s == 0:
                new = new + small_row(7 + LAYERS + l)
            streams[s] = new
            if l + 1 < LAYERS:
                acts[l + 1, s] = new.astype(BF16)

    def fetch(m):
        for k in range(G - 1):
            if m in w_turned and k == FARTHEST:
                await_bytes(wbuf.at[m, c, 0, fars, 0], wt_recv.at[m])
            else:
                await_bytes(line(m, near[k]), wn_recv.at[m, k])
            w_core(m, line(m, near[k]))

    def fetched(m):
        await_bytes(wbuf.at[m, c], wc_recv.at[m])

    for m in range(MOVED):
        fetch(m)
        fetched(m)
        if m == 0:
            for d in others:
                pl.semaphore_signal(barrier, inc=1, device_id=d, device_id_type=MESH)
        if m % 2 == 0:
            block_in(m // 2)
        else:
            block_out(m // 2)
        if m == MOVED - 2:
            proj_a = [jnp.sum(streams[s] * out_row, axis=1, keepdims=True) for s in range(4)]
            bias_row = small_row(6 + 2 * LAYERS)
            proj_a[0] = proj_a[0] + jnp.sum(bias_row * out_row, axis=1, keepdims=True)
            await_bytes(qslot_g.at[pl.ds(0, 2 * G - 1)], s_recv.at[S_QNEAR])
            q_row = []
            for tt in range(n_t):
                total = qslot_g[(tt // 2) * B * 2 + tt % 2, 0:1]
                for i in range(1, B):
                    total = total + qslot_g[((tt // 2) * B + i) * 2 + tt % 2, 0:1]
                q_row.append(total)
            q_row = jnp.concatenate(q_row, 1)
            counted = slot_sum(qslot_g, 2 * G)[1:2, 0:1]

    last = LAYERS - 1
    proj = [
        proj_a[s] + jnp.sum(hidden[last, s].astype(F32) * q_row, axis=1, keepdims=True) for s in range(4)
    ]
    tau = proj[0]
    sign_tau = sign_of(tau)
    abs_tau = jnp.abs(tau)
    grad_time = [units[k] * abs_tau + distance * sign_tau * proj[1 + k] for k in range(3)]
    square = grad_time[0] * grad_time[0] + grad_time[1] * grad_time[1] + grad_time[2] * grad_time[2]
    error = square - truth * truth
    total_err = jnp.sum(mask * jnp.abs(error), axis=0, keepdims=True)
    seed = mask * sign_of(error)
    g_time = [2.0 * grad_time[k] * seed for k in range(3)]
    g_tau = sign_tau * (units[0] * g_time[0] + units[1] * g_time[1] + units[2] * g_time[2])
    g_proj = [g_tau] + [distance * sign_tau * g_time[k] for k in range(3)]
    v_row = jnp.sum(
        sum(hidden[last, s].astype(F32) * g_proj[s] for s in range(4)), axis=0, keepdims=True
    )
    for tt in range(n_t):
        vsend[tt % 2, tt // 2] = jnp.broadcast_to(v_row[:, tt * cw : (tt + 1) * cw], (8, cw))
    vslot_g[me_near] = vsend[c, y]
    for (o, cc), d in zip(q_coords, q_devices):
        remote(vsend.at[cc, lax.div(o, B)], vslot_g.at[me_near], s_send.at[S_VNEAR], s_recv.at[S_VNEAR], d)

    def v_far():
        await_bytes(vslot_g.at[pl.ds(0, 2 * G - 1)], s_recv.at[S_VNEAR])
        vslot_z[a] = slot_sum(vslot_g, 2 * G)
        for d in reversed(z_devices):
            remote(vslot_z.at[a], vslot_z.at[a], s_send.at[S_VFAR], s_recv.at[S_VFAR], d)

    pieces = [(far[k], k) for k in reversed(range(A - 1))] + [(a, None)]

    def start_core(m, value):
        low = value.astype(BF16)
        for tt in range(n_t):
            block = low[:, tt * cw : (tt + 1) * cw].reshape(A, B, R, cw)
            for i in range(B):
                gsend[m, tt % 2, :, (tt // 2) * B + i] = block[:, i]
        for z, _ in pieces:
            remote(gsend.at[m, 1 - c, z], gcore.at[m, z], g_send.at[0], gc_recv.at[m], core_device)

    def core_sum(m, j):
        z = pieces[j][0]
        gone[m, z] = (gsend[m, c, z].astype(F32) + gcore[m, z].astype(F32)).astype(BF16)

    def start_near(m):
        await_bytes(gcore.at[m], gc_recv.at[m])
        for j, (z, kz) in enumerate(pieces):
            core_sum(m, j)
            for k in plain_near(m, g_turned):
                remote(
                    gone.at[m, z, near[k]],
                    gslot_n.at[m, j, k],
                    g_send.at[0],
                    gn_recv.at[m, j],
                    g_devices[k],
                )
            if m in g_turned and kz is not None:
                remote(
                    gone.at[m, z, near[FARTHEST]],
                    tslot_z.at[m, kz],
                    g_send.at[0],
                    gt_recv.at[m, 0],
                    z_devices[kz],
                )

    def start_far(m):
        count_of = len(plain_near(m, g_turned))
        for j, (z, k) in enumerate(pieces):
            if count_of:
                await_bytes(gslot_n.at[m, j, pl.ds(0, count_of)], gn_recv.at[m, j])
            total = slot_sum(gslot_n.at[m, j], count_of, gone[m, z, g].astype(F32))
            if k is None:
                gown[m] = total
            else:
                gtwo[m, k] = total.astype(BF16)
                remote(gtwo.at[m, k], gslot_z.at[m, k], g_send.at[0], gz_recv.at[m], z_devices[k])

    def start_turned(m):
        if m in g_turned:
            await_bytes(tslot_z.at[m], gt_recv.at[m, 0])
            total = slot_sum(tslot_z.at[m], A - 1, gone[m, a, near[FARTHEST]].astype(F32))
            tlow[m] = total.astype(BF16)
            remote(tlow.at[m], tslot_n.at[m], g_send.at[0], gt_recv.at[m, 1], g_devices[FARTHEST])

    def finish(m):
        await_bytes(gslot_z.at[m], gz_recv.at[m])
        total = slot_sum(gslot_z.at[m], A - 1, gown[m])
        if m in g_turned:
            await_bytes(tslot_n.at[m], gt_recv.at[m, 1])
            total = total + tslot_n[m].astype(F32)
        return total

    bias_in = [None] * LAYERS
    bias_out = [None] * LAYERS

    def back_last():
        z = pre[last, 0] + small_row(7 + last)
        e = jnp.exp(jnp.minimum(z, 0.0))
        slope = jnp.where(z > 0, 1.0, e)
        curve = jnp.where(z > 0, 0.0, e)
        mixed = g_proj[1] * pre[last, 1] + g_proj[2] * pre[last, 2] + g_proj[3] * pre[last, 3]
        gz = q_row * (g_proj[0] * slope + curve * mixed)
        bias_in[last] = jnp.sum(gz, axis=0, keepdims=True)
        gpre[0] = gz.astype(BF16)
        slope = slope * q_row
        for k in range(1, 4):
            gpre[k] = (g_proj[k] * slope).astype(BF16)

    def back_out(l):
        bias_out[l] = jnp.sum(grad[0], axis=0, keepdims=True)
        gb = gbranch[...].reshape(M, D)
        start_core(2 * l + 1, tn(gb, hidden[l].reshape(M, D)))

    def back_in(l):
        gb = gbranch[...].reshape(M, D)
        gh = nn(gb, weight(2 * l + 1)).reshape(4, Pn, D)
        z = pre[l, 0] + small_row(7 + l)
        e = jnp.exp(jnp.minimum(z, 0.0))
        slope = jnp.where(z > 0, 1.0, e)
        curve = jnp.where(z > 0, 0.0, e)
        gz = gh[0] * slope + curve * (gh[1] * pre[l, 1] + gh[2] * pre[l, 2] + gh[3] * pre[l, 3])
        bias_in[l] = jnp.sum(gz, axis=0, keepdims=True)
        gpre[0] = gz.astype(BF16)
        for k in range(1, 4):
            gpre[k] = (gh[k] * slope).astype(BF16)

    def back_weight(l):
        start_core(2 * l, tn(acts[l].reshape(M, D), gpre[...].reshape(M, D)))

    def back_through(l):
        back = nt(gpre[...].reshape(M, D), weight(2 * l)).reshape(4, Pn, D)
        for s in range(4):
            value = (out_row * g_proj[s] if l == last else grad[s]) + back[s]
            grad[s] = value
            if l > 0:
                gbranch[s] = value.astype(BF16)

    back_last()
    back_weight(1)
    tau_sum = jnp.sum(g_proj[0], axis=0, keepdims=True)
    bias_out[last] = out_row * tau_sum
    g_out_row = bias_row * tau_sum + jnp.sum(
        streams[0] * g_proj[0] + streams[1] * g_proj[1] + streams[2] * g_proj[2] + streams[3] * g_proj[3],
        axis=0,
        keepdims=True,
    )
    back_through(1)
    back_out(0)
    start_near(2)
    back_in(0)
    back_weight(0)
    start_near(1)
    back_through(0)
    v_far()

    z0 = inner[...]
    e0 = jnp.exp(jnp.minimum(z0, 0.0))
    slope0 = jnp.where(z0 > 0, 1.0, e0)
    curve0 = jnp.where(z0 > 0, 0.0, e0)
    first_rows = [small_row(j) for j in range(6)]
    g_inner = grad[0] * slope0 + curve0 * (
        grad[1] * first_rows[3] + grad[2] * first_rows[4] + grad[3] * first_rows[5]
    )
    rows = [jnp.sum(xs[j] * g_inner, axis=0, keepdims=True) for j in range(6)]
    for k in range(3):
        rows[3 + k] = rows[3 + k] + jnp.sum(grad[1 + k] * slope0, axis=0, keepdims=True)
    rows.append(jnp.sum(g_inner, axis=0, keepdims=True))
    rows = rows + bias_in + bias_out + [g_out_row]

    lanes = lax.broadcasted_iota(jnp.int32, (1, cw), 1)
    weight_sq = jnp.zeros((1, cw), F32)
    for m in range(MATS):
        part = jnp.sum(master[m // 2, m % 2] * master[m // 2, m % 2], keepdims=True)
        weight_sq = jnp.where(lanes == m, part, weight_sq)
    own_small = spbuf[t]
    weight_sq = jnp.where(lanes == MATS, jnp.sum(own_small * own_small, keepdims=True) / (A * B), weight_sq)
    tail = [
        jnp.broadcast_to(total_err, (1, cw)),
        weight_sq,
        jnp.zeros((2, cw), F32),
    ]
    for tt in range(n_t):
        sgsend[tt % 2, tt // 2] = jnp.concatenate([r[:, tt * cw : (tt + 1) * cw] for r in rows] + tail, 0)
    sgslot_g[me_near] = sgsend[c, y]
    for (o, cc), d in zip(q_coords, q_devices):
        remote(sgsend.at[cc, lax.div(o, B)], sgslot_g.at[me_near], s_send.at[S_NEAR], s_recv.at[S_NEAR], d)
    start_near(0)

    for copy in local[7:]:
        copy.wait()
    tile_rows = lax.broadcasted_iota(jnp.int32, (8, 128), 0)

    def step(gradient, momentum):
        new = momentum_coef * momentum + gradient
        return new, gradient + momentum_coef * new

    def settle(m, total):
        at = (m // 2, m % 2)
        gr = total / counted
        new, direction = step(gr, moment[at])
        grad_b[at] = gr
        moment_b[at] = new
        return jnp.where(tile_rows == m, jnp.sum(direction * direction, keepdims=True), 0.0)

    start_far(2)
    start_turned(2)
    start_far(1)
    start_turned(1)

    await_bytes(vslot_z.at[fars], s_recv.at[S_VFAR])
    v_part = slot_sum(vslot_z, A)[0:1]
    product = jnp.sum(last_low * v_part, axis=1, keepdims=True)
    place = lax.broadcasted_iota(jnp.int32, (R, cw), 1) - lax.broadcasted_iota(jnp.int32, (R, cw), 0)
    product_row = jnp.sum(jnp.where(place == (dp * R) % cw, product, 0.0), axis=0, keepdims=True)
    psend[...] = jnp.broadcast_to(product_row, (8, cw))
    column = (dp * R) // cw
    mine_too = column == t
    slot = (dp % (cw // R)) * n_t + t
    pl.semaphore_wait(barrier, len(others))
    for k in reversed(range(1, A * B)):
        remote(
            psend, pslot.at[slot], s_send.at[S_PROD], s_recv.at[S_PROD], (in_dp[k], column)
        )

    @pl.when(mine_too)
    def _():
        pslot[slot] = psend[...]

    @pl.when(jnp.logical_not(mine_too))
    def _():
        remote(psend, pslot.at[slot], s_send.at[S_PROD], s_recv.at[S_PROD], (dp, column))

    def await_products(wait, ref, count_of, sems):
        @pl.when(mine_too)
        def _():
            wait(ref.at[pl.ds(0, count_of - 1)], sems.at[S_PROD])

        @pl.when(jnp.logical_not(mine_too))
        def _():
            wait(ref.at[pl.ds(0, count_of)], sems.at[S_PROD])

    start_far(0)
    start_turned(0)
    await_bytes(sgslot_g.at[pl.ds(0, 2 * G - 1)], s_recv.at[S_NEAR])
    sgtwo[...] = slot_sum(sgslot_g, 2 * G)
    sgslot_z[a] = sgtwo[...]
    for d in reversed(z_devices):
        remote(sgtwo, sgslot_z.at[a], s_send.at[S_FAR], s_recv.at[S_FAR], d)

    parts = settle(MATS - 1, out_column * v_part)
    for m in (2, 1, 0):
        parts = parts + settle(m, finish(m))
    slots = (cw // R) * n_t
    await_products(await_bytes, pslot, slots, s_recv)
    await_bytes(sgslot_z.at[fars], s_recv.at[S_FAR])
    sred[...] = slot_sum(sgslot_z, A)
    head_row = sred[SMALL - 1 : SMALL]
    for i in range(slots):
        head_row = head_row + pslot[i, 0:1]
    sred[SMALL - 1 : SMALL] = head_row
    gr = sred[0:SMALL, :] / counted
    new, dir_small = step(gr, msmall[...])
    grad_s[...] = gr
    moment_s[...] = new
    parts = parts + jnp.where(
        tile_rows == MATS, jnp.sum(dir_small * dir_small, keepdims=True) / (A * B), 0.0
    )
    me = (a * G + g) * 2 + c
    arslot[me] = parts
    for d in everyone:
        remote(arslot.at[me], arslot.at[me], s_send.at[S_ALL], s_recv.at[S_ALL], d)
    loss_b[...] = sred[SMALL : SMALL + 1, 0:1] / counted
    bias_b[...] = grad_s[7 : 7 + 2 * LAYERS, :]
    await_bytes(arslot.at[pl.ds(0, len(everyone))], s_recv.at[S_ALL])
    dir_sq = jnp.sum(arslot[...], axis=0)

    def rate_of(m):
        size = sred[SMALL + 1 : SMALL + 2, m : m + 1]
        return spread_rate * jnp.sqrt(size) / jnp.sqrt(dir_sq[m : m + 1, 0:1] + norm_epsilon)

    for m in range(MATS):
        at = (m // 2, m % 2)
        direction = grad_b[at] + momentum_coef * moment_b[at]
        new = master[at] - rate_of(m) * direction
        master_b[at] = new
        average_b[at] = average_decay * average[at] + (1.0 - average_decay) * new
        low_b[at] = new.astype(BF16)
    new = own_small - rate_of(MATS) * dir_small
    master_s[...] = new
    average_s[...] = average_decay * asmall[...] + (1.0 - average_decay) * new

    n_w, n_g = len(w_turned), len(g_turned)
    gathered = MOVED * (A - 1 + G - 1 + A * G) + (A - 1) * (MOVED * (G - 1) - n_w) + n_w * (A - 1)
    scattered = MOVED * (A - 1 + A * G) + A * (MOVED * (G - 1) - n_g) + n_g * A
    await_sent(sized.at[pl.ds(0, gathered)], w_send.at[0])
    await_sent(sized.at[pl.ds(0, scattered)], g_send.at[0])
    await_sent(qslot_z.at[fars], s_send.at[S_QFAR])
    await_sent(vslot_z.at[fars], s_send.at[S_VFAR])
    await_sent(qslot_g.at[pl.ds(0, 2 * G - 1)], s_send.at[S_QNEAR])
    await_sent(vslot_g.at[pl.ds(0, 2 * G - 1)], s_send.at[S_VNEAR])
    await_sent(sgslot_g.at[pl.ds(0, 2 * G - 1)], s_send.at[S_NEAR])
    await_products(await_sent, pdone, A * B, s_send)
    await_sent(sgslot_z.at[fars], s_send.at[S_FAR])
    await_sent(arslot.at[pl.ds(0, len(everyone))], s_send.at[S_ALL])
    await_sent(spbuf.at[pl.ds(0, n_t - 1)], s_send.at[S_PAR])


def write_out(*refs):
    sems = refs[-1]
    count = (len(refs) - 1) // 2
    copies = [
        pltpu.make_async_copy(refs[i], refs[count + i], sems.at[i]) for i in range(count)
    ]
    for copy in copies:
        copy.start()
    for copy in copies:
        copy.wait()


def body(
    axes,
    coords,
    model_ids,
    cells,
    valid,
    slowness_grid,
    master_blocks,
    small_params,
    moment_blocks,
    moment_small,
    average_blocks,
    average_small,
):
    n_dp, n_t = axes
    A = 4 if n_dp % 4 == 0 else n_dp
    B = n_dp // A
    C = n_t // 2
    G = C * B
    R, cw = master_blocks.shape[2:]
    D = R * n_dp
    PB = coords.shape[1]
    Pn = PB // n_t
    dims = (A, B, C, R, cw, Pn, D)
    anywhere = pl.BlockSpec(memory_space=pltpu.HBM)
    vmem = pl.BlockSpec(memory_space=pltpu.VMEM)
    S = SMALL + 4
    args = (
        coords,
        model_ids,
        cells,
        valid,
        slowness_grid,
        master_blocks,
        small_params,
        moment_blocks,
        moment_small,
        average_blocks,
        average_small,
    )
    V = pltpu.VMEM
    DMA = pltpu.SemaphoreType.DMA
    block = (master_blocks.shape, F32)
    short = (small_params.shape, F32)
    shapes = [
        ((1, 1), F32),
        block,
        short,
        ((2 * LAYERS, cw), F32),
        block,
        short,
        block,
        short,
        block,
        short,
        (master_blocks.shape, BF16),
    ]
    results = pl.pallas_call(
        functools.partial(kernel, dims),
        out_shape=tuple(V(*shape) for shape in shapes),
        in_specs=[anywhere] * len(args),
        out_specs=(vmem,) * len(shapes),
        scratch_shapes=[
            V(coords.shape, F32),
            V((PB,), jnp.int32),
            V((PB,), jnp.int32),
            V((PB,), jnp.int32),
            V(slowness_grid.shape, F32),
            V(master_blocks.shape, F32),
            V(master_blocks.shape, F32),
            V(small_params.shape, F32),
            V(master_blocks.shape, F32),
            V(small_params.shape, F32),
            V((n_t, SMALL, cw), F32),
            V((PB, 128), F32),
            V((S, cw), F32),
            V((MOVED, 2, C, A, B, R, cw), BF16),
            V((4, Pn, D), F32),
            V((LAYERS, 4, Pn, D), BF16),
            V((LAYERS, 4, Pn, D), F32),
            V((LAYERS, 4, Pn, D), BF16),
            V((4, Pn, D), F32),
            V((4, Pn, D), BF16),
            V((4, Pn, D), BF16),
            V((Pn, D), F32),
            V((MOVED, 2, A, G, R, cw), BF16),
            V((MOVED, A, G, R, cw), BF16),
            V((MOVED, A, G, R, cw), BF16),
            V((MOVED, A, G - 1, R, cw), BF16),
            V((MOVED, A - 1, R, cw), BF16),
            V((MOVED, A - 1, R, cw), BF16),
            V((MOVED, R, cw), F32),
            V((MOVED, A - 1, R, cw), BF16),
            V((MOVED, R, cw), BF16),
            V((MOVED, R, cw), BF16),
            V((2, C, S, cw), F32),
            V((8, cw), F32),
            V(((cw // R) * n_t, 8, cw), F32),
            V((n_dp, 8, cw), F32),
            V((MOVED * A * (2 * G + 1), R, cw), BF16),
            V((2 * G, S, cw), F32),
            V((S, cw), F32),
            V((A, S, cw), F32),
            V((2 * A * G, 8, 128), F32),
            V((A, 8, cw), F32),
            V((2 * G, 8, cw), F32),
            V((2, C, 8, cw), F32),
            V((2 * G, 8, cw), F32),
            V((A, 8, cw), F32),
            pltpu.SemaphoreType.DMA((len(args),)),
            DMA((1,)),
            DMA((MOVED, A - 1)),
            DMA((MOVED, G - 1)),
            DMA((MOVED,)),
            DMA((MOVED,)),
            DMA((1,)),
            DMA((MOVED,)),
            DMA((MOVED, A)),
            DMA((MOVED, 2)),
            DMA((MOVED,)),
            DMA((9,)),
            DMA((9,)),
        ],
        compiler_params=pltpu.CompilerParams(
            collective_id=0, has_side_effects=True, vmem_limit_bytes=60 << 20
        ),
    )(*args)

    results = pl.pallas_call(
        write_out,
        out_shape=tuple(jax.ShapeDtypeStruct(*shape) for shape in shapes),
        in_specs=[vmem] * len(shapes),
        out_specs=(anywhere,) * len(shapes),
        scratch_shapes=[pltpu.SemaphoreType.DMA((len(shapes),))],
        compiler_params=pltpu.CompilerParams(vmem_limit_bytes=4 << 20),
    )(*results)
    return (results[0].reshape(()),) + tuple(results[1:])


def solution(mesh):
    blocks = P(None, None, "dp", "tensor")
    small = P(None, "tensor")
    in_specs = (
        P(None, "dp"),
        P("dp"),
        P("dp"),
        P("dp"),
        P(),
        blocks,
        small,
        blocks,
        small,
        blocks,
        small,
    )
    out_specs = (P(), blocks, small, small, blocks, small, blocks, small, blocks, small, blocks)
    axes = (mesh.shape["dp"], mesh.shape["tensor"])
    return jax.shard_map(
        functools.partial(body, axes), mesh=mesh, in_specs=in_specs, out_specs=out_specs, check_vma=False
    )
```

```python
import functools

import jax
import jax.numpy as jnp
from jax import lax
from jax.experimental import pallas as pl
from jax.experimental.pallas import tpu as pltpu
from jax.sharding import PartitionSpec as P

LAYERS = 2
MATS = 2 * LAYERS
SMALL = 12
MESH = pl.DeviceIdType.MESH
F32 = jnp.float32
BF16 = jnp.bfloat16

momentum_coef = 0.5
average_decay = 0.5
spread_rate = 0.5
norm_epsilon = 1e-12

MOVED = MATS - 1
W_TURNED = (0, 1)
G_TURNED = (2, 1, 0)


def partners(i, size):
    values, bit = [i], 1
    while bit < size:
        change = bit - 2 * bit * lax.rem(lax.div(i, bit), 2)
        values = values + [value + change for value in values]
        bit *= 2
    return values


def nn(left, right):
    return lax.dot_general(left, right, (((1,), (0,)), ((), ())), preferred_element_type=F32)


def nt(left, right):
    return lax.dot_general(left, right, (((1,), (1,)), ((), ())), preferred_element_type=F32)


def tn(left, right):
    return lax.dot_general(left, right, (((0,), (0,)), ((), ())), preferred_element_type=F32)


def sign_of(v):
    return jnp.where(v > 0, 1.0, jnp.where(v < 0, -1.0, 0.0))


def kernel(
    dims,
    coords_hbm,
    model_hbm,
    cells_hbm,
    valid_hbm,
    grid_hbm,
    master_hbm,
    small_hbm,
    moment_hbm,
    msmall_hbm,
    average_hbm,
    asmall_hbm,
    loss_b,
    grad_b,
    grad_s,
    bias_b,
    moment_b,
    moment_s,
    master_b,
    master_s,
    average_b,
    average_s,
    low_b,
    coords,
    model,
    cells,
    valid,
    grid,
    master,
    moment,
    msmall,
    average,
    asmall,
    spbuf,
    columns,
    sred,
    wbuf,
    streams,
    acts,
    pre,
    hidden,
    grad,
    gbranch,
    gpre,
    inner,
    gsend,
    gcore,
    gone,
    gslot_n,
    gtwo,
    gslot_z,
    gown,
    tslot_z,
    tlow,
    tslot_n,
    sgsend,
    psend,
    pslot,
    pdone,
    sized,
    sgslot_g,
    sgtwo,
    sgslot_z,
    arslot,
    qslot_z,
    qslot_g,
    vsend,
    vslot_g,
    vslot_z,
    in_sem,
    w_send,
    wz_recv,
    wn_recv,
    wt_recv,
    wc_recv,
    g_send,
    gz_recv,
    gn_recv,
    gt_recv,
    gc_recv,
    s_send,
    s_recv,
):
    A, B, C, R, cw, Pn, D = dims
    n_t = 2 * C
    G = C * B
    dp = lax.axis_index("dp")
    t = lax.axis_index("tensor")
    a, b = lax.div(dp, B), lax.rem(dp, B)
    y, c = lax.div(t, 2), lax.rem(t, 2)
    g = y * B + b
    in_a, in_g, in_c, in_dp = partners(a, A), partners(g, G), partners(c, 2), partners(dp, A * B)

    def device(a_, g_, c_):
        return (a_ * B + lax.rem(g_, B), lax.div(g_, B) * 2 + c_)

    far = [in_a[k] for k in range(1, A)]
    near = [in_g[k] for k in range(1, G)]
    z_devices = [device(o, g, c) for o in far]
    g_devices = [device(a, o, c) for o in near]
    core_device = device(a, g, 1 - c)
    q_steps = [(kg, kc) for kg in range(G) for kc in range(2)][1:]
    q_steps.sort(key=lambda step: -(bin(step[0]).count("1") + step[1] / 2))
    q_coords = [(in_g[kg], in_c[kc]) for kg, kc in q_steps]
    q_devices = [device(a, o, cc) for o, cc in q_coords]
    steps = [(ka, kg, kc) for ka in range(A) for kg in range(G) for kc in range(2)][1:]
    steps.sort(key=lambda step: -(step[0] + bin(step[1]).count("1") + step[2] / 2))
    everyone = [device(in_a[ka], in_g[kg], in_c[kc]) for ka, kg, kc in steps]
    others = [d for d, step in zip(everyone, steps) if step[0] and (step[1] or step[2])]

    FARTHEST = G - 2
    w_turned = W_TURNED if G > 2 else ()
    g_turned = G_TURNED if G > 2 else ()

    def plain_near(m, turned):
        return range(G - 2 if m in turned else G - 1)

    S_PROD, S_NEAR, S_FAR, S_ALL, S_PAR, S_QFAR, S_QNEAR, S_VNEAR, S_VFAR = range(9)

    def remote(src, dst, ssem, rsem, device_id):
        copy = pltpu.make_async_remote_copy(
            src_ref=src,
            dst_ref=dst,
            send_sem=ssem,
            recv_sem=rsem,
            device_id=device_id,
            device_id_type=MESH,
        )
        copy.start()
        return copy

    def arrived(copies):
        for copy in copies:
            copy.wait_recv()

    nears, fars = pl.ds(0, G - 1), pl.ds(0, A - 1)

    local = []
    for i, (src, dst) in enumerate(
        [
            (master_hbm, master),
            (small_hbm, spbuf.at[t]),
            (coords_hbm, coords),
            (model_hbm, model),
            (cells_hbm, cells),
            (valid_hbm, valid),
            (grid_hbm, grid),
            (moment_hbm, moment),
            (msmall_hbm, msmall),
            (average_hbm, average),
            (asmall_hbm, asmall),
        ]
    ):
        copy = pltpu.make_async_copy(src, dst, in_sem.at[i])
        copy.start()
        local.append(copy)

    barrier = pltpu.get_barrier_semaphore()
    peers = z_devices + q_devices
    for d in peers:
        pl.semaphore_signal(barrier, inc=1, device_id=d, device_id_type=MESH)

    local[0].wait()
    for m in range(MOVED):
        wbuf[m, c, y, a, b] = master[m // 2, m % 2].astype(BF16)
    local[1].wait()
    pl.semaphore_wait(barrier, len(peers))

    def piece(m, o, z):
        return wbuf.at[m, c, lax.div(o, B), z, lax.rem(o, B)]

    def line(m, o):
        return wbuf.at[m, c, lax.div(o, B), :, lax.rem(o, B)]

    def plane(m, z):
        return wbuf.at[m, c, :, z]

    def await_bytes(ref, rsem):
        pltpu.make_async_remote_copy(
            src_ref=ref,
            dst_ref=ref,
            send_sem=s_send.at[0],
            recv_sem=rsem,
            device_id=core_device,
            device_id_type=MESH,
        ).wait_recv()

    def slot_sum(ref, count_of, value=None):
        for i in range(count_of):
            term = ref[i].astype(F32)
            value = term if value is None else value + term
        return value

    def await_sent(ref, ssem):
        pltpu.make_async_remote_copy(
            src_ref=ref,
            dst_ref=ref,
            send_sem=ssem,
            recv_sem=s_recv.at[0],
            device_id=core_device,
            device_id_type=MESH,
        ).wait_send()

    def w_far(m, ref):
        return [
            remote(ref, ref, w_send.at[0], wz_recv.at[m, k], z_devices[k]) for k in reversed(range(A - 1))
        ][::-1]

    def w_near(m, ref, ks):
        for k in ks:
            remote(ref, ref, w_send.at[0], wn_recv.at[m, k], g_devices[k])

    def w_core(m, ref):
        remote(ref, ref, w_send.at[0], wc_recv.at[m], core_device)

    for k in range(1, n_t):
        o = (t + k) % n_t
        remote(spbuf.at[t], spbuf.at[t], s_send.at[S_PAR], s_recv.at[S_PAR], (dp, o))
    first = {}
    for m in range(MOVED):
        first[m] = w_far(m, piece(m, g, a))
        w_near(m, piece(m, g, a), reversed(range(G - 1)))

    for copy in local[2:7]:
        copy.wait()
    cols = grid.shape[2]
    shift = (cols - 1).bit_length()
    cell = cells[...].reshape(1, -1)
    row_id = model[...].reshape(1, -1) * grid.shape[1] + (cell >> shift)
    col_id = cell & (cols - 1)
    PB = row_id.shape[1]
    packed = jnp.concatenate(
        [
            coords[...],
            row_id.astype(F32),
            col_id.astype(F32),
            valid[...].reshape(1, -1).astype(F32),
            jnp.zeros((128 - 9, PB), F32),
        ],
        0,
    )
    columns[...] = packed.T
    mine = columns[pl.ds(pl.multiple_of(t * Pn, 8), Pn), :]
    xs = [mine[:, j : j + 1] for j in range(6)]
    mask = mine[:, 8:9]
    row_of = mine[:, 6:7].astype(jnp.int32)
    col_of = mine[:, 7:8].astype(jnp.int32)
    table = grid[...].reshape(-1, cols)
    onehot = (
        lax.broadcasted_iota(jnp.int32, (Pn, table.shape[0]), 1) == row_of
    ).astype(BF16)
    high = table.astype(BF16)
    rest = table - high.astype(F32)
    middle = rest.astype(BF16)
    lowest = (rest - middle.astype(F32)).astype(BF16)
    picked = nn(onehot, high) + nn(onehot, middle) + nn(onehot, lowest)
    lane = lax.broadcasted_iota(jnp.int32, (Pn, cols), 1)
    truth = jnp.sum(jnp.where(lane == col_of, picked, 0.0), 1, keepdims=True)
    seps = [xs[3 + k] - xs[k] for k in range(3)]
    distance = jnp.sqrt(seps[0] * seps[0] + seps[1] * seps[1] + seps[2] * seps[2])
    units = [s / distance for s in seps]

    await_bytes(spbuf.at[pl.ds(0, n_t - 1)], s_recv.at[S_PAR])

    def small_row(i):
        return jnp.concatenate([spbuf[tt, i : i + 1, :] for tt in range(n_t)], 1)

    out_row = small_row(7 + 2 * LAYERS)
    last_low = master[LAYERS - 1, 1].astype(BF16).astype(F32)
    feature = lax.broadcasted_iota(jnp.int32, (R, D), 1) - lax.broadcasted_iota(jnp.int32, (R, D), 0)
    out_column = jnp.sum(jnp.where(feature == dp * R, out_row, 0.0), axis=1, keepdims=True)
    q_part = jnp.sum(last_low * out_column, axis=0, keepdims=True)
    count = jnp.sum(mask, axis=0, keepdims=True)
    row_of_8 = lax.broadcasted_iota(jnp.int32, (8, cw), 0)
    qslot_z[a] = jnp.where(row_of_8 == 0, q_part, count)
    for d in reversed(z_devices):
        remote(qslot_z.at[a], qslot_z.at[a], s_send.at[S_QFAR], s_recv.at[S_QFAR], d)

    first_rows = [small_row(j) for j in range(6)]
    z0 = small_row(6) + xs[0] * first_rows[0]
    for j in range(1, 6):
        z0 = z0 + xs[j] * first_rows[j]
    inner[...] = z0
    e0 = jnp.exp(jnp.minimum(z0, 0.0))
    slope0 = jnp.where(z0 > 0, 1.0, e0)
    streams[0] = jnp.where(z0 > 0, z0, e0 - 1.0)
    acts[0, 0] = streams[0].astype(BF16)
    for k in range(3):
        streams[1 + k] = slope0 * first_rows[3 + k]
        acts[0, 1 + k] = streams[1 + k].astype(BF16)

    def pass_on(m):
        for k in range(A - 1):
            first[m][k].wait_recv()
            w_near(m, piece(m, g, far[k]), plain_near(m, w_turned))
        w_core(m, line(m, g))
        if m in w_turned:
            o = near[FARTHEST]
            ref = piece(m, o, a)
            await_bytes(ref, wn_recv.at[m, FARTHEST])
            for d in reversed(z_devices):
                remote(ref, ref, w_send.at[0], wt_recv.at[m], d)

    for m in range(MOVED):
        pass_on(m)
    me_near = g * 2 + c
    await_bytes(qslot_z.at[fars], s_recv.at[S_QFAR])
    qslot_g[me_near] = slot_sum(qslot_z, A)
    for d in q_devices:
        remote(qslot_g.at[me_near], qslot_g.at[me_near], s_send.at[S_QNEAR], s_recv.at[S_QNEAR], d)

    def weight(m):
        return jnp.concatenate([wbuf[m, tt % 2, tt // 2].reshape(D, cw) for tt in range(n_t)], 1)

    M = 4 * Pn

    def block_in(l):
        pre[l] = nn(acts[l].reshape(M, D), weight(2 * l)).reshape(4, Pn, D)
        z = pre[l, 0] + small_row(7 + l)
        e = jnp.exp(jnp.minimum(z, 0.0))
        slope = jnp.where(z > 0, 1.0, e)
        hidden[l, 0] = jnp.where(z > 0, z, e - 1.0).astype(BF16)
        for k in range(1, 4):
            hidden[l, k] = (slope * pre[l, k]).astype(BF16)

    def block_out(l):
        branch = nt(hidden[l].reshape(M, D), weight(2 * l + 1)).reshape(4, Pn, D)
        for s in range(4):
            new = streams[s] + branch[s]
            if s == 0:
                new = new + small_row(7 + LAYERS + l)
            streams[s] = new
            if l + 1 < LAYERS:
                acts[l + 1, s] = new.astype(BF16)

    def fetch(m):
        for k in range(G - 1):
            if m in w_turned and k == FARTHEST:
                await_bytes(wbuf.at[m, c, 0, fars, 0], wt_recv.at[m])
            else:
                await_bytes(line(m, near[k]), wn_recv.at[m, k])
            w_core(m, line(m, near[k]))

    def fetched(m):
        await_bytes(wbuf.at[m, c], wc_recv.at[m])

    for m in range(MOVED):
        fetch(m)
        fetched(m)
        if m == 0:
            for d in others:
                pl.semaphore_signal(barrier, inc=1, device_id=d, device_id_type=MESH)
        if m % 2 == 0:
            block_in(m // 2)
        else:
            block_out(m // 2)
        if m == MOVED - 2:
            proj_a = [jnp.sum(streams[s] * out_row, axis=1, keepdims=True) for s in range(4)]
            bias_row = small_row(6 + 2 * LAYERS)
            proj_a[0] = proj_a[0] + jnp.sum(bias_row * out_row, axis=1, keepdims=True)
            await_bytes(qslot_g.at[pl.ds(0, 2 * G - 1)], s_recv.at[S_QNEAR])
            q_row = []
            for tt in range(n_t):
                total = qslot_g[(tt // 2) * B * 2 + tt % 2, 0:1]
                for i in range(1, B):
                    total = total + qslot_g[((tt // 2) * B + i) * 2 + tt % 2, 0:1]
                q_row.append(total)
            q_row = jnp.concatenate(q_row, 1)
            counted = slot_sum(qslot_g, 2 * G)[1:2, 0:1]

    last = LAYERS - 1
    proj = [
        proj_a[s] + jnp.sum(hidden[last, s].astype(F32) * q_row, axis=1, keepdims=True) for s in range(4)
    ]
    tau = proj[0]
    sign_tau = sign_of(tau)
    abs_tau = jnp.abs(tau)
    grad_time = [units[k] * abs_tau + distance * sign_tau * proj[1 + k] for k in range(3)]
    square = grad_time[0] * grad_time[0] + grad_time[1] * grad_time[1] + grad_time[2] * grad_time[2]
    error = square - truth * truth
    total_err = jnp.sum(mask * jnp.abs(error), axis=0, keepdims=True)
    seed = mask * sign_of(error)
    g_time = [2.0 * grad_time[k] * seed for k in range(3)]
    g_tau = sign_tau * (units[0] * g_time[0] + units[1] * g_time[1] + units[2] * g_time[2])
    g_proj = [g_tau] + [distance * sign_tau * g_time[k] for k in range(3)]
    def v_far():
        await_bytes(vslot_g.at[pl.ds(0, 2 * G - 1)], s_recv.at[S_VNEAR])
        vslot_z[a] = slot_sum(vslot_g, 2 * G)
        for d in reversed(z_devices):
            remote(vslot_z.at[a], vslot_z.at[a], s_send.at[S_VFAR], s_recv.at[S_VFAR], d)

    pieces = [(far[k], k) for k in reversed(range(A - 1))] + [(a, None)]

    def start_core(m, value):
        low = value.astype(BF16)
        for tt in range(n_t):
            block = low[:, tt * cw : (tt + 1) * cw].reshape(A, B, R, cw)
            for i in range(B):
                gsend[m, tt % 2, :, (tt // 2) * B + i] = block[:, i]
        for z, _ in pieces:
            remote(gsend.at[m, 1 - c, z], gcore.at[m, z], g_send.at[0], gc_recv.at[m], core_device)

    def core_sum(m, j):
        z = pieces[j][0]
        gone[m, z] = (gsend[m, c, z].astype(F32) + gcore[m, z].astype(F32)).astype(BF16)

    def start_near(m):
        await_bytes(gcore.at[m], gc_recv.at[m])
        for j, (z, kz) in enumerate(pieces):
            core_sum(m, j)
            for k in plain_near(m, g_turned):
                remote(
                    gone.at[m, z, near[k]],
                    gslot_n.at[m, j, k],
                    g_send.at[0],
                    gn_recv.at[m, j],
                    g_devices[k],
                )
            if m in g_turned and kz is not None:
                remote(
                    gone.at[m, z, near[FARTHEST]],
                    tslot_z.at[m, kz],
                    g_send.at[0],
                    gt_recv.at[m, 0],
                    z_devices[kz],
                )

    def start_far(m):
        count_of = len(plain_near(m, g_turned))
        for j, (z, k) in enumerate(pieces):
            if count_of:
                await_bytes(gslot_n.at[m, j, pl.ds(0, count_of)], gn_recv.at[m, j])
            total = slot_sum(gslot_n.at[m, j], count_of, gone[m, z, g].astype(F32))
            if k is None:
                gown[m] = total
            else:
                gtwo[m, k] = total.astype(BF16)
                remote(gtwo.at[m, k], gslot_z.at[m, k], g_send.at[0], gz_recv.at[m], z_devices[k])

    def start_turned(m):
        if m in g_turned:
            await_bytes(tslot_z.at[m], gt_recv.at[m, 0])
            total = slot_sum(tslot_z.at[m], A - 1, gone[m, a, near[FARTHEST]].astype(F32))
            tlow[m] = total.astype(BF16)
            remote(tlow.at[m], tslot_n.at[m], g_send.at[0], gt_recv.at[m, 1], g_devices[FARTHEST])

    def finish(m):
        await_bytes(gslot_z.at[m], gz_recv.at[m])
        total = slot_sum(gslot_z.at[m], A - 1, gown[m])
        if m in g_turned:
            await_bytes(tslot_n.at[m], gt_recv.at[m, 1])
            total = total + tslot_n[m].astype(F32)
        return total

    bias_in = [None] * LAYERS
    bias_out = [None] * LAYERS

    def back_last():
        z = pre[last, 0] + small_row(7 + last)
        e = jnp.exp(jnp.minimum(z, 0.0))
        slope = jnp.where(z > 0, 1.0, e)
        curve = jnp.where(z > 0, 0.0, e)
        mixed = g_proj[1] * pre[last, 1] + g_proj[2] * pre[last, 2] + g_proj[3] * pre[last, 3]
        gz = q_row * (g_proj[0] * slope + curve * mixed)
        bias_in[last] = jnp.sum(gz, axis=0, keepdims=True)
        gpre[0] = gz.astype(BF16)
        slope = slope * q_row
        for k in range(1, 4):
            gpre[k] = (g_proj[k] * slope).astype(BF16)

    def back_out(l):
        bias_out[l] = jnp.sum(grad[0], axis=0, keepdims=True)
        gb = gbranch[...].reshape(M, D)
        start_core(2 * l + 1, tn(gb, hidden[l].reshape(M, D)))

    def back_in(l):
        gb = gbranch[...].reshape(M, D)
        gh = nn(gb, weight(2 * l + 1)).reshape(4, Pn, D)
        z = pre[l, 0] + small_row(7 + l)
        e = jnp.exp(jnp.minimum(z, 0.0))
        slope = jnp.where(z > 0, 1.0, e)
        curve = jnp.where(z > 0, 0.0, e)
        gz = gh[0] * slope + curve * (gh[1] * pre[l, 1] + gh[2] * pre[l, 2] + gh[3] * pre[l, 3])
        bias_in[l] = jnp.sum(gz, axis=0, keepdims=True)
        gpre[0] = gz.astype(BF16)
        for k in range(1, 4):
            gpre[k] = (gh[k] * slope).astype(BF16)

    def back_weight(l):
        start_core(2 * l, tn(acts[l].reshape(M, D), gpre[...].reshape(M, D)))

    def back_through(l):
        back = nt(gpre[...].reshape(M, D), weight(2 * l)).reshape(4, Pn, D)
        for s in range(4):
            value = (out_row * g_proj[s] if l == last else grad[s]) + back[s]
            grad[s] = value
            if l > 0:
                gbranch[s] = value.astype(BF16)

    back_last()
    back_weight(1)
    v_row = jnp.sum(
        sum(hidden[last, s].astype(F32) * g_proj[s] for s in range(4)), axis=0, keepdims=True
    )
    for tt in range(n_t):
        vsend[tt % 2, tt // 2] = jnp.broadcast_to(v_row[:, tt * cw : (tt + 1) * cw], (8, cw))
    vslot_g[me_near] = vsend[c, y]
    for (o, cc), d in zip(q_coords, q_devices):
        remote(vsend.at[cc, lax.div(o, B)], vslot_g.at[me_near], s_send.at[S_VNEAR], s_recv.at[S_VNEAR], d)

    tau_sum = jnp.sum(g_proj[0], axis=0, keepdims=True)
    bias_out[last] = out_row * tau_sum
    g_out_row = bias_row * tau_sum + jnp.sum(
        streams[0] * g_proj[0] + streams[1] * g_proj[1] + streams[2] * g_proj[2] + streams[3] * g_proj[3],
        axis=0,
        keepdims=True,
    )
    back_through(1)
    back_out(0)
    start_near(2)
    back_in(0)
    back_weight(0)
    start_near(1)
    back_through(0)
    v_far()

    z0 = inner[...]
    e0 = jnp.exp(jnp.minimum(z0, 0.0))
    slope0 = jnp.where(z0 > 0, 1.0, e0)
    curve0 = jnp.where(z0 > 0, 0.0, e0)
    first_rows = [small_row(j) for j in range(6)]
    g_inner = grad[0] * slope0 + curve0 * (
        grad[1] * first_rows[3] + grad[2] * first_rows[4] + grad[3] * first_rows[5]
    )
    rows = [jnp.sum(xs[j] * g_inner, axis=0, keepdims=True) for j in range(6)]
    for k in range(3):
        rows[3 + k] = rows[3 + k] + jnp.sum(grad[1 + k] * slope0, axis=0, keepdims=True)
    rows.append(jnp.sum(g_inner, axis=0, keepdims=True))
    rows = rows + bias_in + bias_out + [g_out_row]

    lanes = lax.broadcasted_iota(jnp.int32, (1, cw), 1)
    weight_sq = jnp.zeros((1, cw), F32)
    for m in range(MATS):
        part = jnp.sum(master[m // 2, m % 2] * master[m // 2, m % 2], keepdims=True)
        weight_sq = jnp.where(lanes == m, part, weight_sq)
    own_small = spbuf[t]
    weight_sq = jnp.where(lanes == MATS, jnp.sum(own_small * own_small, keepdims=True) / (A * B), weight_sq)
    tail = [
        jnp.broadcast_to(total_err, (1, cw)),
        weight_sq,
        jnp.zeros((2, cw), F32),
    ]
    for tt in range(n_t):
        sgsend[tt % 2, tt // 2] = jnp.concatenate([r[:, tt * cw : (tt + 1) * cw] for r in rows] + tail, 0)
    sgslot_g[me_near] = sgsend[c, y]
    for (o, cc), d in zip(q_coords, q_devices):
        remote(sgsend.at[cc, lax.div(o, B)], sgslot_g.at[me_near], s_send.at[S_NEAR], s_recv.at[S_NEAR], d)
    start_near(0)

    for copy in local[7:]:
        copy.wait()
    tile_rows = lax.broadcasted_iota(jnp.int32, (8, 128), 0)

    def step(gradient, momentum):
        new = momentum_coef * momentum + gradient
        return new, gradient + momentum_coef * new

    def settle(m, total):
        at = (m // 2, m % 2)
        gr = total / counted
        new, direction = step(gr, moment[at])
        grad_b[at] = gr
        moment_b[at] = new
        return jnp.where(tile_rows == m, jnp.sum(direction * direction, keepdims=True), 0.0)

    start_far(2)
    start_turned(2)
    start_far(1)
    start_turned(1)

    await_bytes(vslot_z.at[fars], s_recv.at[S_VFAR])
    v_part = slot_sum(vslot_z, A)[0:1]
    product = jnp.sum(last_low * v_part, axis=1, keepdims=True)
    place = lax.broadcasted_iota(jnp.int32, (R, cw), 1) - lax.broadcasted_iota(jnp.int32, (R, cw), 0)
    product_row = jnp.sum(jnp.where(place == (dp * R) % cw, product, 0.0), axis=0, keepdims=True)
    psend[...] = jnp.broadcast_to(product_row, (8, cw))
    column = (dp * R) // cw
    mine_too = column == t
    slot = (dp % (cw // R)) * n_t + t
    pl.semaphore_wait(barrier, len(others))
    for k in reversed(range(1, A * B)):
        remote(
            psend, pslot.at[slot], s_send.at[S_PROD], s_recv.at[S_PROD], (in_dp[k], column)
        )

    @pl.when(mine_too)
    def _():
        pslot[slot] = psend[...]

    @pl.when(jnp.logical_not(mine_too))
    def _():
        remote(psend, pslot.at[slot], s_send.at[S_PROD], s_recv.at[S_PROD], (dp, column))

    def await_products(wait, ref, count_of, sems):
        @pl.when(mine_too)
        def _():
            wait(ref.at[pl.ds(0, count_of - 1)], sems.at[S_PROD])

        @pl.when(jnp.logical_not(mine_too))
        def _():
            wait(ref.at[pl.ds(0, count_of)], sems.at[S_PROD])

    start_far(0)
    start_turned(0)
    await_bytes(sgslot_g.at[pl.ds(0, 2 * G - 1)], s_recv.at[S_NEAR])
    sgtwo[...] = slot_sum(sgslot_g, 2 * G)
    sgslot_z[a] = sgtwo[...]
    for d in reversed(z_devices):
        remote(sgtwo, sgslot_z.at[a], s_send.at[S_FAR], s_recv.at[S_FAR], d)

    parts = settle(MATS - 1, out_column * v_part)
    for m in (2, 1, 0):
        parts = parts + settle(m, finish(m))
    slots = (cw // R) * n_t
    await_products(await_bytes, pslot, slots, s_recv)
    await_bytes(sgslot_z.at[fars], s_recv.at[S_FAR])
    sred[...] = slot_sum(sgslot_z, A)
    head_row = sred[SMALL - 1 : SMALL]
    for i in range(slots):
        head_row = head_row + pslot[i, 0:1]
    sred[SMALL - 1 : SMALL] = head_row
    gr = sred[0:SMALL, :] / counted
    new, dir_small = step(gr, msmall[...])
    grad_s[...] = gr
    moment_s[...] = new
    parts = parts + jnp.where(
        tile_rows == MATS, jnp.sum(dir_small * dir_small, keepdims=True) / (A * B), 0.0
    )
    me = (a * G + g) * 2 + c
    arslot[me] = parts
    for d in everyone:
        remote(arslot.at[me], arslot.at[me], s_send.at[S_ALL], s_recv.at[S_ALL], d)
    loss_b[...] = sred[SMALL : SMALL + 1, 0:1] / counted
    bias_b[...] = grad_s[7 : 7 + 2 * LAYERS, :]
    await_bytes(arslot.at[pl.ds(0, len(everyone))], s_recv.at[S_ALL])
    dir_sq = jnp.sum(arslot[...], axis=0)

    def rate_of(m):
        size = sred[SMALL + 1 : SMALL + 2, m : m + 1]
        return spread_rate * jnp.sqrt(size) / jnp.sqrt(dir_sq[m : m + 1, 0:1] + norm_epsilon)

    for m in range(MATS):
        at = (m // 2, m % 2)
        direction = grad_b[at] + momentum_coef * moment_b[at]
        new = master[at] - rate_of(m) * direction
        master_b[at] = new
        average_b[at] = average_decay * average[at] + (1.0 - average_decay) * new
        low_b[at] = new.astype(BF16)
    new = own_small - rate_of(MATS) * dir_small
    master_s[...] = new
    average_s[...] = average_decay * asmall[...] + (1.0 - average_decay) * new

    n_w, n_g = len(w_turned), len(g_turned)
    gathered = MOVED * (A - 1 + G - 1 + A * G) + (A - 1) * (MOVED * (G - 1) - n_w) + n_w * (A - 1)
    scattered = MOVED * (A - 1 + A * G) + A * (MOVED * (G - 1) - n_g) + n_g * A
    await_sent(sized.at[pl.ds(0, gathered)], w_send.at[0])
    await_sent(sized.at[pl.ds(0, scattered)], g_send.at[0])
    await_sent(qslot_z.at[fars], s_send.at[S_QFAR])
    await_sent(vslot_z.at[fars], s_send.at[S_VFAR])
    await_sent(qslot_g.at[pl.ds(0, 2 * G - 1)], s_send.at[S_QNEAR])
    await_sent(vslot_g.at[pl.ds(0, 2 * G - 1)], s_send.at[S_VNEAR])
    await_sent(sgslot_g.at[pl.ds(0, 2 * G - 1)], s_send.at[S_NEAR])
    await_products(await_sent, pdone, A * B, s_send)
    await_sent(sgslot_z.at[fars], s_send.at[S_FAR])
    await_sent(arslot.at[pl.ds(0, len(everyone))], s_send.at[S_ALL])
    await_sent(spbuf.at[pl.ds(0, n_t - 1)], s_send.at[S_PAR])


def write_out(*refs):
    sems = refs[-1]
    count = (len(refs) - 1) // 2
    copies = [
        pltpu.make_async_copy(refs[i], refs[count + i], sems.at[i]) for i in range(count)
    ]
    for copy in copies:
        copy.start()
    for copy in copies:
        copy.wait()


def body(
    axes,
    coords,
    model_ids,
    cells,
    valid,
    slowness_grid,
    master_blocks,
    small_params,
    moment_blocks,
    moment_small,
    average_blocks,
    average_small,
):
    n_dp, n_t = axes
    A = 4 if n_dp % 4 == 0 else n_dp
    B = n_dp // A
    C = n_t // 2
    G = C * B
    R, cw = master_blocks.shape[2:]
    D = R * n_dp
    PB = coords.shape[1]
    Pn = PB // n_t
    dims = (A, B, C, R, cw, Pn, D)
    anywhere = pl.BlockSpec(memory_space=pltpu.HBM)
    vmem = pl.BlockSpec(memory_space=pltpu.VMEM)
    S = SMALL + 4
    args = (
        coords,
        model_ids,
        cells,
        valid,
        slowness_grid,
        master_blocks,
        small_params,
        moment_blocks,
        moment_small,
        average_blocks,
        average_small,
    )
    V = pltpu.VMEM
    DMA = pltpu.SemaphoreType.DMA
    block = (master_blocks.shape, F32)
    short = (small_params.shape, F32)
    shapes = [
        ((1, 1), F32),
        block,
        short,
        ((2 * LAYERS, cw), F32),
        block,
        short,
        block,
        short,
        block,
        short,
        (master_blocks.shape, BF16),
    ]
    results = pl.pallas_call(
        functools.partial(kernel, dims),
        out_shape=tuple(V(*shape) for shape in shapes),
        in_specs=[anywhere] * len(args),
        out_specs=(vmem,) * len(shapes),
        scratch_shapes=[
            V(coords.shape, F32),
            V((PB,), jnp.int32),
            V((PB,), jnp.int32),
            V((PB,), jnp.int32),
            V(slowness_grid.shape, F32),
            V(master_blocks.shape, F32),
            V(master_blocks.shape, F32),
            V(small_params.shape, F32),
            V(master_blocks.shape, F32),
            V(small_params.shape, F32),
            V((n_t, SMALL, cw), F32),
            V((PB, 128), F32),
            V((S, cw), F32),
            V((MOVED, 2, C, A, B, R, cw), BF16),
            V((4, Pn, D), F32),
            V((LAYERS, 4, Pn, D), BF16),
            V((LAYERS, 4, Pn, D), F32),
            V((LAYERS, 4, Pn, D), BF16),
            V((4, Pn, D), F32),
            V((4, Pn, D), BF16),
            V((4, Pn, D), BF16),
            V((Pn, D), F32),
            V((MOVED, 2, A, G, R, cw), BF16),
            V((MOVED, A, G, R, cw), BF16),
            V((MOVED, A, G, R, cw), BF16),
            V((MOVED, A, G - 1, R, cw), BF16),
            V((MOVED, A - 1, R, cw), BF16),
            V((MOVED, A - 1, R, cw), BF16),
            V((MOVED, R, cw), F32),
            V((MOVED, A - 1, R, cw), BF16),
            V((MOVED, R, cw), BF16),
            V((MOVED, R, cw), BF16),
            V((2, C, S, cw), F32),
            V((8, cw), F32),
            V(((cw // R) * n_t, 8, cw), F32),
            V((n_dp, 8, cw), F32),
            V((MOVED * A * (2 * G + 1), R, cw), BF16),
            V((2 * G, S, cw), F32),
            V((S, cw), F32),
            V((A, S, cw), F32),
            V((2 * A * G, 8, 128), F32),
            V((A, 8, cw), F32),
            V((2 * G, 8, cw), F32),
            V((2, C, 8, cw), F32),
            V((2 * G, 8, cw), F32),
            V((A, 8, cw), F32),
            pltpu.SemaphoreType.DMA((len(args),)),
            DMA((1,)),
            DMA((MOVED, A - 1)),
            DMA((MOVED, G - 1)),
            DMA((MOVED,)),
            DMA((MOVED,)),
            DMA((1,)),
            DMA((MOVED,)),
            DMA((MOVED, A)),
            DMA((MOVED, 2)),
            DMA((MOVED,)),
            DMA((9,)),
            DMA((9,)),
        ],
        compiler_params=pltpu.CompilerParams(
            collective_id=0, has_side_effects=True, vmem_limit_bytes=60 << 20
        ),
    )(*args)

    results = pl.pallas_call(
        write_out,
        out_shape=tuple(jax.ShapeDtypeStruct(*shape) for shape in shapes),
        in_specs=[vmem] * len(shapes),
        out_specs=(anywhere,) * len(shapes),
        scratch_shapes=[pltpu.SemaphoreType.DMA((len(shapes),))],
        compiler_params=pltpu.CompilerParams(vmem_limit_bytes=4 << 20),
    )(*results)
    return (results[0].reshape(()),) + tuple(results[1:])


def solution(mesh):
    blocks = P(None, None, "dp", "tensor")
    small = P(None, "tensor")
    in_specs = (
        P(None, "dp"),
        P("dp"),
        P("dp"),
        P("dp"),
        P(),
        blocks,
        small,
        blocks,
        small,
        blocks,
        small,
    )
    out_specs = (P(), blocks, small, small, blocks, small, blocks, small, blocks, small, blocks)
    axes = (mesh.shape["dp"], mesh.shape["tensor"])
    return jax.shard_map(
        functools.partial(body, axes), mesh=mesh, in_specs=in_specs, out_specs=out_specs, check_vma=False
    )
```
